32 devices in a mesh: plots: 8 (over y, x, core), band: 4 (over z).
Axes of the slice: x: 2, y: 2, z: 4, core: 2. Of those that a mesh axis runs over, the one named last changes fastest.
Arguments:
- patches: bfloat16 [32, 1024, 768], P('plots', 'band'), may hold values from -6 to 6
- norm1_gain: float32 [768], replicated, may hold values from 0.1 to 1.9
- w_query: bfloat16 [768, 768], replicated, may hold values from -0.4375 to 0.4375
- w_key: bfloat16 [768, 768], replicated, may hold values from -0.21875 to 0.21875
- w_value: bfloat16 [768, 768], replicated, may hold values from -0.21875 to 0.21875
- w_out: bfloat16 [768, 768], replicated, may hold values from -0.875 to 0.875
- norm2_gain: float32 [768], replicated, may hold values from 0.1 to 1.9
- w_gate: bfloat16 [768, 2048], replicated, may hold values from -0.21875 to 0.21875
- w_up: bfloat16 [768, 2048], replicated, may hold values from -0.21875 to 0.21875
- w_down: bfloat16 [2048, 768], replicated, may hold values from -0.25 to 0.25
- out_grad: bfloat16 [32, 1024, 768], P('plots', 'band'), may hold values from -6 to 6
- plot_rows: int32 [32], P('plots'), may hold values from 8 to 16, as said below
- plot_cols: int32 [32], P('plots'), may hold values from 32 to 64
- global_index: int32 [32, 128], P('plots'), may hold values from 0 to 1023, as said below
Outputs:
- mixed_out: bfloat16 [32, 1024, 768], P('plots', 'band')
- patch_grad: bfloat16 [32, 1024, 768], P('plots', 'band')
- norm1_grad: float32 [768], replicated
- query_grad: float32 [768, 768], replicated
- key_grad: float32 [768, 768], replicated
- value_grad: float32 [768, 768], replicated
- out_proj_grad: float32 [768, 768], replicated
- norm2_grad: float32 [768], replicated
- gate_grad: float32 [768, 2048], replicated
- up_grad: float32 [768, 2048], replicated
- down_grad: float32 [2048, 768], replicated
The draws below stay inside these ranges and needn't reach their ends.
Inputs may be any that keep to these rules, and one draw needn't show every extreme that they name: `plot_rows`: in each aligned group of 4 plots one plot has 16 rows and 64 columns. `global_index`: A plot's 128 indices are distinct valid slots of that plot.
All inputs are finite; a program needn't handle non-finite values.
Results may differ from the reference program's by a relative error of at most 0.017.
The reference program's roundings to bfloat16 on the way count: a program that leaves them out, or rounds other values in their place, can miss the bound.
Values may be sent and summed in bfloat16 or wider, within the bound.
No kernel may reach another device: no remote copies, remote signals or barrier semaphores. Data moves between devices by JAX's collectives and lax.ppermute only.
A program may use at most 256 MiB of HBM per device.

```python
import jax
import jax.numpy as jnp
from jax import lax

D = 768
H = 12
HD = 64
FF = 2048
PLOTS_DEV = 4
ROWS_DEV = 4
COLS = 64
WIN = 2
GLOBALS = 128
PLOTS = 32
GRID_ROWS = 16
SLOTS = 1024
N_BAND = 4


def plot_shape(key):
    row_key, col_key, pick_key = jax.random.split(key, 3)
    grid_rows = jax.random.randint(row_key, (PLOTS,), GRID_ROWS // 2, GRID_ROWS + 1)
    grid_cols = jax.random.randint(col_key, (PLOTS,), COLS // 2, COLS + 1)
    picked = jax.random.randint(pick_key, (PLOTS // PLOTS_DEV,), 0, PLOTS_DEV)
    filled = jnp.arange(PLOTS, dtype=jnp.int32) % PLOTS_DEV == jnp.repeat(picked, PLOTS_DEV)
    grid_rows = jnp.where(filled, GRID_ROWS, grid_rows).astype(jnp.int32)
    grid_cols = jnp.where(filled, COLS, grid_cols).astype(jnp.int32)
    return (grid_rows, grid_cols, filled)


def draw_plot_rows(key, part):
    base_key = key
    return plot_shape(base_key)[0]


def draw_plot_cols(key, part):
    base_key = key
    return plot_shape(base_key)[1]


def draw_global_index(key, part):
    base_key = key
    key = jax.random.fold_in(key, 3)
    grid_rows, grid_cols, filled = plot_shape(base_key)
    slot_index = jnp.arange(SLOTS, dtype=jnp.int32)
    inside = ((slot_index // COLS)[None, :] < grid_rows[:, None]) & ((slot_index % COLS)[None, :] < grid_cols[:, None])
    ranking = jax.random.randint(key, (PLOTS, SLOTS), 0, 2 ** 18) * SLOTS + slot_index[None, :]
    forced = filled[:, None] & ((slot_index == 0) | (slot_index == SLOTS - 1))[None, :]
    ranking = jnp.where(forced, ranking + 2 ** 30, ranking)
    ranking = jnp.where(inside, ranking, -1 - slot_index[None, :])
    return lax.top_k(ranking, GLOBALS)[1].astype(jnp.int32)


def level_of(key, extent, shards, smallest, top_value):
    def one(dim, shards_of):
        draws = jax.random.uniform(jax.random.fold_in(jax.random.fold_in(key, 6), dim), (shards_of,), jnp.float32, smallest / len(shards), top_value / len(shards))
        return jnp.repeat(jnp.exp(draws), extent[dim] // shards_of).reshape((-1,) + (1,) * (len(extent) - dim - 1))

    level = one(*shards[0])
    for cut in shards[1:]:
        level = level * one(*cut)
    return level


def gaussian(own_key, shape, width, most, shards=(), kind=jnp.bfloat16):
    level = level_of(own_key, shape, shards, -0.22, 0.18) if shards else 1.0
    values = jax.random.normal(own_key, shape, jnp.float32) * width * level
    return jnp.minimum(jnp.maximum(values, -most), most).astype(kind)


def setup_inputs(seed: int = 0) -> dict:
    seeds = jax.random.split(jax.random.key(seed), 15)
    patches = gaussian(seeds[0], (PLOTS, SLOTS, D), 1.0, 6.0, ((0, 8), (1, 4)))
    norm1_gain = jnp.clip(1.0 + 0.18 * jax.random.normal(seeds[1], (D,), jnp.float32), 0.1, 1.9)
    w_query = gaussian(seeds[2], (D, D), (D // 4) ** -0.5, 0.4375)
    w_key = gaussian(seeds[3], (D, D), D ** -0.5, 0.21875)
    w_value = gaussian(seeds[4], (D, D), D ** -0.5, 0.21875)
    w_out = gaussian(seeds[5], (D, D), (D // 16) ** -0.5, 0.875)
    norm2_gain = jnp.clip(1.0 + 0.18 * jax.random.normal(seeds[6], (D,), jnp.float32), 0.1, 1.9)
    w_gate = gaussian(seeds[7], (D, FF), D ** -0.5, 0.21875)
    w_up = gaussian(seeds[8], (D, FF), D ** -0.5, 0.21875)
    w_down = gaussian(seeds[9], (FF, D), (FF // 4) ** -0.5, 0.25)
    out_grad = gaussian(seeds[10], (PLOTS, SLOTS, D), 1.0, 6.0, ((0, 8), (1, 4)))
    plot_rows = draw_plot_rows(jax.random.fold_in(seeds[14], 71), 0)
    plot_cols = draw_plot_cols(jax.random.fold_in(seeds[14], 71), 0)
    global_index = draw_global_index(jax.random.fold_in(seeds[14], 71), 0)
    return {"patches": patches, "norm1_gain": norm1_gain, "w_query": w_query, "w_key": w_key, "w_value": w_value, "w_out": w_out, "norm2_gain": norm2_gain, "w_gate": w_gate, "w_up": w_up, "w_down": w_down, "out_grad": out_grad, "plot_rows": plot_rows, "plot_cols": plot_cols, "global_index": global_index}


@jax.custom_vjp
def low(v):
    return lax.optimization_barrier(v.astype(jnp.bfloat16)).astype(jnp.float32)

@jax.custom_vjp
def low_back(v):
    return v

def low_keep(v):
    return (low(v), None)

def low_pass(kept, grad):
    return (grad,)

def back_keep(v):
    return (v, None)

def back_low(kept, grad):
    return (low(grad),)
low.defvjp(low_keep, low_pass)
low_back.defvjp(back_keep, back_low)

def rms_norm(values, gain):
    inverse = lax.rsqrt(lax.optimization_barrier(jnp.mean(values * values, axis=-1, keepdims=True)) + 1e-06)
    return values * inverse * gain

def project(left, weight):
    return jnp.dot(left, weight, precision=lax.Precision.HIGHEST)

def plot_forward(params, patch, plot_rows, plot_cols, chosen):
    norm1, weight_q, weight_k, weight_v, weight_o, norm2, weight_g, weight_u, weight_d = params
    band_slots = ROWS_DEV * COLS
    window_slots = (ROWS_DEV + 2 * WIN) * COLS
    margin = WIN * COLS
    hidden = low(rms_norm(patch, norm1))
    query = low_back(low(project(hidden, weight_q))).reshape(SLOTS, H, HD)
    keys = low_back(low(project(hidden, weight_k))).reshape(SLOTS, H, HD)
    values = low_back(low(project(hidden, weight_v))).reshape(SLOTS, H, HD)
    global_keys = keys[chosen]
    global_values = values[chosen]
    keys_padded = jnp.pad(keys, ((margin, margin), (0, 0), (0, 0)))
    values_padded = jnp.pad(values, ((margin, margin), (0, 0), (0, 0)))

    def band_block(band_number):
        start = (band_number * band_slots).astype(jnp.int32)
        query_block = lax.dynamic_slice_in_dim(query, start, band_slots, 0)
        key_block = jnp.concatenate([lax.dynamic_slice_in_dim(keys_padded, start, window_slots, 0), global_keys], 0)
        value_block = jnp.concatenate([lax.dynamic_slice_in_dim(values_padded, start, window_slots, 0), global_values], 0)
        query_row = band_number * ROWS_DEV + jnp.arange(band_slots, dtype=jnp.int32) // COLS
        position = jnp.arange(window_slots, dtype=jnp.int32)
        key_row = band_number * ROWS_DEV - WIN + position // COLS
        key_col = position % COLS
        inside = (key_row >= 0) & (key_row < plot_rows) & (key_col < plot_cols)
        near = jnp.abs(key_row[None, :] - query_row[:, None]) <= WIN
        allowed = jnp.concatenate([near & inside[None, :], jnp.ones((band_slots, GLOBALS), dtype=bool)], 1)
        scores = low_back(jnp.einsum('qhd,khd->hqk', query_block, key_block, precision=lax.Precision.HIGHEST) * HD ** (-0.5))
        scores = jnp.where(allowed[None], scores, -1e+30)
        highest = lax.optimization_barrier(jnp.max(scores, axis=-1, keepdims=True))
        expont = jnp.exp(scores - highest)
        probs = expont / lax.optimization_barrier(jnp.sum(expont, axis=-1, keepdims=True))
        attended = jnp.einsum('hqk,khd->qhd', low(probs), value_block, precision=lax.Precision.HIGHEST)
        return attended.reshape(band_slots, H * HD)
    mixed = lax.map(jax.checkpoint(band_block), jnp.arange(N_BAND, dtype=jnp.int32))
    attended = low_back(low(mixed.reshape(SLOTS, D)))
    resid = patch + low_back(project(attended, weight_o))
    hidden2 = low(rms_norm(resid, norm2))
    gate = low_back(project(hidden2, weight_g))
    up_proj = low_back(project(hidden2, weight_u))
    inner = low(jax.nn.gelu(gate, approximate=True) * up_proj)
    return resid + low_back(project(inner, weight_d))

def reference(patches, norm1_gain, w_query, w_key, w_value, w_out, norm2_gain, w_gate, w_up, w_down, out_grad, plot_rows, plot_cols, global_index):
    params = tuple((weight.astype(jnp.float32) for weight in (norm1_gain, w_query, w_key, w_value, w_out, norm2_gain, w_gate, w_up, w_down)))

    def one_plot(totals, entry):
        patch, cotangent, rows_here, cols_here, chosen = entry

        def forward(weights, inputs):
            return plot_forward(weights, inputs, rows_here, cols_here, chosen)
        result, backward = jax.vjp(forward, params, patch.astype(jnp.float32))
        weight_grads, input_grad = backward(cotangent.astype(jnp.float32))
        totals = tuple((total + grad for total, grad in zip(totals, weight_grads)))
        return (totals, (result.astype(jnp.bfloat16), input_grad.astype(jnp.bfloat16)))
    zeros = tuple((jnp.zeros_like(weight) for weight in params))
    totals, outputs = lax.scan(one_plot, zeros, (patches, out_grad, plot_rows, plot_cols, global_index))
    return (outputs[0], outputs[1], totals[0], totals[1], totals[2], totals[3], totals[4], totals[5], totals[6], totals[7], totals[8])
```

```python
import functools

import jax
import jax.numpy as jnp
from jax import lax
from jax.experimental import pallas as pl
from jax.experimental.pallas import tpu as pltpu
from jax.sharding import PartitionSpec as P

H = 12
HD = 64
COLS = 64
WIN = 2
TILE_ROWS = 4
PAIR = 2 * HD
BF = jnp.bfloat16
F32 = jnp.float32
LOG2E = 1.4426950408889634
SCALE2 = LOG2E * HD ** (-0.5)


def dot_nt(a, b):
    return lax.dot_general(a, b, (((1,), (1,)), ((), ())), preferred_element_type=F32)


def dot_nn(a, b):
    return lax.dot_general(a, b, (((1,), (0,)), ((), ())), preferred_element_type=F32)


def dot_tn(a, b):
    return lax.dot_general(a, b, (((0,), (0,)), ((), ())), preferred_element_type=F32)


def tiles_of(rows):
    out = []
    for first in range(0, rows, TILE_ROWS):
        low = max(first - WIN, 0)
        high = min(first + TILE_ROWS + WIN, rows)
        out.append((first * COLS, low * COLS, high * COLS))
    return out


def fill_bias(bias_ref, limits_ref, tiles):
    rows_here = limits_ref[0]
    cols_here = limits_ref[1]
    for number, (query_lo, key_lo, key_hi) in enumerate(tiles):
        count = key_hi - key_lo
        shape = (count, TILE_ROWS * COLS)
        key = lax.broadcasted_iota(jnp.int32, shape, 0) + key_lo
        query = lax.broadcasted_iota(jnp.int32, shape, 1) + query_lo
        key_row = key // COLS
        apart = key_row - query // COLS
        seen = (apart <= WIN) & (apart >= -WIN) & (key_row < rows_here) & (key % COLS < cols_here)
        bias_ref[number, :count, :] = jnp.where(seen, 0.0, -1e30).astype(F32)


def picker_rows(index_ref, slots):
    chosen = index_ref[:, 0:1]
    lanes = lax.broadcasted_iota(jnp.int32, (chosen.shape[0], slots), 1)
    return (lanes == chosen).astype(F32).astype(BF)


def attend_kernel(
    limits_ref, index_ref, q_ref, k_ref, v_ref, out_ref, lse_ref, bias_ref, pick_ref, value_t
):
    slots = q_ref.shape[0]
    tiles = tiles_of(slots // COLS)
    span = TILE_ROWS * COLS

    @pl.when(pl.program_id(0) == 0)
    def _():
        fill_bias(bias_ref, limits_ref, tiles)
        pick_ref[...] = picker_rows(index_ref, slots)

    global_keys = dot_nn(pick_ref[...], k_ref[...]).astype(BF)
    global_values = dot_nn(pick_ref[...], v_ref[...])
    global_values_t = jnp.transpose(global_values).astype(BF)
    value_t[...] = jnp.transpose(v_ref[...].astype(F32)).astype(BF)
    lane = lax.broadcasted_iota(jnp.int32, (span, PAIR), 1)
    for number, (query_lo, key_lo, key_hi) in enumerate(tiles):
        count = key_hi - key_lo
        query = q_ref[query_lo : query_lo + span, :]
        heads = []
        for half in range(2):
            masked = jnp.where((lane < HD) == (half == 0), query, jnp.zeros_like(query))
            window = dot_nt(k_ref[key_lo:key_hi, :], masked) * SCALE2 + bias_ref[number, :count, :]
            wide = dot_nt(global_keys, masked) * SCALE2
            highest = jnp.maximum(
                jnp.max(window, axis=0, keepdims=True), jnp.max(wide, axis=0, keepdims=True)
            )
            window = jnp.exp2(window - highest)
            wide = jnp.exp2(wide - highest)
            total = jnp.sum(window, axis=0, keepdims=True) + jnp.sum(wide, axis=0, keepdims=True)
            inverse = 1.0 / total
            window = (window * inverse).astype(BF)
            wide = (wide * inverse).astype(BF)
            rows = slice(half * HD, half * HD + HD)
            heads.append(
                dot_nn(value_t[rows, key_lo:key_hi], window) + dot_nn(global_values_t[rows, :], wide)
            )
            lse_ref[0, half : half + 1, query_lo : query_lo + span] = highest + jnp.log2(total)
        joined = jnp.concatenate(heads, axis=0)
        out_ref[query_lo : query_lo + span, :] = jnp.transpose(joined).astype(BF)


def attend_back_kernel(
    limits_ref,
    index_ref,
    index_t_ref,
    q_ref,
    k_ref,
    v_ref,
    g_ref,
    lse_ref,
    dq_ref,
    dk_ref,
    dv_ref,
    bias_ref,
    pick_ref,
    pick_t_ref,
    key_t,
    dk_acc,
    dv_acc,
):
    slots = q_ref.shape[0]
    tiles = tiles_of(slots // COLS)
    span = TILE_ROWS * COLS
    globals_here = index_ref.shape[0]

    @pl.when(pl.program_id(0) == 0)
    def _():
        fill_bias(bias_ref, limits_ref, tiles)
        pick_ref[...] = picker_rows(index_ref, slots)
        down = lax.broadcasted_iota(jnp.int32, (slots, globals_here), 0)
        pick_t_ref[...] = (down == index_t_ref[0:1, :]).astype(F32).astype(BF)

    global_keys_f = dot_nn(pick_ref[...], k_ref[...])
    global_keys = global_keys_f.astype(BF)
    global_keys_t = jnp.transpose(global_keys_f).astype(BF)
    global_values = dot_nn(pick_ref[...], v_ref[...]).astype(BF)
    key_t[...] = jnp.transpose(k_ref[...].astype(F32)).astype(BF)
    dk_acc[...] = jnp.zeros_like(dk_acc)
    dv_acc[...] = jnp.zeros_like(dv_acc)
    dk_global = jnp.zeros((globals_here, PAIR), F32)
    dv_global = jnp.zeros((globals_here, PAIR), F32)
    lane = lax.broadcasted_iota(jnp.int32, (span, PAIR), 1)
    for number, (query_lo, key_lo, key_hi) in enumerate(tiles):
        count = key_hi - key_lo
        query = q_ref[query_lo : query_lo + span, :]
        grad = g_ref[query_lo : query_lo + span, :]
        keys = k_ref[key_lo:key_hi, :]
        values = v_ref[key_lo:key_hi, :]
        heads = []
        for half in range(2):
            mine = (lane < HD) == (half == 0)
            query_m = jnp.where(mine, query, jnp.zeros_like(query))
            grad_m = jnp.where(mine, grad, jnp.zeros_like(grad))
            lse = lse_ref[0, half : half + 1, query_lo : query_lo + span]
            window = jnp.exp2(dot_nt(keys, query_m) * SCALE2 + (bias_ref[number, :count, :] - lse))
            wide = jnp.exp2(dot_nt(global_keys, query_m) * SCALE2 - lse)
            window_g = dot_nt(values, grad_m)
            wide_g = dot_nt(global_values, grad_m)
            weighted = jnp.sum(window * window_g, axis=0, keepdims=True) + jnp.sum(
                wide * wide_g, axis=0, keepdims=True
            )
            window_s = (window * (window_g - weighted)).astype(BF)
            wide_s = (wide * (wide_g - weighted)).astype(BF)
            dv_acc[key_lo:key_hi, :] += dot_nn(window.astype(BF), grad_m)
            dk_acc[key_lo:key_hi, :] += dot_nn(window_s, query_m)
            dv_global += dot_nn(wide.astype(BF), grad_m)
            dk_global += dot_nn(wide_s, query_m)
            rows = slice(half * HD, half * HD + HD)
            heads.append(
                dot_nn(key_t[rows, key_lo:key_hi], window_s) + dot_nn(global_keys_t[rows, :], wide_s)
            )
        joined = jnp.concatenate(heads, axis=0) * HD ** (-0.5)
        dq_ref[query_lo : query_lo + span, :] = jnp.transpose(joined).astype(BF)

    def spread(part):
        high = part.astype(BF)
        rest = part - high.astype(F32)
        middle = rest.astype(BF)
        low = (rest - middle.astype(F32)).astype(BF)
        picks = pick_t_ref[...]
        return dot_nn(picks, high) + dot_nn(picks, middle) + dot_nn(picks, low)

    dk_ref[...] = ((dk_acc[...] + spread(dk_global)) * HD ** (-0.5)).astype(BF)
    dv_ref[...] = (dv_acc[...] + spread(dv_global)).astype(BF)


def attention_parts(slots, width, globals_here):
    pairs = width // PAIR
    tall = (TILE_ROWS + 2 * WIN) * COLS
    tiles = slots // (TILE_ROWS * COLS)
    limits = pl.BlockSpec(memory_space=pltpu.SMEM)
    index = pl.BlockSpec((globals_here, 128), lambda p: (0, 0))
    block = pl.BlockSpec((slots, PAIR), lambda p: (0, p))
    lse = pl.BlockSpec((1, 8, slots), lambda p: (p, 0, 0))
    bias = pltpu.VMEM((tiles, tall, TILE_ROWS * COLS), F32)
    pick = pltpu.VMEM((globals_here, slots), BF)
    return pairs, limits, index, block, lse, bias, pick


def attention(query, keys, values, limits, index):
    slots, width = query.shape
    globals_here = index.shape[0]
    pairs, lim, idx, block, lse, bias, pick = attention_parts(slots, width, globals_here)
    return pl.pallas_call(
        attend_kernel,
        grid=(pairs,),
        in_specs=[lim, idx, block, block, block],
        out_specs=[block, lse],
        out_shape=[
            jax.ShapeDtypeStruct((slots, width), BF),
            jax.ShapeDtypeStruct((pairs, 8, slots), F32),
        ],
        scratch_shapes=[bias, pick, pltpu.VMEM((PAIR, slots), BF)],
        compiler_params=pltpu.CompilerParams(vmem_limit_bytes=40 * 2**20),
        name="attend",
    )(limits, index, query, keys, values)


def attention_back(query, keys, values, grad, lse_in, limits, index, index_t):
    slots, width = query.shape
    globals_here = index.shape[0]
    pairs, lim, idx, block, lse, bias, pick = attention_parts(slots, width, globals_here)
    idx_t = pl.BlockSpec((8, globals_here), lambda p: (0, 0))
    low = jax.ShapeDtypeStruct((slots, width), BF)
    return pl.pallas_call(
        attend_back_kernel,
        grid=(pairs,),
        in_specs=[lim, idx, idx_t, block, block, block, block, lse],
        out_specs=[block, block, block],
        out_shape=[low, low, low],
        scratch_shapes=[
            bias,
            pick,
            pltpu.VMEM((slots, globals_here), BF),
            pltpu.VMEM((PAIR, slots), BF),
            pltpu.VMEM((slots, PAIR), F32),
            pltpu.VMEM((slots, PAIR), F32),
        ],
        compiler_params=pltpu.CompilerParams(vmem_limit_bytes=40 * 2**20),
        name="attend_back",
    )(limits, index, index_t, query, keys, values, grad, lse_in)


def flip(axis, bit):
    count = lax.axis_size(axis)
    return [(i, i ^ bit) for i in range(count)]


def take(array, number, axis=0):
    return lax.dynamic_index_in_dim(array, number, axis, keepdims=False)


def add_low(left, right):
    return (left.astype(F32) + right.astype(F32)).astype(BF)


def swap_to_plots(blocks):
    count = lax.axis_size("band")
    here = lax.axis_index("band")
    got = [take(blocks, here)]
    for bit in range(1, count):
        got.append(lax.ppermute(take(blocks, here ^ bit), "band", flip("band", bit)))
    stacked = jnp.stack(got)
    return jnp.concatenate([take(stacked, here ^ band) for band in range(count)])


def swap_to_bands(whole):
    count = lax.axis_size("band")
    here = lax.axis_index("band")
    blocks = whole.reshape(count, whole.shape[0] // count, whole.shape[1])
    got = [take(blocks, here)]
    for bit in range(1, count):
        got.append(lax.ppermute(take(blocks, here ^ bit), "band", flip("band", bit)))
    stacked = jnp.stack(got)
    return jnp.stack([take(stacked, here ^ plot) for plot in range(count)])


def stages(reverse):
    plots = lax.axis_size("plots")
    band = lax.axis_size("band")
    bits = [("plots", 1 << n) for n in range(plots.bit_length() - 1)]
    tail = [("band", 1 << n) for n in range(band.bit_length() - 1)]
    first, rest = bits[:1], bits[1:]
    return first + (rest[::-1] if reverse else rest) + tail


def scatter_sum(matrix, order):
    for axis, bit in order:
        mine = (lax.axis_index(axis) // bit) % 2
        halves = matrix.reshape(2, matrix.shape[0] // 2, matrix.shape[1])
        arrived = lax.ppermute(take(halves, 1 - mine), axis, flip(axis, bit))
        matrix = add_low(take(halves, mine), arrived)
    return matrix


def gather_all(matrix, order):
    for axis, bit in order[::-1]:
        mine = (lax.axis_index(axis) // bit) % 2
        other = lax.ppermute(matrix, axis, flip(axis, bit))
        matrix = jnp.where(
            mine == 0,
            jnp.concatenate([matrix, other]),
            jnp.concatenate([other, matrix]),
        )
    return matrix


def rms_norm(values, gain):
    inverse = lax.rsqrt(jnp.mean(values * values, axis=-1, keepdims=True) + 1e-06)
    return values * inverse * gain


def per_device(
    patches,
    norm1_gain,
    w_query,
    w_key,
    w_value,
    w_out,
    norm2_gain,
    w_gate,
    w_up,
    w_down,
    out_grad,
    plot_rows,
    plot_cols,
    global_index,
):
    width = patches.shape[2]
    here = lax.axis_index("band")
    x_low = swap_to_plots(patches)
    dy = swap_to_plots(out_grad)
    limits = jnp.stack([take(plot_rows, here), take(plot_cols, here)])
    chosen = take(global_index, here)
    index = jnp.broadcast_to(chosen[:, None], (chosen.shape[0], 128))
    index_t = jnp.broadcast_to(chosen[None, :], (8, chosen.shape[0]))

    inputs = x_low.astype(F32)
    hidden = rms_norm(inputs, norm1_gain).astype(BF)
    query = dot_nn(hidden, w_query).astype(BF)
    keys = dot_nn(hidden, w_key).astype(BF)
    values = dot_nn(hidden, w_value).astype(BF)
    attended, lse = attention(query, keys, values, limits, index)
    resid = inputs + dot_nn(attended, w_out)
    hidden2 = rms_norm(resid, norm2_gain).astype(BF)
    gate = dot_nn(hidden2, w_gate)
    up_proj = dot_nn(hidden2, w_up)
    activated, gelu_back = jax.vjp(lambda value_in: jax.nn.gelu(value_in, approximate=True), gate)
    inner = (activated * up_proj).astype(BF)
    mixed_out = (resid + dot_nn(inner, w_down)).astype(BF)
    mixed_out = swap_to_bands(mixed_out)
    grad_down_t = dot_tn(dy, inner)
    grad_inner = dot_nt(dy, w_down)
    grad_gate = gelu_back(grad_inner * up_proj)[0].astype(BF)
    grad_up = (grad_inner * activated).astype(BF)
    grad_w_gate = dot_tn(hidden2, grad_gate)
    grad_w_up = dot_tn(hidden2, grad_up)
    grad_hidden2 = dot_nt(grad_gate, w_gate) + dot_nt(grad_up, w_up)
    norm2_back = jax.vjp(rms_norm, resid, norm2_gain)[1]
    grad_resid, grad_norm2 = norm2_back(grad_hidden2)
    grad_resid = grad_resid + dy.astype(F32)
    resid_low = grad_resid.astype(BF)
    grad_w_out = dot_tn(attended, resid_low)
    grad_attended = dot_nt(resid_low, w_out).astype(BF)
    first = jnp.concatenate([grad_w_gate, grad_w_up, grad_down_t, grad_w_out], 1).astype(BF)
    order = stages(False)
    first = scatter_sum(first, order)

    grad_query, grad_keys, grad_values = attention_back(
        query, keys, values, grad_attended, lse, limits, index, index_t
    )
    grad_w_query = dot_tn(hidden, grad_query)
    grad_w_key = dot_tn(hidden, grad_keys)
    grad_w_value = dot_tn(hidden, grad_values)
    second = jnp.concatenate([grad_w_query, grad_w_key, grad_w_value], 1).astype(BF)
    other = stages(True)
    second = scatter_sum(second, other)
    grad_hidden = (
        dot_nt(grad_query, w_query) + dot_nt(grad_keys, w_key) + dot_nt(grad_values, w_value)
    )
    norm1_back = jax.vjp(rms_norm, inputs, norm1_gain)[1]
    grad_inputs, grad_norm1 = norm1_back(grad_hidden)
    patch_grad = (grad_inputs + grad_resid).astype(BF)
    patch_grad = swap_to_bands(patch_grad)
    gains = lax.psum(jnp.stack([grad_norm1, grad_norm2]), ("plots", "band"))

    first = gather_all(first, order).astype(F32)
    second = gather_all(second, other).astype(F32)
    ff = w_gate.shape[1]
    return (
        mixed_out,
        patch_grad,
        gains[0],
        second[:, :width],
        second[:, width : 2 * width],
        second[:, 2 * width :],
        first[:, 3 * ff :],
        gains[1],
        first[:, :ff],
        first[:, ff : 2 * ff],
        jnp.transpose(first[:, 2 * ff : 3 * ff]),
    )


def solution(mesh):
    rows = P("plots", "band", None)
    in_specs = (rows,) + (P(),) * 9 + (rows, P("plots"), P("plots"), P("plots", None))
    out_specs = (rows, rows) + (P(),) * 9
    return jax.shard_map(
        per_device, mesh=mesh, in_specs=in_specs, out_specs=out_specs, check_vma=False
    )
```

```python
import functools

import jax
import jax.numpy as jnp
from jax import lax
from jax.experimental import pallas as pl
from jax.experimental.pallas import tpu as pltpu
from jax.sharding import PartitionSpec as P

H = 12
HD = 64
COLS = 64
WIN = 2
TILE_ROWS = 2
PAIR = 2 * HD
BF = jnp.bfloat16
F32 = jnp.float32
LOG2E = 1.4426950408889634
SCALE2 = LOG2E * HD ** (-0.5)
SMALL = pl.CostEstimate(flops=1, bytes_accessed=1, transcendentals=0)


def dot_nt(a, b):
    return lax.dot_general(a, b, (((1,), (1,)), ((), ())), preferred_element_type=F32)


def dot_nn(a, b):
    return lax.dot_general(a, b, (((1,), (0,)), ((), ())), preferred_element_type=F32)


def dot_tn(a, b):
    return lax.dot_general(a, b, (((0,), (0,)), ((), ())), preferred_element_type=F32)


def tiles_of(rows):
    out = []
    for first in range(0, rows, TILE_ROWS):
        low = max(first - WIN, 0)
        high = min(first + TILE_ROWS + WIN, rows)
        out.append((first * COLS, low * COLS, high * COLS))
    return out


def fill_bias(bias_ref, limits_ref, tiles):
    rows_here = limits_ref[0]
    cols_here = limits_ref[1]
    span = TILE_ROWS * COLS
    for number, (query_lo, key_lo, key_hi) in enumerate(tiles):
        count = key_hi - key_lo
        shape = (count, 2 * span)
        key = lax.broadcasted_iota(jnp.int32, shape, 0) + key_lo
        query = lax.broadcasted_iota(jnp.int32, shape, 1) % span + query_lo
        key_row = key // COLS
        apart = key_row - query // COLS
        seen = (apart <= WIN) & (apart >= -WIN) & (key_row < rows_here) & (key % COLS < cols_here)
        bias_ref[number, :count, :] = jnp.where(seen, 0.0, -1e30).astype(F32)


def picker_rows(index_ref, slots):
    chosen = index_ref[:, 0:1]
    lanes = lax.broadcasted_iota(jnp.int32, (chosen.shape[0], slots), 1)
    return (lanes == chosen).astype(F32).astype(BF)


def two_heads(block, lane):
    none = jnp.zeros_like(block)
    return jnp.concatenate([jnp.where(lane < HD, block, none), jnp.where(lane < HD, none, block)])


def own_heads(sums, span):
    return jnp.transpose(jnp.concatenate([sums[:HD, :span], sums[HD:, span:]], axis=0))


def attend_kernel(
    limits_ref, index_ref, q_ref, k_ref, v_ref, out_ref, lse_ref, bias_ref, pick_ref, value_t
):
    slots = q_ref.shape[0]
    tiles = tiles_of(slots // COLS)
    span = TILE_ROWS * COLS

    @pl.when(pl.program_id(0) == 0)
    def _():
        fill_bias(bias_ref, limits_ref, tiles)
        pick_ref[...] = picker_rows(index_ref, slots)

    global_keys = dot_nn(pick_ref[...], k_ref[...]).astype(BF)
    global_values_t = jnp.transpose(dot_nn(pick_ref[...], v_ref[...])).astype(BF)
    value_t[...] = jnp.transpose(v_ref[...].astype(F32)).astype(BF)
    lane = lax.broadcasted_iota(jnp.int32, (span, PAIR), 1)
    for number, (query_lo, key_lo, key_hi) in enumerate(tiles):
        count = key_hi - key_lo
        query = two_heads(q_ref[query_lo : query_lo + span, :], lane)
        window = dot_nt(k_ref[key_lo:key_hi, :], query) * SCALE2 + bias_ref[number, :count, :]
        wide = dot_nt(global_keys, query) * SCALE2
        highest = jnp.maximum(
            jnp.max(window, axis=0, keepdims=True), jnp.max(wide, axis=0, keepdims=True)
        )
        window = jnp.exp2(window - highest)
        wide = jnp.exp2(wide - highest)
        total = jnp.sum(window, axis=0, keepdims=True) + jnp.sum(wide, axis=0, keepdims=True)
        inverse = 1.0 / total
        sums = dot_nn(value_t[:, key_lo:key_hi], (window * inverse).astype(BF))
        sums = sums + dot_nn(global_values_t, (wide * inverse).astype(BF))
        lse_ref[0, number : number + 1, :] = highest + jnp.log2(total)
        out_ref[query_lo : query_lo + span, :] = own_heads(sums, span).astype(BF)


def attend_back_kernel(
    limits_ref,
    index_ref,
    index_t_ref,
    q_ref,
    k_ref,
    v_ref,
    g_ref,
    lse_ref,
    out_ref,
    bias_ref,
    pick_ref,
    pick_t_ref,
    key_t,
    dk_acc,
    dv_acc,
):
    slots = q_ref.shape[0]
    tiles = tiles_of(slots // COLS)
    span = TILE_ROWS * COLS
    globals_here = index_ref.shape[0]

    @pl.when(pl.program_id(0) == 0)
    def _():
        fill_bias(bias_ref, limits_ref, tiles)
        pick_ref[...] = picker_rows(index_ref, slots)
        down = lax.broadcasted_iota(jnp.int32, (slots, globals_here), 0)
        pick_t_ref[...] = (down == index_t_ref[0:1, :]).astype(F32).astype(BF)

    global_keys_f = dot_nn(pick_ref[...], k_ref[...])
    global_keys = global_keys_f.astype(BF)
    global_keys_t = jnp.transpose(global_keys_f).astype(BF)
    global_values = dot_nn(pick_ref[...], v_ref[...]).astype(BF)
    key_t[...] = jnp.transpose(k_ref[...].astype(F32)).astype(BF)
    dk_acc[...] = jnp.zeros_like(dk_acc)
    dv_acc[...] = jnp.zeros_like(dv_acc)
    dk_global = jnp.zeros((globals_here, PAIR), F32)
    dv_global = jnp.zeros((globals_here, PAIR), F32)
    lane = lax.broadcasted_iota(jnp.int32, (span, PAIR), 1)
    for number, (query_lo, key_lo, key_hi) in enumerate(tiles):
        count = key_hi - key_lo
        query = two_heads(q_ref[query_lo : query_lo + span, :], lane)
        grad = two_heads(g_ref[query_lo : query_lo + span, :], lane)
        keys = k_ref[key_lo:key_hi, :]
        values = v_ref[key_lo:key_hi, :]
        lse = lse_ref[0, number : number + 1, :]
        window = jnp.exp2(dot_nt(keys, query) * SCALE2 + (bias_ref[number, :count, :] - lse))
        wide = jnp.exp2(dot_nt(global_keys, query) * SCALE2 - lse)
        window_g = dot_nt(values, grad)
        wide_g = dot_nt(global_values, grad)
        weighted = jnp.sum(window * window_g, axis=0, keepdims=True) + jnp.sum(
            wide * wide_g, axis=0, keepdims=True
        )
        window_s = (window * (window_g - weighted)).astype(BF)
        wide_s = (wide * (wide_g - weighted)).astype(BF)
        dv_acc[key_lo:key_hi, :] += dot_nn(window.astype(BF), grad)
        dk_acc[key_lo:key_hi, :] += dot_nn(window_s, query)
        dv_global += dot_nn(wide.astype(BF), grad)
        dk_global += dot_nn(wide_s, query)
        sums = dot_nn(key_t[:, key_lo:key_hi], window_s) + dot_nn(global_keys_t, wide_s)
        sums = own_heads(sums, span) * HD ** (-0.5)
        out_ref[0, query_lo : query_lo + span, :] = sums.astype(BF)

    def spread(part):
        high = part.astype(BF)
        rest = part - high.astype(F32)
        middle = rest.astype(BF)
        low = (rest - middle.astype(F32)).astype(BF)
        picks = pick_t_ref[...]
        return dot_nn(picks, high) + dot_nn(picks, middle) + dot_nn(picks, low)

    out_ref[1] = ((dk_acc[...] + spread(dk_global)) * HD ** (-0.5)).astype(BF)
    out_ref[2] = (dv_acc[...] + spread(dv_global)).astype(BF)


def attention_parts(slots, width, globals_here):
    pairs = width // PAIR
    tall = (TILE_ROWS + 2 * WIN) * COLS
    tiles = slots // (TILE_ROWS * COLS)
    limits = pl.BlockSpec(memory_space=pltpu.SMEM)
    index = pl.BlockSpec((globals_here, 128), lambda p: (0, 0))
    block = pl.BlockSpec((slots, PAIR), lambda p: (0, p))
    lse = pl.BlockSpec((1, tiles, 2 * TILE_ROWS * COLS), lambda p: (p, 0, 0))
    bias = pltpu.VMEM((tiles, tall, 2 * TILE_ROWS * COLS), F32)
    pick = pltpu.VMEM((globals_here, slots), BF)
    return pairs, limits, index, block, lse, bias, pick


def attention(query, keys, values, limits, index):
    slots, width = query.shape
    globals_here = index.shape[0]
    pairs, lim, idx, block, lse, bias, pick = attention_parts(slots, width, globals_here)
    return pl.pallas_call(
        attend_kernel,
        grid=(pairs,),
        in_specs=[lim, idx, block, block, block],
        out_specs=[block, lse],
        out_shape=[
            jax.ShapeDtypeStruct((slots, width), BF),
            jax.ShapeDtypeStruct((pairs, *lse.block_shape[1:]), F32),
        ],
        scratch_shapes=[bias, pick, pltpu.VMEM((PAIR, slots), BF)],
        compiler_params=pltpu.CompilerParams(vmem_limit_bytes=14 * 2**20),
        cost_estimate=SMALL,
        name="attend",
    )(limits, index, query, keys, values)


def attention_back(query, keys, values, grad, lse_in, limits, index, index_t, first, count):
    slots, width = query.shape
    globals_here = index.shape[0]
    _, lim, idx, _, lse, bias, pick = attention_parts(slots, width, globals_here)
    idx_t = pl.BlockSpec((8, globals_here), lambda p: (0, 0))
    out_block = pl.BlockSpec((3, slots, PAIR), lambda p: (0, 0, p))
    block = pl.BlockSpec((slots, PAIR), lambda p: (0, first + p))
    lse = pl.BlockSpec(lse.block_shape, lambda p: (first + p, 0, 0))
    return pl.pallas_call(
        attend_back_kernel,
        grid=(count,),
        in_specs=[lim, idx, idx_t, block, block, block, block, lse],
        out_specs=out_block,
        out_shape=jax.ShapeDtypeStruct((3, slots, count * PAIR), BF),
        scratch_shapes=[
            bias,
            pick,
            pltpu.VMEM((slots, globals_here), BF),
            pltpu.VMEM((PAIR, slots), BF),
            pltpu.VMEM((slots, PAIR), F32),
            pltpu.VMEM((slots, PAIR), F32),
        ],
        compiler_params=pltpu.CompilerParams(vmem_limit_bytes=20 * 2**20),
        cost_estimate=SMALL,
        name="attend_back",
    )(limits, index, index_t, query, keys, values, grad, lse_in)


def turn_kernel(in_ref, out_ref):
    out_ref[...] = jnp.transpose(in_ref[...].astype(F32)).astype(BF)


def turn(matrix):
    rows, columns = matrix.shape
    wide = 256
    return pl.pallas_call(
        turn_kernel,
        grid=(columns // wide,),
        in_specs=[pl.BlockSpec((rows, wide), lambda g: (0, g))],
        out_specs=pl.BlockSpec((wide, rows), lambda g: (g, 0)),
        out_shape=jax.ShapeDtypeStruct((columns, rows), BF),
        compiler_params=pltpu.CompilerParams(vmem_limit_bytes=16 * 2**20),
        cost_estimate=SMALL,
        name="turn",
    )(matrix)


def weight_grad_kernel(spans, swapped, norms, place_ref, left_ref, *refs):
    rights, out_ref = refs[: len(spans)], refs[-1]
    rows = out_ref.shape[1]
    half = 4 * rows
    start = pl.multiple_of(place_ref[0] * half, half)
    mine = left_ref[pl.ds(start, half), :]

    def store(sums, at):
        for block in range(4):
            spot = (block >> 1) | ((block & 1) << 1) if swapped else block
            part = sums[block * rows : (block + 1) * rows]
            out_ref[spot ^ place_ref[1], :, at : at + sums.shape[1]] = part

    at = 0
    for right, span in zip(rights, spans):
        for number, first, count in span:
            for step in range(0, count, 512):
                wide = min(512, count - step)
                columns = right[number, :, first + step : first + step + wide]
                store(dot_nn(mine, columns).astype(BF), at)
                at += wide
    if norms:
        top = lax.broadcasted_iota(jnp.int32, (8, 128), 0) == 0
        lane = lax.broadcasted_iota(jnp.int32, (8, 128), 1)
        picks = jnp.where(top & (lane == 0), 1.0, 0.0)
        other = jnp.where(top & (lane == 1), 1.0, 0.0)
        first, second = refs[len(spans) : len(spans) + 2]
        columns = pl.ds(pl.multiple_of(start, 128), half)
        sums = dot_tn(first[:, columns], picks) + dot_tn(second[:, columns], other)
        store(sums.astype(BF), at)


IN_VMEM = pl.BlockSpec(memory_space=pltpu.VMEM)
IN_SMEM = pl.BlockSpec(memory_space=pltpu.SMEM)


def weight_grad(place, left, rights, spans, swapped=False, norms=()):
    half = left.shape[0] // 2
    total = sum(count for span in spans for _, _, count in span) + (128 if norms else 0)
    return pl.pallas_call(
        functools.partial(weight_grad_kernel, spans, swapped, bool(norms)),
        in_specs=[IN_SMEM] + [IN_VMEM] * (1 + len(rights) + len(norms)),
        out_specs=IN_VMEM,
        out_shape=jax.ShapeDtypeStruct((4, half // 4, total), BF),
        compiler_params=pltpu.CompilerParams(vmem_limit_bytes=12 * 2**20),
        cost_estimate=SMALL,
        name="weight_grad",
    )(place, left, *rights, *norms)


def ffn_kernel(
    place_ref,
    hidden_ref,
    hidden_t,
    dy_ref,
    dy_t,
    gate_w,
    up_w,
    down_w,
    inner_ref,
    gate_ref,
    up_ref,
    near_ref,
    far_ref,
):
    rows = 256
    slope = (2.0 / 3.141592653589793) ** 0.5
    for start in range(0, hidden_ref.shape[0], rows):
        here = slice(start, start + rows)
        gate = dot_nn(hidden_ref[here, :], gate_w[...])
        up = dot_nn(hidden_ref[here, :], up_w[...])
        back = dot_nn(dy_ref[here, :], down_w[...])
        square = gate * gate
        share = 0.5 + 0.5 * jnp.tanh(gate * (slope + (0.044715 * slope) * square))
        active = gate * share
        inner_ref[here, :] = (active * up).astype(BF)
        up_ref[here, :] = (back * active).astype(BF)
        steep = share + (active - active * share) * (
            2.0 * slope + (6.0 * 0.044715 * slope) * square
        )
        gate_ref[here, :] = (back * up * steep).astype(BF)
    height = near_ref.shape[2]
    late = pl.program_id(0) >= pl.num_programs(0) // 2
    turned = (False, True, late)
    lefts, rights = (hidden_t, hidden_t, dy_t), (gate_ref, up_ref, inner_ref)
    for number, (left, right, swapped) in enumerate(zip(lefts, rights, turned)):
        sums = dot_nn(left[...], right[...]).astype(BF)
        for half in range(2):

            def put(target, half=half, sums=sums, number=number, swapped=swapped):
                for block in range(4):
                    straight = block ^ place_ref[1]
                    crossed = ((block >> 1) | ((block & 1) << 1)) ^ place_ref[2]
                    at = (4 * half + block) * height
                    spot = jnp.where(swapped, crossed, straight)
                    target[number, spot] = sums[at : at + height]

            pl.when(place_ref[0] == half)(functools.partial(put, near_ref))
            pl.when(place_ref[0] != half)(functools.partial(put, far_ref))


def ffn(place, hidden, hidden_t, dy, dy_t, w_gate, w_up, w_down_t):
    tokens, width = hidden.shape
    units = w_gate.shape[1]
    chunk = 512
    weight = pl.BlockSpec((width, chunk), lambda g: (0, g))
    wide = pl.BlockSpec((tokens, chunk), lambda g: (0, g))
    half = pl.BlockSpec((3, 4, width // 8, chunk), lambda g: (0, 0, 0, g))
    return pl.pallas_call(
        ffn_kernel,
        grid=(units // chunk,),
        in_specs=[IN_SMEM] + [IN_VMEM] * 4 + [weight] * 3,
        out_specs=[wide, wide, wide, half, half],
        out_shape=[jax.ShapeDtypeStruct((tokens, units), BF)] * 3
        + [jax.ShapeDtypeStruct((3, 4, width // 8, units), BF)] * 2,
        compiler_params=pltpu.CompilerParams(vmem_limit_bytes=32 * 2**20),
        cost_estimate=SMALL,
        name="ffn",
    )(place, hidden, hidden_t, dy, dy_t, w_gate, w_up, w_down_t)


def norm_back(values, gain, grad):
    inverse = lax.rsqrt(jnp.mean(values * values, axis=-1, keepdims=True) + 1e-06)
    scaled = values * inverse
    pulled = grad * gain
    shared = jnp.mean(scaled * pulled, axis=-1, keepdims=True)
    return inverse * (pulled - scaled * shared), jnp.sum(grad * scaled, axis=0, keepdims=True)


def patch_kernel(splits, *refs):
    parts, refs = refs[:splits], refs[splits:]
    x_ref, grad_ref, gain_ref, *weights, out_ref, norm_ref = refs
    grad = 0.0
    for number, weight in enumerate(weights):
        part = jnp.concatenate([ref[number] for ref in parts], axis=1)
        grad = grad + dot_nn(part, weight[...])
    pulled, gain = norm_back(x_ref[...].astype(F32), gain_ref[...], grad)
    out_ref[...] = (pulled + grad_ref[...]).astype(BF)

    @pl.when(pl.program_id(0) == 0)
    def _():
        norm_ref[...] = jnp.zeros_like(norm_ref)

    norm_ref[0:1, :] += gain


def patch_back(parts, x, grad, gain, w_query, w_key, w_value):
    tokens, width = x.shape
    rows = 512
    slim = pl.BlockSpec((rows, width), lambda g: (g, 0))
    part_specs = [pl.BlockSpec((3, rows, part.shape[2]), lambda g: (0, g, 0)) for part in parts]
    return pl.pallas_call(
        functools.partial(patch_kernel, len(parts)),
        grid=(tokens // rows,),
        in_specs=part_specs + [slim, slim] + [IN_VMEM] * 4,
        out_specs=[slim, pl.BlockSpec((8, width), lambda g: (0, 0))],
        out_shape=[
            jax.ShapeDtypeStruct((tokens, width), BF),
            jax.ShapeDtypeStruct((8, width), F32),
        ],
        compiler_params=pltpu.CompilerParams(vmem_limit_bytes=28 * 2**20),
        cost_estimate=SMALL,
        name="patch_back",
    )(*parts, x, grad, gain, w_query, w_key, w_value)


def assemble_kernel(recipe, place_ref, *refs):
    streams = len(refs) - len(recipe)
    ins, outs = refs[:streams], refs[streams:]
    step = pl.program_id(0)
    for far in range(2):

        @pl.when((step >= 4) == (far == 1))
        def _(far=far):
            for out_ref, pieces in zip(outs, recipe):
                at = 0
                for stream, first, columns in pieces:
                    part = ins[2 * stream + far][0, :, first : first + columns]
                    out_ref[:, at : at + columns] = part.astype(F32)
                    at += columns


def assemble(place, streams, swapped, recipe):
    rows = streams[0][0].shape[1]
    in_specs = []
    for (near, far), swap in zip(streams, swapped):

        def near_at(g, place, swap=swap):
            at = jnp.minimum(g, 3)
            return ((at >> 1) | ((at & 1) << 1) if swap else at, 0, 0)

        def far_at(g, place, swap=swap):
            at = jnp.maximum(g - 4, 0)
            return ((at >> 1) | ((at & 1) << 1) if swap else at, 0, 0)

        in_specs += [
            pl.BlockSpec((1, rows, near.shape[2]), near_at),
            pl.BlockSpec((1, rows, far.shape[2]), far_at),
        ]
    widths = [sum(columns for _, _, columns in pieces) for pieces in recipe]
    return pl.pallas_call(
        functools.partial(assemble_kernel, recipe),
        grid_spec=pltpu.PrefetchScalarGridSpec(
            num_scalar_prefetch=1,
            grid=(8,),
            in_specs=in_specs,
            out_specs=[pl.BlockSpec((rows, w), lambda g, place: (g ^ place[2], 0)) for w in widths],
        ),
        out_shape=[jax.ShapeDtypeStruct((8 * rows, w), F32) for w in widths],
        compiler_params=pltpu.CompilerParams(vmem_limit_bytes=24 * 2**20),
        cost_estimate=SMALL,
        name="assemble",
    )(place, *[part for pair in streams for part in pair])


def assemble_turned_kernel(place_ref, *refs):
    *ins, out_ref, rows_ref = refs
    height = ins[0].shape[1]
    step = pl.program_id(0)
    for stream in range(2):

        @pl.when((step >= pl.num_programs(0) // 2) == (stream == 1))
        def _(stream=stream):
            for far in range(2):
                for at in range(4):
                    spot = (at >> 1) | ((at & 1) << 1) if stream else at
                    block = (4 * far + spot) ^ place_ref[2]
                    start = pl.multiple_of(block * height, height)
                    part = ins[2 * stream + far][at]
                    rows_ref[pl.ds(start, height), :] = part.astype(F32)

    out_ref[...] = jnp.transpose(rows_ref[...])


def assemble_turned(place, streams, first, columns):
    rows = streams[0][0].shape[1]
    chunk = 256
    half = columns // 2 // chunk
    skip = first // chunk

    def early(g, place):
        return (0, 0, skip + jnp.minimum(g, half - 1))

    def late(g, place):
        return (0, 0, skip + jnp.maximum(g - half, 0))

    block = (4, rows, chunk)
    return pl.pallas_call(
        assemble_turned_kernel,
        grid_spec=pltpu.PrefetchScalarGridSpec(
            num_scalar_prefetch=1,
            grid=(2 * half,),
            in_specs=[pl.BlockSpec(block, where) for where in (early, early, late, late)],
            out_specs=pl.BlockSpec((chunk, 8 * rows), lambda g, place: (g, 0)),
            scratch_shapes=[pltpu.VMEM((8 * rows, chunk), F32)],
        ),
        out_shape=jax.ShapeDtypeStruct((columns, 8 * rows), F32),
        compiler_params=pltpu.CompilerParams(vmem_limit_bytes=12 * 2**20),
        cost_estimate=SMALL,
        name="assemble_turned",
    )(place, *[part for pair in streams for part in pair])


CORE, ACROSS, ALONG = 1, 2, 4


def flip(axis, bit):
    count = lax.axis_size(axis)
    return [(i, i ^ bit) for i in range(count)]


def swap(array, axis, bit):
    return lax.ppermute(array, axis, flip(axis, bit))


def take(array, number, axis=0):
    return lax.dynamic_index_in_dim(array, number, axis, keepdims=False)


def add_low(left, right):
    return (left.astype(F32) + right.astype(F32)).astype(BF)


def apart(blocks):
    here = lax.axis_index("band")
    return tuple(take(blocks, here ^ bit) for bit in range(blocks.shape[0]))


def exchange(pieces):
    return pieces[:1] + tuple(swap(piece, "band", bit + 1) for bit, piece in enumerate(pieces[1:]))


def in_order(*pieces):
    here = lax.axis_index("band")
    stacked = jnp.stack(pieces)
    return jnp.stack([take(stacked, here ^ band) for band in range(len(pieces))])


def far_bits():
    plots = lax.axis_size("plots")
    band = lax.axis_size("band")
    bits = [("plots", 1 << n) for n in range(3, plots.bit_length() - 1)]
    return bits + [("band", 1 << n) for n in range(band.bit_length() - 1)]


class Line:
    def __init__(self):
        self.last = ()

    def __call__(self, step, *inputs):
        inputs, _ = lax.optimization_barrier((inputs, self.last))
        self.last = step(*inputs)
        return self.last


def halve(near, arrived):
    half = near.shape[0] // 2
    return add_low(near[:half], arrived[:half]), add_low(near[half:], arrived[half:])


def settle(near, arrived):
    return add_low(near[0], arrived[0])


def split_far(axis, bit):
    def step(matrix):
        mine = (lax.axis_index(axis) // bit) % 2
        halves = matrix.reshape(2, matrix.shape[0] // 2, matrix.shape[1])
        return take(halves, mine), take(halves, 1 - mine)

    return step


def split_sum(axis, bit):
    return lambda near, arrived: split_far(axis, bit)(add_low(near, arrived))


def join_far(axis, bit):
    def step(matrix, other):
        mine = (lax.axis_index(axis) // bit) % 2
        return jnp.where(
            mine == 0, jnp.concatenate([matrix, other]), jnp.concatenate([other, matrix])
        )

    return step


def join(near, arrived):
    return jnp.concatenate([near, arrived])


def rms_norm(values, gain):
    inverse = lax.rsqrt(jnp.mean(values * values, axis=-1, keepdims=True) + 1e-06)
    return values * inverse * gain


def per_device(
    patches,
    norm1_gain,
    w_query,
    w_key,
    w_value,
    w_out,
    norm2_gain,
    w_gate,
    w_up,
    w_down,
    out_grad,
    plot_rows,
    plot_cols,
    global_index,
):
    width = patches.shape[2]
    here = lax.axis_index("band")
    run = Line()
    slots = patches.shape[0] * patches.shape[1]
    pieces = exchange(run(apart, patches))
    w_down_t, w_query_t = run(turn, w_down), run(turn, w_query)
    w_key_t, w_value_t = run(turn, w_key), run(turn, w_value)
    w_gate_t, w_up_t, w_out_t = run(turn, w_gate), run(turn, w_up), run(turn, w_out)
    x_low = run(in_order, *pieces).reshape(slots, width)
    limits = jnp.stack([take(plot_rows, here), take(plot_cols, here)])
    chosen = take(global_index, here)
    index = jnp.broadcast_to(chosen[:, None], (chosen.shape[0], 128))
    index_t = jnp.broadcast_to(chosen[None, :], (8, chosen.shape[0]))

    me = lax.axis_index("plots")
    core, across, along = me % 2, (me // ACROSS) % 2, (me // ALONG) % 2
    square, square_t = 2 * across + along, 2 * along + across
    whole = 4 * core + square
    place_near = jnp.stack([core, square, whole])
    place_far = jnp.stack([1 - core, square, whole])
    place_near_t = jnp.stack([core, square_t, whole])
    place_far_t = jnp.stack([1 - core, square_t, whole])
    ff = w_gate.shape[1]

    def front(x_low, gain, w_query, w_key, w_value):
        hidden = rms_norm(x_low.astype(F32), gain).astype(BF)
        query = dot_nn(hidden, w_query).astype(BF)
        keys = dot_nn(hidden, w_key).astype(BF)
        values = dot_nn(hidden, w_value).astype(BF)
        return hidden, query, keys, values

    def middle(x_low, attended, w_out, gain):
        resid = x_low.astype(F32) + dot_nn(attended, w_out)
        hidden2 = rms_norm(resid, gain).astype(BF)
        return resid, hidden2

    hidden, query, keys, values = run(front, x_low, norm1_gain, w_query, w_key, w_value)
    dy_pieces = exchange(run(apart, out_grad))
    attended, lse = run(attention, query, keys, values, limits, index)
    resid, hidden2 = run(middle, x_low, attended, w_out, norm2_gain)
    hidden2_t = run(turn, hidden2)
    attended_t = run(turn, attended)
    hidden_t = run(turn, hidden)
    dy = run(in_order, *dy_pieces).reshape(slots, width)
    dy_t = run(turn, dy)
    place_ffn = jnp.stack([core, square, square_t])
    inner, grad_gate, grad_up, ffn_near, ffn_far = run(
        ffn, place_ffn, hidden2, hidden2_t, dy, dy_t, w_gate, w_up, w_down_t
    )
    core_swap = functools.partial(swap, axis="plots", bit=CORE)
    across_swap = functools.partial(swap, axis="plots", bit=ACROSS)
    along_swap = functools.partial(swap, axis="plots", bit=ALONG)
    far = far_bits()

    def grad_of(place, swapped, *spans):
        return lambda left, rights, norms=(): weight_grad(
            place, left, rights, spans, swapped, norms
        )

    def side(*parts):
        return split_far(*far[0])(jnp.concatenate(parts, 1))

    ffn_come = core_swap(ffn_far)
    mixed_out = run(
        lambda resid, inner, w: (resid + dot_nn(inner, w)).astype(BF), resid, inner, w_down
    )

    def first_halves(near, come):
        total = add_low(near, come)
        one = jnp.concatenate([total[0], total[2, :, :, : ff // 2]], 2)
        two = jnp.concatenate([total[1], total[2, :, :, ff // 2 :]], 2)
        return (one[:2], one[2:]), (two[:2], two[2:])

    (gate_near, gate_go), (up_near, up_go) = run(first_halves, ffn_near, ffn_come)
    gate_come, up_come = across_swap(gate_go), along_swap(up_go)
    mixed_pieces = exchange(run(apart, mixed_out.reshape(patches.shape)))

    def ffn_back(resid, dy, gain, grad_gate, grad_up, w_gate, w_up):
        grad = dot_nn(grad_gate, w_gate) + dot_nn(grad_up, w_up)
        pulled, norm2 = norm_back(resid, gain, grad)
        pulled = pulled + dy.astype(F32)
        return pulled, pulled.astype(BF), jnp.broadcast_to(norm2, (8, width))

    grad_resid, resid_low, norm2 = run(
        ffn_back, resid, dy, norm2_gain, grad_gate, grad_up, w_gate_t, w_up_t
    )
    grad_attended = run(lambda a, w: dot_nn(a, w).astype(BF), resid_low, w_out_t)
    square_grad = [(0, 0, width)]
    resid_low = resid_low[None]
    out_come = core_swap(run(grad_of(place_far, False, square_grad), attended_t, [resid_low]))
    out_near = run(grad_of(place_near, False, square_grad), attended_t, [resid_low])

    pairs = width // PAIR
    third = pairs // 3

    def back(first):
        return run(
            functools.partial(attention_back, first=first, count=third),
            query,
            keys,
            values,
            grad_attended,
            lse,
            limits,
            index,
            index_t,
        )

    back_0 = back(0)
    gate_near, gate_go = run(halve, gate_near, gate_come)
    gate_come = along_swap(gate_go)
    up_near, up_go = run(halve, up_near, up_come)
    up_come = across_swap(up_go)
    out_near, leaves = run(halve, out_near, out_come)
    out_come = across_swap(leaves)
    back_1 = back(third)
    mixed_out = run(in_order, *mixed_pieces)
    ffn_near, leaves = run(
        lambda a, b, c, d: side(settle(a, b), settle(c, d)), gate_near, gate_come, up_near, up_come
    )
    ffn_come = swap(leaves, *far[0])
    out_near, leaves = run(halve, out_near, out_come)
    out_come = along_swap(leaves)
    back_2 = back(2 * third)
    for axis, bit in far[1:]:
        ffn_near, leaves = run(split_sum(axis, bit), ffn_near, ffn_come)
        ffn_come = swap(leaves, axis, bit)

    parts = [back_0, back_1, back_2]
    wide = third * PAIR
    q_spans = [(0, 0, wide), (1, 0, wide // 2)]
    v_spans = [(1, wide // 2, wide // 2), (2, 0, wide)]
    q_come = core_swap(run(grad_of(place_far, False, *[q_spans] * 3), hidden_t, parts))
    q_near = run(grad_of(place_near, False, *[q_spans] * 3), hidden_t, parts)
    q_near, leaves = run(halve, q_near, q_come)
    q_come = across_swap(leaves)
    patch_grad, norm1 = run(
        patch_back, parts, x_low, grad_resid, norm1_gain[None], w_query_t, w_key_t, w_value_t
    )
    norms = [norm1, norm2]
    v_come = core_swap(run(grad_of(place_far_t, True, *[v_spans] * 3), hidden_t, parts, norms))
    v_near = run(grad_of(place_near_t, True, *[v_spans] * 3), hidden_t, parts, norms)
    ffn_sum = run(add_low, ffn_near, ffn_come)
    ffn_come = swap(ffn_sum, *far[-1])
    v_near, leaves = run(halve, v_near, v_come)
    v_come = along_swap(leaves)
    q_near, leaves = run(halve, q_near, q_come)
    q_come = along_swap(leaves)
    for number in range(len(far) - 1, 0, -1):
        ffn_sum = run(join_far(*far[number]), ffn_sum, ffn_come)
        ffn_come = swap(ffn_sum, *far[number - 1])
    v_near, leaves = run(halve, v_near, v_come)
    v_come = across_swap(leaves)
    cut = 3 * ff // 2
    gate_all, up_all = run(
        lambda a, b: jnp.split(join_far(*far[0])(a, b)[None], [cut], 2), ffn_sum, ffn_come
    )
    gate_come, up_come = along_swap(gate_all), across_swap(up_all)
    qkv_near, leaves = run(
        lambda a, b, c, d, e, f: side(settle(a, b), settle(e, f), settle(c, d)),
        q_near,
        q_come,
        v_near,
        v_come,
        out_near,
        out_come,
    )
    qkv_come = swap(leaves, *far[0])
    gate_all = run(join, gate_all, gate_come)
    gate_come = across_swap(gate_all)
    up_all = run(join, up_all, up_come)
    up_come = along_swap(up_all)
    for axis, bit in far[1:]:
        qkv_near, leaves = run(split_sum(axis, bit), qkv_near, qkv_come)
        qkv_come = swap(leaves, axis, bit)
    qkv_sum = run(add_low, qkv_near, qkv_come)
    qkv_come = swap(qkv_sum, *far[-1])
    for number in range(len(far) - 1, 0, -1):
        qkv_sum = run(join_far(*far[number]), qkv_sum, qkv_come)
        qkv_come = swap(qkv_sum, *far[number - 1])
    cut = 3 * (wide + wide // 2) + width // 2
    q_all, v_all = run(
        lambda a, b: jnp.split(join_far(*far[0])(a, b)[None], [cut], 2), qkv_sum, qkv_come
    )
    q_come, v_come = along_swap(q_all), across_swap(v_all)
    patch_pieces = exchange(run(apart, patch_grad.reshape(patches.shape)))
    gate_all = run(join, gate_all, gate_come)
    gate_come = core_swap(gate_all)
    up_all = run(join, up_all, up_come)
    up_come = core_swap(up_all)
    q_all = run(join, q_all, q_come)
    q_come = across_swap(q_all)
    v_all = run(join, v_all, v_come)
    v_come = along_swap(v_all)
    patch_grad = run(in_order, *patch_pieces)
    ffn_streams = (gate_all, gate_come), (up_all, up_come)
    gate, up = run(
        lambda *streams: assemble(
            place_near, streams, [False, True], [[(0, 0, ff)], [(1, 0, ff)]]
        ),
        *ffn_streams,
    )
    down = run(lambda *streams: assemble_turned(place_near, streams, ff, ff), *ffn_streams)
    q_all = run(join, q_all, q_come)
    q_come = core_swap(q_all)
    v_all = run(join, v_all, v_come)
    v_come = core_swap(v_all)
    half = wide // 2
    rest = width // 2
    recipe = [[], [], [], [(0, 3 * (wide + half), rest), (1, 0, rest)]]
    for number in range(3):
        at = number * (wide + half)
        recipe[0].append((0, at, wide))
        recipe[1] += [(0, at + wide, half), (1, rest + at, half)]
        recipe[2].append((1, rest + at + half, wide))
    recipe.append([(1, rest + 3 * (wide + half), 128)])
    q_out, k_out, v_out, out, gains = run(
        lambda *streams: assemble(place_near, streams, [False, True], recipe),
        (q_all, q_come),
        (v_all, v_come),
    )
    return (
        mixed_out,
        patch_grad,
        gains[:, 0],
        q_out,
        k_out,
        v_out,
        out,
        gains[:, 1],
        gate,
        up,
        down,
    )


def solution(mesh):
    rows = P("plots", "band", None)
    in_specs = (rows,) + (P(),) * 9 + (rows, P("plots"), P("plots"), P("plots", None))
    out_specs = (rows, rows) + (P(),) * 9
    return jax.shard_map(
        per_device, mesh=mesh, in_specs=in_specs, out_specs=out_specs, check_vma=False
    )
```

```python
import functools

import jax
import jax.numpy as jnp
from jax import lax
from jax.experimental import pallas as pl
from jax.experimental.pallas import tpu as pltpu
from jax.sharding import PartitionSpec as P

H = 12
HD = 64
COLS = 64
WIN = 2
TILE_ROWS = 2
PAIR = 2 * HD
BF = jnp.bfloat16
F32 = jnp.float32
LOG2E = 1.4426950408889634
SCALE2 = LOG2E * HD ** (-0.5)
SMALL = pl.CostEstimate(flops=10**10, bytes_accessed=1, transcendentals=0)


def dot_nt(a, b):
    return lax.dot_general(a, b, (((1,), (1,)), ((), ())), preferred_element_type=F32)


def dot_nn(a, b):
    return lax.dot_general(a, b, (((1,), (0,)), ((), ())), preferred_element_type=F32)


def dot_tn(a, b):
    return lax.dot_general(a, b, (((0,), (0,)), ((), ())), preferred_element_type=F32)


def tiles_of(rows):
    out = []
    for first in range(0, rows, TILE_ROWS):
        low = max(first - WIN, 0)
        high = min(first + TILE_ROWS + WIN, rows)
        out.append((first * COLS, low * COLS, high * COLS))
    return out


def fill_bias(bias_ref, limits_ref, tiles):
    rows_here = limits_ref[0]
    cols_here = limits_ref[1]
    span = TILE_ROWS * COLS
    for number, (query_lo, key_lo, key_hi) in enumerate(tiles):
        count = key_hi - key_lo
        shape = (count, 2 * span)
        key = lax.broadcasted_iota(jnp.int32, shape, 0) + key_lo
        query = lax.broadcasted_iota(jnp.int32, shape, 1) % span + query_lo
        key_row = key // COLS
        apart = key_row - query // COLS
        seen = (apart <= WIN) & (apart >= -WIN) & (key_row < rows_here) & (key % COLS < cols_here)
        bias_ref[number, :count, :] = jnp.where(seen, 0.0, -1e30).astype(F32)


def picker_rows(index_ref, slots):
    chosen = index_ref[:, 0:1]
    lanes = lax.broadcasted_iota(jnp.int32, (chosen.shape[0], slots), 1)
    return (lanes == chosen).astype(F32).astype(BF)


def two_heads(block, lane):
    none = jnp.zeros_like(block)
    return jnp.concatenate([jnp.where(lane < HD, block, none), jnp.where(lane < HD, none, block)])


def own_heads(sums, span):
    return jnp.transpose(jnp.concatenate([sums[:HD, :span], sums[HD:, span:]], axis=0))


def attend_kernel(
    limits_ref, index_ref, q_ref, k_ref, v_ref, out_ref, lse_ref, bias_ref, pick_ref, value_t
):
    slots = q_ref.shape[0]
    tiles = tiles_of(slots // COLS)
    span = TILE_ROWS * COLS

    @pl.when(pl.program_id(0) == 0)
    def _():
        fill_bias(bias_ref, limits_ref, tiles)
        pick_ref[...] = picker_rows(index_ref, slots)

    global_keys = dot_nn(pick_ref[...], k_ref[...]).astype(BF)
    global_values_t = jnp.transpose(dot_nn(pick_ref[...], v_ref[...])).astype(BF)
    value_t[...] = jnp.transpose(v_ref[...].astype(F32)).astype(BF)
    lane = lax.broadcasted_iota(jnp.int32, (span, PAIR), 1)
    for number, (query_lo, key_lo, key_hi) in enumerate(tiles):
        count = key_hi - key_lo
        query = two_heads(q_ref[query_lo : query_lo + span, :], lane)
        window = dot_nt(k_ref[key_lo:key_hi, :], query) * SCALE2 + bias_ref[number, :count, :]
        wide = dot_nt(global_keys, query) * SCALE2
        highest = jnp.maximum(
            jnp.max(window, axis=0, keepdims=True), jnp.max(wide, axis=0, keepdims=True)
        )
        window = jnp.exp2(window - highest)
        wide = jnp.exp2(wide - highest)
        total = jnp.sum(window, axis=0, keepdims=True) + jnp.sum(wide, axis=0, keepdims=True)
        inverse = 1.0 / total
        sums = dot_nn(value_t[:, key_lo:key_hi], (window * inverse).astype(BF))
        sums = sums + dot_nn(global_values_t, (wide * inverse).astype(BF))
        lse_ref[0, number : number + 1, :] = highest + jnp.log2(total)
        out_ref[query_lo : query_lo + span, :] = own_heads(sums, span).astype(BF)


def attend_back_kernel(
    limits_ref,
    index_ref,
    index_t_ref,
    q_ref,
    k_ref,
    v_ref,
    g_ref,
    lse_ref,
    out_ref,
    bias_ref,
    pick_ref,
    pick_t_ref,
    key_t,
    dk_acc,
    dv_acc,
):
    slots = q_ref.shape[0]
    tiles = tiles_of(slots // COLS)
    span = TILE_ROWS * COLS
    globals_here = index_ref.shape[0]

    @pl.when(pl.program_id(0) == 0)
    def _():
        fill_bias(bias_ref, limits_ref, tiles)
        pick_ref[...] = picker_rows(index_ref, slots)
        down = lax.broadcasted_iota(jnp.int32, (slots, globals_here), 0)
        pick_t_ref[...] = (down == index_t_ref[0:1, :]).astype(F32).astype(BF)

    global_keys_f = dot_nn(pick_ref[...], k_ref[...])
    global_keys = global_keys_f.astype(BF)
    global_keys_t = jnp.transpose(global_keys_f).astype(BF)
    global_values = dot_nn(pick_ref[...], v_ref[...]).astype(BF)
    key_t[...] = jnp.transpose(k_ref[...].astype(F32)).astype(BF)
    dk_acc[...] = jnp.zeros_like(dk_acc)
    dv_acc[...] = jnp.zeros_like(dv_acc)
    dk_global = jnp.zeros((globals_here, PAIR), F32)
    dv_global = jnp.zeros((globals_here, PAIR), F32)
    lane = lax.broadcasted_iota(jnp.int32, (span, PAIR), 1)
    for number, (query_lo, key_lo, key_hi) in enumerate(tiles):
        count = key_hi - key_lo
        query = two_heads(q_ref[query_lo : query_lo + span, :], lane)
        grad = two_heads(g_ref[query_lo : query_lo + span, :], lane)
        keys = k_ref[key_lo:key_hi, :]
        values = v_ref[key_lo:key_hi, :]
        lse = lse_ref[0, number : number + 1, :]
        window = jnp.exp2(dot_nt(keys, query) * SCALE2 + (bias_ref[number, :count, :] - lse))
        wide = jnp.exp2(dot_nt(global_keys, query) * SCALE2 - lse)
        window_g = dot_nt(values, grad)
        wide_g = dot_nt(global_values, grad)
        weighted = jnp.sum(window * window_g, axis=0, keepdims=True) + jnp.sum(
            wide * wide_g, axis=0, keepdims=True
        )
        window_s = (window * (window_g - weighted)).astype(BF)
        wide_s = (wide * (wide_g - weighted)).astype(BF)
        dv_acc[key_lo:key_hi, :] += dot_nn(window.astype(BF), grad)
        dk_acc[key_lo:key_hi, :] += dot_nn(window_s, query)
        dv_global += dot_nn(wide.astype(BF), grad)
        dk_global += dot_nn(wide_s, query)
        sums = dot_nn(key_t[:, key_lo:key_hi], window_s) + dot_nn(global_keys_t, wide_s)
        sums = own_heads(sums, span) * HD ** (-0.5)
        out_ref[0, query_lo : query_lo + span, :] = sums.astype(BF)

    def spread(part):
        high = part.astype(BF)
        rest = part - high.astype(F32)
        middle = rest.astype(BF)
        low = (rest - middle.astype(F32)).astype(BF)
        picks = pick_t_ref[...]
        return dot_nn(picks, high) + dot_nn(picks, middle) + dot_nn(picks, low)

    out_ref[1] = ((dk_acc[...] + spread(dk_global)) * HD ** (-0.5)).astype(BF)
    out_ref[2] = (dv_acc[...] + spread(dv_global)).astype(BF)


def attention_parts(slots, width, globals_here):
    pairs = width // PAIR
    tall = (TILE_ROWS + 2 * WIN) * COLS
    tiles = slots // (TILE_ROWS * COLS)
    limits = pl.BlockSpec(memory_space=pltpu.SMEM)
    index = pl.BlockSpec((globals_here, 128), lambda p: (0, 0))
    block = pl.BlockSpec((slots, PAIR), lambda p: (0, p))
    lse = pl.BlockSpec((1, tiles, 2 * TILE_ROWS * COLS), lambda p: (p, 0, 0))
    bias = pltpu.VMEM((tiles, tall, 2 * TILE_ROWS * COLS), F32)
    pick = pltpu.VMEM((globals_here, slots), BF)
    return pairs, limits, index, block, lse, bias, pick


def attention(query, keys, values, limits, index):
    slots, width = query.shape
    globals_here = index.shape[0]
    pairs, lim, idx, block, lse, bias, pick = attention_parts(slots, width, globals_here)
    return pl.pallas_call(
        attend_kernel,
        grid=(pairs,),
        in_specs=[lim, idx, block, block, block],
        out_specs=[block, lse],
        out_shape=[
            jax.ShapeDtypeStruct((slots, width), BF),
            jax.ShapeDtypeStruct((pairs, *lse.block_shape[1:]), F32),
        ],
        scratch_shapes=[bias, pick, pltpu.VMEM((PAIR, slots), BF)],
        compiler_params=pltpu.CompilerParams(vmem_limit_bytes=12 * 2**20),
        cost_estimate=SMALL,
        name="attend",
    )(limits, index, query, keys, values)


def attention_back(query, keys, values, grad, lse_in, limits, index, index_t, first, count):
    slots, width = query.shape
    globals_here = index.shape[0]
    _, lim, idx, _, lse, bias, pick = attention_parts(slots, width, globals_here)
    idx_t = pl.BlockSpec((8, globals_here), lambda p: (0, 0))
    out_block = pl.BlockSpec((3, slots, PAIR), lambda p: (0, 0, p))
    block = pl.BlockSpec((slots, PAIR), lambda p: (0, first + p))
    lse = pl.BlockSpec(lse.block_shape, lambda p: (first + p, 0, 0))
    return pl.pallas_call(
        attend_back_kernel,
        grid=(count,),
        in_specs=[lim, idx, idx_t, block, block, block, block, lse],
        out_specs=out_block,
        out_shape=jax.ShapeDtypeStruct((3, slots, count * PAIR), BF),
        scratch_shapes=[
            bias,
            pick,
            pltpu.VMEM((slots, globals_here), BF),
            pltpu.VMEM((PAIR, slots), BF),
            pltpu.VMEM((slots, PAIR), F32),
            pltpu.VMEM((slots, PAIR), F32),
        ],
        compiler_params=pltpu.CompilerParams(vmem_limit_bytes=14 * 2**20),
        cost_estimate=SMALL,
        name="attend_back",
    )(limits, index, index_t, query, keys, values, grad, lse_in)


def turn_kernel(in_ref, out_ref):
    out_ref[...] = jnp.transpose(in_ref[...].astype(F32)).astype(BF)


def turn(matrix):
    rows, columns = matrix.shape
    wide = 256
    return pl.pallas_call(
        turn_kernel,
        grid=(columns // wide,),
        in_specs=[pl.BlockSpec((rows, wide), lambda g: (0, g))],
        out_specs=pl.BlockSpec((wide, rows), lambda g: (g, 0)),
        out_shape=jax.ShapeDtypeStruct((columns, rows), BF),
        compiler_params=pltpu.CompilerParams(vmem_limit_bytes=8 * 2**20),
        cost_estimate=SMALL,
        name="turn",
    )(matrix)


def weight_grad_kernel(groups, swapped, norms, place_ref, *refs):
    refs, out_ref = list(refs[:-1]), refs[-1]
    rows = out_ref.shape[1]
    half = 4 * rows
    start = pl.multiple_of(place_ref[0] * half, half)

    def store(sums, at):
        for block in range(4):
            spot = (block >> 1) | ((block & 1) << 1) if swapped else block
            part = sums[block * rows : (block + 1) * rows]
            out_ref[spot ^ place_ref[1], :, at : at + sums.shape[1]] = part

    at = 0
    for spans in groups:
        mine = refs.pop(0)[pl.ds(start, half), :]
        for span in spans:
            right = refs.pop(0)
            for number, first, count in span:
                for step in range(0, count, 512):
                    wide = min(512, count - step)
                    columns = right[number, :, first + step : first + step + wide]
                    store(dot_nn(mine, columns).astype(BF), at)
                    at += wide
    if norms:
        top = lax.broadcasted_iota(jnp.int32, (8, 128), 0) == 0
        lane = lax.broadcasted_iota(jnp.int32, (8, 128), 1)
        columns = pl.ds(pl.multiple_of(start, 128), half)
        sums = jnp.zeros((half, 128), F32)
        for number, norm in enumerate(refs):
            picks = jnp.where(top & (lane == number), 1.0, 0.0)
            sums = sums + dot_tn(norm[:, columns], picks)
        store(sums.astype(BF), at)


TINY = pl.CostEstimate(flops=1, bytes_accessed=1, transcendentals=0)
IN_VMEM = pl.BlockSpec(memory_space=pltpu.VMEM)
IN_SMEM = pl.BlockSpec(memory_space=pltpu.SMEM)


def weight_grad(place, groups, norms=(), *, spans, swapped=False):
    half = groups[0][0].shape[0] // 2
    inputs = [array for left, rights in groups for array in (left, *rights)]
    total = sum(count for group in spans for span in group for _, _, count in span)
    total += 128 if norms else 0
    inputs += list(norms)
    return pl.pallas_call(
        functools.partial(weight_grad_kernel, spans, swapped, bool(norms)),
        in_specs=[IN_SMEM] + [IN_VMEM] * len(inputs),
        out_specs=IN_VMEM,
        out_shape=jax.ShapeDtypeStruct((4, half // 4, total), BF),
        compiler_params=pltpu.CompilerParams(vmem_limit_bytes=8 * 2**20),
        cost_estimate=SMALL,
        name="weight_grad",
    )(place, *inputs)


def ffn_kernel(
    place_ref,
    hidden_ref,
    hidden_t,
    dy_ref,
    dy_t,
    gate_w,
    up_w,
    down_w,
    inner_ref,
    gate_ref,
    up_ref,
    near_ref,
    far_ref,
):
    rows = 256
    slope = (2.0 / 3.141592653589793) ** 0.5
    for start in range(0, hidden_ref.shape[0], rows):
        here = slice(start, start + rows)
        gate = dot_nn(hidden_ref[here, :], gate_w[...])
        up = dot_nn(hidden_ref[here, :], up_w[...])
        back = dot_nn(dy_ref[here, :], down_w[...])
        square = gate * gate
        share = 0.5 + 0.5 * jnp.tanh(gate * (slope + (0.044715 * slope) * square))
        active = gate * share
        inner_ref[here, :] = (active * up).astype(BF)
        up_ref[here, :] = (back * active).astype(BF)
        steep = share + (active - active * share) * (
            2.0 * slope + (6.0 * 0.044715 * slope) * square
        )
        gate_ref[here, :] = (back * up * steep).astype(BF)
    height = near_ref.shape[2]
    late = pl.program_id(0) >= pl.num_programs(0) // 2
    turned = (False, True, late)
    lefts, rights = (hidden_t, hidden_t, dy_t), (gate_ref, up_ref, inner_ref)
    for number, (left, right, swapped) in enumerate(zip(lefts, rights, turned)):
        sums = dot_nn(left[...], right[...]).astype(BF)
        for half in range(2):

            def put(target, half=half, sums=sums, number=number, swapped=swapped):
                for block in range(4):
                    straight = block ^ place_ref[1]
                    crossed = ((block >> 1) | ((block & 1) << 1)) ^ place_ref[2]
                    at = (4 * half + block) * height
                    spot = jnp.where(swapped, crossed, straight)
                    target[number, spot] = sums[at : at + height]

            pl.when(place_ref[0] == half)(functools.partial(put, near_ref))
            pl.when(place_ref[0] != half)(functools.partial(put, far_ref))


def ffn(place, hidden, hidden_t, dy, dy_t, w_gate, w_up, w_down_t):
    tokens, width = hidden.shape
    units = w_gate.shape[1]
    chunk = 512
    weight = pl.BlockSpec((width, chunk), lambda g: (0, g))
    wide = pl.BlockSpec((tokens, chunk), lambda g: (0, g))
    half = pl.BlockSpec((3, 4, width // 8, chunk), lambda g: (0, 0, 0, g))
    return pl.pallas_call(
        ffn_kernel,
        grid=(units // chunk,),
        in_specs=[IN_SMEM] + [IN_VMEM] * 4 + [weight] * 3,
        out_specs=[wide, wide, wide, half, half],
        out_shape=[jax.ShapeDtypeStruct((tokens, units), BF)] * 3
        + [jax.ShapeDtypeStruct((3, 4, width // 8, units), BF)] * 2,
        compiler_params=pltpu.CompilerParams(vmem_limit_bytes=32 * 2**20),
        cost_estimate=SMALL,
        name="ffn",
    )(place, hidden, hidden_t, dy, dy_t, w_gate, w_up, w_down_t)


def norm_back(values, gain, grad):
    inverse = lax.rsqrt(jnp.mean(values * values, axis=-1, keepdims=True) + 1e-06)
    scaled = values * inverse
    pulled = grad * gain
    shared = jnp.mean(scaled * pulled, axis=-1, keepdims=True)
    return inverse * (pulled - scaled * shared), jnp.sum(grad * scaled, axis=0, keepdims=True)


def patch_kernel(splits, *refs):
    parts, refs = refs[:splits], refs[splits:]
    x_ref, grad_ref, gain_ref, *weights, out_ref, norm_ref = refs
    grad = 0.0
    for number, weight in enumerate(weights):
        part = jnp.concatenate([ref[number] for ref in parts], axis=1)
        grad = grad + dot_nn(part, weight[...])
    pulled, gain = norm_back(x_ref[...].astype(F32), gain_ref[...], grad)
    out_ref[...] = (pulled + grad_ref[...]).astype(BF)

    @pl.when(pl.program_id(0) == 0)
    def _():
        norm_ref[...] = jnp.zeros_like(norm_ref)

    norm_ref[0:1, :] += gain


def patch_back(parts, x, grad, gain, w_query, w_key, w_value):
    tokens, width = x.shape
    rows = 512
    slim = pl.BlockSpec((rows, width), lambda g: (g, 0))
    part_specs = [pl.BlockSpec((3, rows, part.shape[2]), lambda g: (0, g, 0)) for part in parts]
    return pl.pallas_call(
        functools.partial(patch_kernel, len(parts)),
        grid=(tokens // rows,),
        in_specs=part_specs + [slim, slim] + [IN_VMEM] * 4,
        out_specs=[slim, pl.BlockSpec((8, width), lambda g: (0, 0))],
        out_shape=[
            jax.ShapeDtypeStruct((tokens, width), BF),
            jax.ShapeDtypeStruct((8, width), F32),
        ],
        compiler_params=pltpu.CompilerParams(vmem_limit_bytes=22 * 2**20),
        cost_estimate=SMALL,
        name="patch_back",
    )(*parts, x, grad, gain, w_query, w_key, w_value)


def assemble_kernel(recipe, place_ref, near_ref, far_ref, *outs):
    step = pl.program_id(0)
    for far, ref in enumerate((near_ref, far_ref)):

        @pl.when((step >= 4) == (far == 1))
        def _(ref=ref):
            for out_ref, pieces in zip(outs, recipe):
                at = 0
                for first, columns in pieces:
                    part = ref[0, :, first : first + columns]
                    out_ref[:, at : at + columns] = part.astype(F32)
                    at += columns


def assemble(place, near, far, recipe):
    rows = near.shape[1]
    block = (1, rows, near.shape[2])
    widths = [sum(columns for _, columns in pieces) for pieces in recipe]
    return pl.pallas_call(
        functools.partial(assemble_kernel, recipe),
        grid_spec=pltpu.PrefetchScalarGridSpec(
            num_scalar_prefetch=1,
            grid=(8,),
            in_specs=[
                pl.BlockSpec(block, lambda g, place: (jnp.minimum(g, 3), 0, 0)),
                pl.BlockSpec(block, lambda g, place: (jnp.maximum(g - 4, 0), 0, 0)),
            ],
            out_specs=[pl.BlockSpec((rows, w), lambda g, place: (g ^ place[2], 0)) for w in widths],
        ),
        out_shape=[jax.ShapeDtypeStruct((8 * rows, w), F32) for w in widths],
        compiler_params=pltpu.CompilerParams(vmem_limit_bytes=16 * 2**20),
        cost_estimate=SMALL,
        name="assemble",
    )(place, near, far)


def assemble_turned_kernel(place_ref, near_ref, far_ref, out_ref, rows_ref):
    height = near_ref.shape[1]
    for far, ref in enumerate((near_ref, far_ref)):
        for at in range(4):
            block = (4 * far + at) ^ place_ref[2]
            start = pl.multiple_of(block * height, height)
            rows_ref[pl.ds(start, height), :] = ref[at].astype(F32)
    out_ref[...] = jnp.transpose(rows_ref[...])


def assemble_turned(place, near, far, firsts, columns):
    rows = near.shape[1]
    chunk = 256
    half = columns // 2 // chunk
    one, two = (first // chunk for first in firsts)

    def where(g, place):
        return (0, 0, jnp.where(g < half, one + g, two + g - half))

    return pl.pallas_call(
        assemble_turned_kernel,
        grid_spec=pltpu.PrefetchScalarGridSpec(
            num_scalar_prefetch=1,
            grid=(2 * half,),
            in_specs=[pl.BlockSpec((4, rows, chunk), where)] * 2,
            out_specs=pl.BlockSpec((chunk, 8 * rows), lambda g, place: (g, 0)),
            scratch_shapes=[pltpu.VMEM((8 * rows, chunk), F32)],
        ),
        out_shape=jax.ShapeDtypeStruct((columns, 8 * rows), F32),
        compiler_params=pltpu.CompilerParams(vmem_limit_bytes=12 * 2**20),
        cost_estimate=SMALL,
        name="assemble_turned",
    )(place, near, far)


def small(name, kernel, shapes, *inputs, scalars=()):
    many = [jax.ShapeDtypeStruct(shape, BF) for shape in shapes]
    scalars = [jnp.stack(scalars)] if scalars else []
    return pl.pallas_call(
        kernel,
        in_specs=[IN_SMEM] * len(scalars) + [IN_VMEM] * len(inputs),
        out_specs=[IN_VMEM] * len(many),
        out_shape=many,
        compiler_params=pltpu.CompilerParams(vmem_limit_bytes=8 * 2**20),
        cost_estimate=TINY,
        name=name,
    )(*scalars, *inputs)


def add_low(left, right):
    return (left.astype(F32) + right.astype(F32)).astype(BF)


def halve(near, arrived):
    half = near.shape[0] // 2
    shape = (half, *near.shape[1:])

    def kernel(near, come, stays, leaves):
        for block in range(half):
            stays[block] = add_low(near[block], come[block])
            leaves[block] = add_low(near[half + block], come[half + block])

    return small("halve", kernel, [shape, shape], near, arrived)


def first_halves_kernel(near, come, one_stays, one_leaves, two_stays, two_leaves):
    step = pl.program_id(0)
    units = near.shape[3]
    half = units // 2
    for number, outs in enumerate(((one_stays, two_stays), (one_leaves, two_leaves))):

        @pl.when((step >= 2) == (number == 1))
        def _(outs=outs):
            last = add_low(near[2, 0], come[2, 0])
            for stream, out in enumerate(outs):
                out[0, :, :units] = add_low(near[stream, 0], come[stream, 0])
                out[0, :, units:] = last[:, stream * half : (stream + 1) * half]


def first_halves(near, come):
    _, blocks, rows, units = near.shape
    wide = units + units // 2
    stays = pl.BlockSpec((1, rows, wide), lambda g: (jnp.minimum(g, 1), 0, 0))
    leaves = pl.BlockSpec((1, rows, wide), lambda g: (jnp.maximum(g - 2, 0), 0, 0))
    block = pl.BlockSpec((3, 1, rows, units), lambda g: (0, g, 0, 0))
    one, one_go, two, two_go = pl.pallas_call(
        first_halves_kernel,
        grid=(blocks,),
        in_specs=[block, block],
        out_specs=[stays, leaves, stays, leaves],
        out_shape=[jax.ShapeDtypeStruct((2, rows, wide), BF)] * 4,
        compiler_params=pltpu.CompilerParams(vmem_limit_bytes=14 * 2**20),
        cost_estimate=SMALL,
        name="first_halves",
    )(near, come)
    return (one, one_go), (two, two_go)


def join(near, arrived):
    half = near.shape[0]

    def kernel(near, come, out):
        for block in range(half):
            out[block] = near[block]
            out[half + block] = come[block]

    return small("join", kernel, [(2 * half, *near.shape[1:])], near, arrived)[0]


def join_both(one, one_come, two, two_come):
    blocks, rows, wide = one.shape
    other = two.shape[2]

    def kernel(one, one_come, two, two_come, out):
        for number, (left, right) in enumerate(((one, two), (one_come, two_come))):
            for block in range(blocks):
                at = blocks * number + block
                out[at, :, :wide] = left[block]
                out[(at >> 1) | ((at & 1) << 1), :, wide:] = right[block]

    shape = (2 * blocks, rows, wide + other)
    return small("join_both", kernel, [shape], one, one_come, two, two_come)[0]


def apart(blocks):
    count = blocks.shape[0]

    def kernel(here, blocks, *outs):
        for bit, out in enumerate(outs):
            out[...] = blocks[here[0] ^ bit]

    return small(
        "apart", kernel, [blocks.shape[1:]] * count, blocks, scalars=[lax.axis_index("band")]
    )


def in_order(*pieces):
    count = len(pieces)

    def kernel(here, *refs):
        for bit in range(count):
            refs[count][here[0] ^ bit] = refs[bit][...]

    shape = (count, *pieces[0].shape)
    return small("in_order", kernel, [shape], *pieces, scalars=[lax.axis_index("band")])[0]


def bit_of(axis, bit):
    return (lax.axis_index(axis) // bit) % 2


def part_of(columns):
    size = -(-columns // 256) * 128
    return size, columns - size


def rows_apart(axis, bit):
    def step(*streams):
        height = streams[0].shape[1] // 2
        widths = [stream.shape[2] for stream in streams[::2]]
        shape = (height, sum(widths))

        def kernel(mine, *refs):
            ins, (stays, leaves) = refs[:-2], refs[-2:]
            for out, half in ((stays, mine[0]), (leaves, 1 - mine[0])):
                rows = pl.ds(pl.multiple_of(half * height, height), height)
                at = 0
                for near, come, wide in zip(ins[::2], ins[1::2], widths):
                    out[:, at : at + wide] = add_low(near[0, rows, :], come[0, rows, :])
                    at += wide

        return small(
            "rows_apart", kernel, [shape, shape], *streams, scalars=[bit_of(axis, bit)]
        )

    return step


def columns_apart(axis, bit):
    def step(near, come):
        size, skip = part_of(near.shape[1])
        shape = (near.shape[0], size)

        def kernel(mine, near, come, stays, leaves):
            for out, half in ((stays, mine[0]), (leaves, 1 - mine[0])):
                columns = pl.ds(pl.multiple_of(half * skip, 128), size)
                out[...] = add_low(near[:, columns], come[:, columns])

        return small(
            "columns_apart", kernel, [shape, shape], near, come, scalars=[bit_of(axis, bit)]
        )

    return step


def add_up(near, come):
    def kernel(near, come, out):
        out[...] = add_low(near[...], come[...])

    return small("add_up", kernel, [near.shape], near, come)[0]


def columns_join(axis, bit, columns):
    def step(near, come):
        size, skip = part_of(columns)

        def kernel(mine, near, come, out):
            for piece, half in ((near, mine[0]), (come, 1 - mine[0])):
                out[:, pl.ds(pl.multiple_of(half * skip, 128), size)] = piece[...]

        return small(
            "columns_join",
            kernel,
            [(near.shape[0], columns)],
            near,
            come,
            scalars=[bit_of(axis, bit)],
        )[0]

    return step


def rows_join(axis, bit, widths):
    def step(near, come):
        height = near.shape[0]

        def kernel(mine, near, come, *outs):
            for piece, half in ((near, mine[0]), (come, 1 - mine[0])):
                rows = pl.ds(pl.multiple_of(half * height, height), height)
                at = 0
                for out, wide in zip(outs, widths):
                    out[0, rows, :] = piece[:, at : at + wide]
                    at += wide

        shapes = [(1, 2 * height, wide) for wide in widths]
        return small("rows_join", kernel, shapes, near, come, scalars=[bit_of(axis, bit)])

    return step


CORE, ACROSS, ALONG = 1, 2, 4


def flip(axis, bit):
    count = lax.axis_size(axis)
    return [(i, i ^ bit) for i in range(count)]


def swap(array, axis, bit):
    return lax.ppermute(array, axis, flip(axis, bit))


def take(array, number, axis=0):
    return lax.dynamic_index_in_dim(array, number, axis, keepdims=False)


def exchange(pieces):
    return pieces[:1] + tuple(swap(piece, "band", bit + 1) for bit, piece in enumerate(pieces[1:]))


def far_bits():
    plots = lax.axis_size("plots")
    band = lax.axis_size("band")
    bits = [("plots", 1 << n) for n in range(3, plots.bit_length() - 1)]
    return bits + [("band", 1 << n) for n in range(band.bit_length() - 1)]


class Line:
    def __init__(self):
        self.last = ()

    def __call__(self, step, *inputs):
        inputs, _ = lax.optimization_barrier((inputs, self.last))
        self.last = step(*inputs)
        return self.last


def side(axis, bit):
    def step(*streams):
        sums = [add_low(near[0], come[0]) for near, come in zip(streams[::2], streams[1::2])]
        return split_far(axis, bit)(jnp.concatenate(sums, 1))

    return step


def split_far(axis, bit):
    def step(matrix):
        halves = matrix.reshape(2, matrix.shape[0] // 2, matrix.shape[1])
        mine = bit_of(axis, bit)
        return take(halves, mine), take(halves, 1 - mine)

    return step


def join_far(axis, bit):
    def step(matrix, other):
        return jnp.where(
            bit_of(axis, bit) == 0,
            jnp.concatenate([matrix, other]),
            jnp.concatenate([other, matrix]),
        )

    return step


def travel(run, widths, *streams):
    far = far_bits()
    if len(far) == 2:
        (first, second), columns = far, sum(widths)
        near, leaves = run(rows_apart(*first), *streams)
        come = swap(leaves, *first)
        yield
        near, leaves = run(columns_apart(*second), near, come)
        come = swap(leaves, *second)
        yield
        near = run(add_up, near, come)
        come = swap(near, *second)
        yield
        near = run(columns_join(*second, columns), near, come)
        come = swap(near, *first)
        yield
        return run(rows_join(*first, widths), near, come)
    near, leaves = run(side(*far[0]), *streams)
    come = swap(leaves, *far[0])
    yield
    for axis, bit in far[1:]:
        near, leaves = run(
            lambda near, come, far=(axis, bit): split_far(*far)(add_low(near, come)), near, come
        )
        come = swap(leaves, axis, bit)
        yield
    near = run(add_low, near, come)
    for axis, bit in far[::-1]:
        come = swap(near, axis, bit)
        yield
        near = run(join_far(axis, bit), near, come)
    cuts = [sum(widths[: n + 1]) for n in range(len(widths) - 1)]
    return run(lambda a: jnp.split(a[None], cuts, 2), near)


def rest_of(steps):
    while True:
        try:
            next(steps)
        except StopIteration as end:
            return end.value


def rms_norm(values, gain):
    inverse = lax.rsqrt(jnp.mean(values * values, axis=-1, keepdims=True) + 1e-06)
    return values * inverse * gain


def per_device(
    patches,
    norm1_gain,
    w_query,
    w_key,
    w_value,
    w_out,
    norm2_gain,
    w_gate,
    w_up,
    w_down,
    out_grad,
    plot_rows,
    plot_cols,
    global_index,
):
    width = patches.shape[2]
    here = lax.axis_index("band")
    run = Line()
    slots = patches.shape[0] * patches.shape[1]
    pieces = exchange(run(apart, patches))
    w_down_t, w_query_t = run(turn, w_down), run(turn, w_query)
    w_key_t, w_value_t = run(turn, w_key), run(turn, w_value)
    w_gate_t, w_up_t, w_out_t = run(turn, w_gate), run(turn, w_up), run(turn, w_out)
    x_low = run(in_order, *pieces).reshape(slots, width)
    limits = jnp.stack([take(plot_rows, here), take(plot_cols, here)])
    chosen = take(global_index, here)
    index = jnp.broadcast_to(chosen[:, None], (chosen.shape[0], 128))
    index_t = jnp.broadcast_to(chosen[None, :], (8, chosen.shape[0]))

    me = lax.axis_index("plots")
    core, across, along = me % 2, (me // ACROSS) % 2, (me // ALONG) % 2
    square, square_t = 2 * across + along, 2 * along + across
    whole = 4 * core + square
    place_near = jnp.stack([core, square, whole])
    place_far = jnp.stack([1 - core, square, whole])
    place_near_t = jnp.stack([core, square_t, whole])
    place_far_t = jnp.stack([1 - core, square_t, whole])
    ff = w_gate.shape[1]

    def front(x_low, gain, w_query, w_key, w_value):
        hidden = rms_norm(x_low.astype(F32), gain).astype(BF)
        query = dot_nn(hidden, w_query).astype(BF)
        keys = dot_nn(hidden, w_key).astype(BF)
        values = dot_nn(hidden, w_value).astype(BF)
        return hidden, query, keys, values

    def middle(x_low, attended, w_out, gain):
        resid = x_low.astype(F32) + dot_nn(attended, w_out)
        hidden2 = rms_norm(resid, gain).astype(BF)
        return resid, hidden2

    hidden, query, keys, values = run(front, x_low, norm1_gain, w_query, w_key, w_value)
    dy_pieces = exchange(run(apart, out_grad))
    attended, lse = run(attention, query, keys, values, limits, index)
    resid, hidden2 = run(middle, x_low, attended, w_out, norm2_gain)
    hidden2_t = run(turn, hidden2)
    dy = run(in_order, *dy_pieces).reshape(slots, width)
    dy_t = run(turn, dy)
    place_ffn = jnp.stack([core, square, square_t])
    inner, grad_gate, grad_up, ffn_near, ffn_far = run(
        ffn, place_ffn, hidden2, hidden2_t, dy, dy_t, w_gate, w_up, w_down_t
    )
    core_swap = functools.partial(swap, axis="plots", bit=CORE)
    across_swap = functools.partial(swap, axis="plots", bit=ACROSS)
    along_swap = functools.partial(swap, axis="plots", bit=ALONG)
    far = far_bits()

    ffn_come = core_swap(ffn_far)
    grad_hidden2 = run(
        lambda a, b, c, d: dot_nn(a, c) + dot_nn(b, d), grad_gate, grad_up, w_gate_t, w_up_t
    )
    (gate_near, gate_go), (up_near, up_go) = run(first_halves, ffn_near, ffn_come)
    gate_come, up_come = across_swap(gate_go), along_swap(up_go)

    def resid_back(resid, dy, gain, grad):
        pulled, norm2 = norm_back(resid, gain, grad)
        pulled = pulled + dy.astype(F32)
        return pulled, pulled.astype(BF), jnp.broadcast_to(norm2, (8, width))

    grad_resid, resid_low, norm2 = run(resid_back, resid, dy, norm2_gain, grad_hidden2)
    grad_attended = run(lambda a, w: dot_nn(a, w).astype(BF), resid_low, w_out_t)
    mixed_out = run(
        lambda resid, inner, w: (resid + dot_nn(inner, w)).astype(BF), resid, inner, w_down
    )
    mixed_pieces = exchange(run(apart, mixed_out.reshape(patches.shape)))

    third = width // PAIR // 3

    def back(first):
        return run(
            functools.partial(attention_back, first=first, count=third),
            query,
            keys,
            values,
            grad_attended,
            lse,
            limits,
            index,
            index_t,
        )

    back_0 = back(0)
    gate_near, gate_go = run(halve, gate_near, gate_come)
    gate_come = along_swap(gate_go)
    up_near, up_go = run(halve, up_near, up_come)
    up_come = across_swap(up_go)
    back_1 = back(third)
    attended_t = run(turn, attended)
    wide_ffn = ff + ff // 2
    ffn_steps = travel(run, [wide_ffn] * 2, gate_near, gate_come, up_near, up_come)
    next(ffn_steps)
    back_2 = back(2 * third)
    mixed_out = run(in_order, *mixed_pieces)
    hidden_t = run(turn, hidden)
    next(ffn_steps)

    parts = [back_0, back_1, back_2]
    wide = third * PAIR
    half = wide // 2
    rest = width // 2
    out_right = resid_low[None]
    groups = [(hidden_t, parts), (attended_t, [out_right])]
    q_spans = [[[(0, 0, wide), (1, 0, half)]] * 3, [[(0, 0, rest)]]]
    v_spans = [[[(1, half, half), (2, 0, wide)]] * 3, [[(0, rest, width - rest)]]]
    q_grad = functools.partial(weight_grad, spans=q_spans)
    patch_grad, norm1 = run(
        patch_back, parts, x_low, grad_resid, norm1_gain[None], w_query_t, w_key_t, w_value_t
    )
    v_grad = functools.partial(weight_grad, spans=v_spans, swapped=True)
    norms = [norm1, norm2]
    pieces = list(run(apart, patch_grad.reshape(patches.shape)))
    q_come = core_swap(run(q_grad, place_far, groups))
    next(ffn_steps)
    v_come = core_swap(run(v_grad, place_far_t, groups, norms))
    q_near = run(q_grad, place_near, groups)
    q_near, leaves = run(halve, q_near, q_come)
    q_come = across_swap(leaves)
    v_near = run(v_grad, place_near_t, groups, norms)
    v_near, leaves = run(halve, v_near, v_come)
    v_come = along_swap(leaves)
    pieces[1] = swap(pieces[1], "band", 1)
    next(ffn_steps)
    pieces[1] = run(lambda a: a, pieces[1])
    q_near, leaves = run(halve, q_near, q_come)
    q_come = along_swap(leaves)
    v_near, leaves = run(halve, v_near, v_come)
    v_come = across_swap(leaves)
    cut = 3 * (wide + half) + rest
    qkv_steps = travel(
        run, [cut, 3 * (wide + half) + width - rest + 128], q_near, q_come, v_near, v_come
    )
    next(qkv_steps)
    gate_all, up_all = rest_of(ffn_steps)
    gate_come, up_come = along_swap(gate_all), across_swap(up_all)
    next(qkv_steps)
    gate_all = run(join, gate_all, gate_come)
    gate_come = across_swap(gate_all)
    up_all = run(join, up_all, up_come)
    up_come = along_swap(up_all)
    next(qkv_steps)
    next(qkv_steps)
    q_all, v_all = rest_of(qkv_steps)
    q_come, v_come = along_swap(q_all), across_swap(v_all)
    far_piece = swap(run(lambda a: a, pieces[2]), "band", 2)
    ffn_near = run(join_both, gate_all, gate_come, up_all, up_come)
    ffn_come = core_swap(ffn_near)
    q_all = run(join, q_all, q_come)
    q_come = across_swap(q_all)
    v_all = run(join, v_all, v_come)
    v_come = along_swap(v_all)
    gate, up = run(
        lambda near, far: assemble(place_near, near, far, [[(0, ff)], [(wide_ffn, ff)]]),
        ffn_near,
        ffn_come,
    )
    pieces[2] = run(lambda a: a, far_piece)
    qkv_near = run(join_both, q_all, q_come, v_all, v_come)
    qkv_come = core_swap(qkv_near)
    pieces[3] = swap(run(lambda a: a, pieces[3]), "band", 3)
    down = run(
        lambda near, far: assemble_turned(place_near, near, far, (ff, wide_ffn + ff), ff),
        ffn_near,
        ffn_come,
    )
    recipe = [[], [], [], [(cut - rest, rest), (cut + 3 * (wide + half), width - rest)]]
    for number in range(3):
        at = number * (wide + half)
        recipe[0].append((at, wide))
        recipe[1] += [(at + wide, half), (cut + at, half)]
        recipe[2].append((cut + at + half, wide))
    recipe.append([(cut + 3 * (wide + half) + width - rest, 128)])
    q_out, k_out, v_out, out, gains = run(
        lambda near, far: assemble(place_near, near, far, recipe), qkv_near, qkv_come
    )
    patch_grad = run(in_order, *pieces)
    return (
        mixed_out,
        patch_grad,
        gains[:, 0],
        q_out,
        k_out,
        v_out,
        out,
        gains[:, 1],
        gate,
        up,
        down,
    )


def solution(mesh):
    rows = P("plots", "band", None)
    in_specs = (rows,) + (P(),) * 9 + (rows, P("plots"), P("plots"), P("plots", None))
    out_specs = (rows, rows) + (P(),) * 9
    return jax.shard_map(
        per_device, mesh=mesh, in_specs=in_specs, out_specs=out_specs, check_vma=False
    )
```

```python
import functools

import jax
import jax.numpy as jnp
from jax import lax
from jax.experimental import pallas as pl
from jax.experimental.pallas import tpu as pltpu
from jax.sharding import PartitionSpec as P

H = 12
HD = 64
COLS = 64
WIN = 2
TILE_ROWS = 2
PAIR = 2 * HD
BF = jnp.bfloat16
F32 = jnp.float32
LOG2E = 1.4426950408889634
SCALE2 = LOG2E * HD ** (-0.5)
SMALL = pl.CostEstimate(flops=10**10, bytes_accessed=1, transcendentals=0)

TINY = pl.CostEstimate(flops=1, bytes_accessed=1, transcendentals=0)
IN_VMEM = pl.BlockSpec(memory_space=pltpu.VMEM)
IN_SMEM = pl.BlockSpec(memory_space=pltpu.SMEM)


def dot_nt(a, b):
    return lax.dot_general(a, b, (((1,), (1,)), ((), ())), preferred_element_type=F32)


def dot_nn(a, b):
    return lax.dot_general(a, b, (((1,), (0,)), ((), ())), preferred_element_type=F32)


def dot_tn(a, b):
    return lax.dot_general(a, b, (((0,), (0,)), ((), ())), preferred_element_type=F32)


def tiles_of(rows):
    out = []
    for first in range(0, rows, TILE_ROWS):
        low = max(first - WIN, 0)
        high = min(first + TILE_ROWS + WIN, rows)
        out.append((first * COLS, low * COLS, high * COLS))
    return out


def fill_bias(bias_ref, limits_ref, tiles):
    rows_here = limits_ref[0]
    cols_here = limits_ref[1]
    span = TILE_ROWS * COLS
    for number, (query_lo, key_lo, key_hi) in enumerate(tiles):
        count = key_hi - key_lo
        shape = (count, 2 * span)
        key = lax.broadcasted_iota(jnp.int32, shape, 0) + key_lo
        query = lax.broadcasted_iota(jnp.int32, shape, 1) % span + query_lo
        key_row = key // COLS
        apart = key_row - query // COLS
        seen = (apart <= WIN) & (apart >= -WIN) & (key_row < rows_here) & (key % COLS < cols_here)
        bias_ref[number, :count, :] = jnp.where(seen, 0.0, -1e30).astype(F32)


def picker_rows(index_ref, slots):
    chosen = index_ref[:, 0:1]
    lanes = lax.broadcasted_iota(jnp.int32, (chosen.shape[0], slots), 1)
    return (lanes == chosen).astype(F32).astype(BF)


def two_heads(block, lane):
    none = jnp.zeros_like(block)
    return jnp.concatenate([jnp.where(lane < HD, block, none), jnp.where(lane < HD, none, block)])


def own_heads(sums, span):
    return jnp.transpose(jnp.concatenate([sums[:HD, :span], sums[HD:, span:]], axis=0))


def masks_kernel(limits_ref, index_ref, index_t_ref, bias_ref, pick_ref, pick_t_ref):
    slots = pick_ref.shape[1]
    fill_bias(bias_ref, limits_ref, tiles_of(slots // COLS))
    pick_ref[...] = picker_rows(index_ref, slots)
    down = lax.broadcasted_iota(jnp.int32, pick_t_ref.shape, 0)
    pick_t_ref[...] = (down == index_t_ref[0:1, :]).astype(F32).astype(BF)


def masks(limits, index, index_t, slots):
    count = index.shape[0]
    tall = (TILE_ROWS + 2 * WIN) * COLS
    tiles = slots // (TILE_ROWS * COLS)
    return pl.pallas_call(
        masks_kernel,
        in_specs=[IN_SMEM, IN_VMEM, IN_VMEM],
        out_specs=[IN_VMEM] * 3,
        out_shape=[
            jax.ShapeDtypeStruct((tiles, tall, 2 * TILE_ROWS * COLS), F32),
            jax.ShapeDtypeStruct((count, slots), BF),
            jax.ShapeDtypeStruct((slots, count), BF),
        ],
        compiler_params=pltpu.CompilerParams(vmem_limit_bytes=8 * 2**20),
        cost_estimate=SMALL,
        name="masks",
    )(limits, index, index_t)


def attend_kernel(bias_ref, pick_ref, q_ref, k_ref, v_ref, out_ref, lse_ref, value_t):
    slots = q_ref.shape[0]
    tiles = tiles_of(slots // COLS)
    span = TILE_ROWS * COLS
    global_keys = dot_nn(pick_ref[...], k_ref[...]).astype(BF)
    global_values_t = jnp.transpose(dot_nn(pick_ref[...], v_ref[...])).astype(BF)
    value_t[...] = jnp.transpose(v_ref[...].astype(F32)).astype(BF)
    lane = lax.broadcasted_iota(jnp.int32, (span, PAIR), 1)
    for number, (query_lo, key_lo, key_hi) in enumerate(tiles):
        count = key_hi - key_lo
        query = two_heads(q_ref[query_lo : query_lo + span, :], lane)
        window = dot_nt(k_ref[key_lo:key_hi, :], query) * SCALE2 + bias_ref[number, :count, :]
        wide = dot_nt(global_keys, query) * SCALE2
        highest = jnp.maximum(
            jnp.max(window, axis=0, keepdims=True), jnp.max(wide, axis=0, keepdims=True)
        )
        window = jnp.exp2(window - highest)
        wide = jnp.exp2(wide - highest)
        total = jnp.sum(window, axis=0, keepdims=True) + jnp.sum(wide, axis=0, keepdims=True)
        inverse = 1.0 / total
        sums = dot_nn(value_t[:, key_lo:key_hi], (window * inverse).astype(BF))
        sums = sums + dot_nn(global_values_t, (wide * inverse).astype(BF))
        lse_ref[0, number : number + 1, :] = highest + jnp.log2(total)
        out_ref[query_lo : query_lo + span, :] = own_heads(sums, span).astype(BF)


def attend_back_kernel(
    bias_ref,
    pick_ref,
    pick_t_ref,
    q_ref,
    k_ref,
    v_ref,
    g_ref,
    lse_ref,
    out_ref,
    key_t,
    dk_acc,
    dv_acc,
):
    slots = q_ref.shape[0]
    tiles = tiles_of(slots // COLS)
    span = TILE_ROWS * COLS
    globals_here = pick_ref.shape[0]
    global_keys_f = dot_nn(pick_ref[...], k_ref[...])
    global_keys = global_keys_f.astype(BF)
    global_keys_t = jnp.transpose(global_keys_f).astype(BF)
    global_values = dot_nn(pick_ref[...], v_ref[...]).astype(BF)
    key_t[...] = jnp.transpose(k_ref[...].astype(F32)).astype(BF)
    dk_acc[...] = jnp.zeros_like(dk_acc)
    dv_acc[...] = jnp.zeros_like(dv_acc)
    dk_global = jnp.zeros((globals_here, PAIR), F32)
    dv_global = jnp.zeros((globals_here, PAIR), F32)
    lane = lax.broadcasted_iota(jnp.int32, (span, PAIR), 1)
    for number, (query_lo, key_lo, key_hi) in enumerate(tiles):
        count = key_hi - key_lo
        query = two_heads(q_ref[query_lo : query_lo + span, :], lane)
        grad = two_heads(g_ref[query_lo : query_lo + span, :], lane)
        keys = k_ref[key_lo:key_hi, :]
        values = v_ref[key_lo:key_hi, :]
        lse = lse_ref[0, number : number + 1, :]
        window = jnp.exp2(dot_nt(keys, query) * SCALE2 + (bias_ref[number, :count, :] - lse))
        wide = jnp.exp2(dot_nt(global_keys, query) * SCALE2 - lse)
        window_g = dot_nt(values, grad)
        wide_g = dot_nt(global_values, grad)
        weighted = jnp.sum(window * window_g, axis=0, keepdims=True) + jnp.sum(
            wide * wide_g, axis=0, keepdims=True
        )
        window_s = (window * (window_g - weighted)).astype(BF)
        wide_s = (wide * (wide_g - weighted)).astype(BF)
        dv_acc[key_lo:key_hi, :] += dot_nn(window.astype(BF), grad)
        dk_acc[key_lo:key_hi, :] += dot_nn(window_s, query)
        dv_global += dot_nn(wide.astype(BF), grad)
        dk_global += dot_nn(wide_s, query)
        sums = dot_nn(key_t[:, key_lo:key_hi], window_s) + dot_nn(global_keys_t, wide_s)
        sums = own_heads(sums, span) * HD ** (-0.5)
        out_ref[0, query_lo : query_lo + span, :] = sums.astype(BF)

    def spread(part):
        high = part.astype(BF)
        rest = part - high.astype(F32)
        middle = rest.astype(BF)
        low = (rest - middle.astype(F32)).astype(BF)
        picks = pick_t_ref[...]
        return dot_nn(picks, high) + dot_nn(picks, middle) + dot_nn(picks, low)

    out_ref[1] = ((dk_acc[...] + spread(dk_global)) * HD ** (-0.5)).astype(BF)
    out_ref[2] = (dv_acc[...] + spread(dv_global)).astype(BF)


def attention(query, keys, values, bias, pick):
    slots, width = query.shape
    pairs = width // PAIR
    block = pl.BlockSpec((slots, PAIR), lambda p: (0, p))
    tiles = slots // (TILE_ROWS * COLS)
    return pl.pallas_call(
        attend_kernel,
        grid=(pairs,),
        in_specs=[IN_VMEM, IN_VMEM, block, block, block],
        out_specs=[block, pl.BlockSpec((1, tiles, 2 * TILE_ROWS * COLS), lambda p: (p, 0, 0))],
        out_shape=[
            jax.ShapeDtypeStruct((slots, width), BF),
            jax.ShapeDtypeStruct((pairs, tiles, 2 * TILE_ROWS * COLS), F32),
        ],
        scratch_shapes=[pltpu.VMEM((PAIR, slots), BF)],
        compiler_params=pltpu.CompilerParams(vmem_limit_bytes=10 * 2**20),
        cost_estimate=SMALL,
        name="attend",
    )(bias, pick, query, keys, values)


def attention_back(query, keys, values, grad, lse, bias, pick, pick_t, first, count):
    slots = query.shape[0]
    block = pl.BlockSpec((slots, PAIR), lambda p: (0, first + p))
    return pl.pallas_call(
        attend_back_kernel,
        grid=(count,),
        in_specs=[IN_VMEM] * 3
        + [block] * 4
        + [pl.BlockSpec((1, *lse.shape[1:]), lambda p: (first + p, 0, 0))],
        out_specs=pl.BlockSpec((3, slots, PAIR), lambda p: (0, 0, p)),
        out_shape=jax.ShapeDtypeStruct((3, slots, count * PAIR), BF),
        scratch_shapes=[
            pltpu.VMEM((PAIR, slots), BF),
            pltpu.VMEM((slots, PAIR), F32),
            pltpu.VMEM((slots, PAIR), F32),
        ],
        compiler_params=pltpu.CompilerParams(vmem_limit_bytes=12 * 2**20),
        cost_estimate=SMALL,
        name="attend_back",
    )(bias, pick, pick_t, query, keys, values, grad, lse)


def project(piece, gain, weights):
    hidden = rms_norm(piece.astype(F32), gain).astype(BF)
    return [hidden] + [dot_nn(hidden, weight[...]).astype(BF) for weight in weights]


def front(piece, gain, *weights):
    def kernel(piece, gain, *refs):
        for out, value in zip(refs[3:], project(piece[...], gain[...], refs[:3])):
            out[...] = value

    return small("front", kernel, [piece.shape] * 4, piece, gain, *weights, cost=SMALL)


def front_last(pieces, parts, gain, *weights):
    count, (rows, width) = len(pieces), pieces[0].shape

    def kernel(here, *refs):
        refs = list(refs)
        pieces = [refs.pop(0) for _ in range(count)]
        parts = [[refs.pop(0) for _ in range(4)] for _ in range(count - 1)]
        gain, weights, outs = refs[0], refs[1:4], refs[4:]
        for bit in range(count):
            place = pl.ds(pl.multiple_of((here[0] ^ bit) * rows, rows), rows)
            outs[0][place, :] = pieces[bit][...]
            if bit < count - 1:
                values = [part[...] for part in parts[bit]]
            else:
                values = project(pieces[bit][...], gain[...], weights)
            for out, value in zip(outs[1:], values):
                out[place, :] = value

    return small(
        "front_last",
        kernel,
        [(count * rows, width)] * 5,
        *pieces,
        *[array for part in parts for array in part],
        gain,
        *weights,
        scalars=[lax.axis_index("band")],
        cost=SMALL,
    )


def middle_kernel(x_ref, attended_ref, w_out, gain_ref, resid_ref, hidden_ref, hidden_t):
    resid = x_ref[...].astype(F32) + dot_nn(attended_ref[...], w_out[...])
    resid_ref[...] = resid
    hidden = rms_norm(resid, gain_ref[...])
    hidden_ref[...] = hidden.astype(BF)
    hidden_t[...] = jnp.transpose(hidden).astype(BF)


def middle(x, attended, w_out, gain):
    slots, width = x.shape
    rows = 256
    block = pl.BlockSpec((rows, width), lambda g: (g, 0))
    return pl.pallas_call(
        middle_kernel,
        grid=(slots // rows,),
        in_specs=[block, block, IN_VMEM, IN_VMEM],
        out_specs=[block, block, pl.BlockSpec((width, rows), lambda g: (0, g))],
        out_shape=[
            jax.ShapeDtypeStruct((slots, width), F32),
            jax.ShapeDtypeStruct((slots, width), BF),
            jax.ShapeDtypeStruct((width, slots), BF),
        ],
        compiler_params=pltpu.CompilerParams(vmem_limit_bytes=12 * 2**20),
        cost_estimate=SMALL,
        name="middle",
    )(x, attended, w_out, gain)


def turn_kernel(in_ref, out_ref):
    out_ref[...] = jnp.transpose(in_ref[...].astype(F32)).astype(BF)


def turn(matrix):
    rows, columns = matrix.shape
    wide = 256
    return pl.pallas_call(
        turn_kernel,
        grid=(columns // wide,),
        in_specs=[pl.BlockSpec((rows, wide), lambda g: (0, g))],
        out_specs=pl.BlockSpec((wide, rows), lambda g: (g, 0)),
        out_shape=jax.ShapeDtypeStruct((columns, rows), BF),
        compiler_params=pltpu.CompilerParams(vmem_limit_bytes=8 * 2**20),
        cost_estimate=SMALL,
        name="turn",
    )(matrix)


def weight_grad_kernel(groups, swapped, norms, place_ref, *refs):
    refs, out_ref = list(refs[:-1]), refs[-1]
    rows = out_ref.shape[1]
    half = 4 * rows
    start = pl.multiple_of(place_ref[0] * half, half)

    def store(sums, at):
        for block in range(4):
            spot = (block >> 1) | ((block & 1) << 1) if swapped else block
            part = sums[block * rows : (block + 1) * rows]
            out_ref[spot ^ place_ref[1], :, at : at + sums.shape[1]] = part

    at = 0
    for spans in groups:
        mine = refs.pop(0)[pl.ds(start, half), :]
        for span in spans:
            right = refs.pop(0)
            for number, first, count in span:
                for step in range(0, count, 512):
                    wide = min(512, count - step)
                    columns = right[number, :, first + step : first + step + wide]
                    store(dot_nn(mine, columns).astype(BF), at)
                    at += wide
    if norms:
        top = lax.broadcasted_iota(jnp.int32, (8, 128), 0) == 0
        lane = lax.broadcasted_iota(jnp.int32, (8, 128), 1)
        columns = pl.ds(pl.multiple_of(start, 128), half)
        sums = jnp.zeros((half, 128), F32)
        for number, norm in enumerate(refs):
            picks = jnp.where(top & (lane == number), 1.0, 0.0)
            sums = sums + dot_tn(norm[:, columns], picks)
        store(sums.astype(BF), at)


def weight_grad(place, groups, norms=(), *, spans, swapped=False):
    half = groups[0][0].shape[0] // 2
    inputs = [array for left, rights in groups for array in (left, *rights)]
    total = sum(count for group in spans for span in group for _, _, count in span)
    total += 128 if norms else 0
    inputs += list(norms)
    return pl.pallas_call(
        functools.partial(weight_grad_kernel, spans, swapped, bool(norms)),
        in_specs=[IN_SMEM] + [IN_VMEM] * len(inputs),
        out_specs=IN_VMEM,
        out_shape=jax.ShapeDtypeStruct((4, half // 4, total), BF),
        compiler_params=pltpu.CompilerParams(vmem_limit_bytes=8 * 2**20),
        cost_estimate=SMALL,
        name="weight_grad",
    )(place, *inputs)


def ffn_kernel(
    place_ref,
    hidden_ref,
    hidden_t,
    dy_ref,
    dy_t,
    gate_w,
    up_w,
    down_w,
    inner_ref,
    gate_ref,
    up_ref,
    near_ref,
    far_ref,
):
    rows = 256
    slope = (2.0 / 3.141592653589793) ** 0.5
    for start in range(0, hidden_ref.shape[0], rows):
        here = slice(start, start + rows)
        gate = dot_nn(hidden_ref[here, :], gate_w[...])
        up = dot_nn(hidden_ref[here, :], up_w[...])
        back = dot_nn(dy_ref[here, :], down_w[...])
        square = gate * gate
        share = 0.5 + 0.5 * jnp.tanh(gate * (slope + (0.044715 * slope) * square))
        active = gate * share
        inner_ref[here, :] = (active * up).astype(BF)
        up_ref[here, :] = (back * active).astype(BF)
        steep = share + (active - active * share) * (
            2.0 * slope + (6.0 * 0.044715 * slope) * square
        )
        gate_ref[here, :] = (back * up * steep).astype(BF)
    height = near_ref.shape[2]
    late = pl.program_id(0) >= pl.num_programs(0) // 2
    turned = (False, True, late)
    lefts, rights = (hidden_t, hidden_t, dy_t), (gate_ref, up_ref, inner_ref)
    for number, (left, right, swapped) in enumerate(zip(lefts, rights, turned)):
        sums = dot_nn(left[...], right[...]).astype(BF)
        for half in range(2):

            def put(target, half=half, sums=sums, number=number, swapped=swapped):
                for block in range(4):
                    straight = block ^ place_ref[1]
                    crossed = ((block >> 1) | ((block & 1) << 1)) ^ place_ref[2]
                    at = (4 * half + block) * height
                    spot = jnp.where(swapped, crossed, straight)
                    target[number, spot] = sums[at : at + height]

            pl.when(place_ref[0] == half)(functools.partial(put, near_ref))
            pl.when(place_ref[0] != half)(functools.partial(put, far_ref))


def ffn(place, hidden, hidden_t, dy, dy_t, w_gate, w_up, w_down_t):
    tokens, width = hidden.shape
    units = w_gate.shape[1]
    chunk = 512
    weight = pl.BlockSpec((width, chunk), lambda g: (0, g))
    wide = pl.BlockSpec((tokens, chunk), lambda g: (0, g))
    half = pl.BlockSpec((3, 4, width // 8, chunk), lambda g: (0, 0, 0, g))
    return pl.pallas_call(
        ffn_kernel,
        grid=(units // chunk,),
        in_specs=[IN_SMEM] + [IN_VMEM] * 4 + [weight] * 3,
        out_specs=[wide, wide, wide, half, half],
        out_shape=[jax.ShapeDtypeStruct((tokens, units), BF)] * 3
        + [jax.ShapeDtypeStruct((3, 4, width // 8, units), BF)] * 2,
        compiler_params=pltpu.CompilerParams(vmem_limit_bytes=32 * 2**20),
        cost_estimate=SMALL,
        name="ffn",
    )(place, hidden, hidden_t, dy, dy_t, w_gate, w_up, w_down_t)


def norm_back(values, gain, grad):
    inverse = lax.rsqrt(jnp.mean(values * values, axis=-1, keepdims=True) + 1e-06)
    scaled = values * inverse
    pulled = grad * gain
    shared = jnp.mean(scaled * pulled, axis=-1, keepdims=True)
    return inverse * (pulled - scaled * shared), jnp.sum(grad * scaled, axis=0, keepdims=True)


def patch_kernel(splits, *refs):
    parts, refs = refs[:splits], refs[splits:]
    x_ref, grad_ref, gain_ref, *weights, out_ref, norm_ref = refs
    grad = 0.0
    for number, weight in enumerate(weights):
        part = jnp.concatenate([ref[number] for ref in parts], axis=1)
        grad = grad + dot_nn(part, weight[...])
    pulled, gain = norm_back(x_ref[...].astype(F32), gain_ref[...], grad)
    out_ref[...] = (pulled + grad_ref[...]).astype(BF)

    @pl.when(pl.program_id(0) == 0)
    def _():
        norm_ref[...] = jnp.zeros_like(norm_ref)

    norm_ref[0:1, :] += gain


def patch_back(parts, x, grad, gain, w_query, w_key, w_value):
    tokens, width = x.shape
    rows = 512
    slim = pl.BlockSpec((rows, width), lambda g: (g, 0))
    part_specs = [pl.BlockSpec((3, rows, part.shape[2]), lambda g: (0, g, 0)) for part in parts]
    return pl.pallas_call(
        functools.partial(patch_kernel, len(parts)),
        grid=(tokens // rows,),
        in_specs=part_specs + [slim, slim] + [IN_VMEM] * 4,
        out_specs=[slim, pl.BlockSpec((8, width), lambda g: (0, 0))],
        out_shape=[
            jax.ShapeDtypeStruct((tokens, width), BF),
            jax.ShapeDtypeStruct((8, width), F32),
        ],
        compiler_params=pltpu.CompilerParams(vmem_limit_bytes=22 * 2**20),
        cost_estimate=SMALL,
        name="patch_back",
    )(*parts, x, grad, gain, w_query, w_key, w_value)


def assemble_kernel(recipe, place_ref, near_ref, far_ref, *outs):
    step = pl.program_id(0)
    for far, ref in enumerate((near_ref, far_ref)):

        @pl.when((step >= 4) == (far == 1))
        def _(ref=ref):
            for out_ref, pieces in zip(outs, recipe):
                at = 0
                for first, columns in pieces:
                    part = ref[0, :, first : first + columns]
                    out_ref[:, at : at + columns] = part.astype(F32)
                    at += columns


def assemble(place, near, far, recipe):
    rows = near.shape[1]
    block = (1, rows, near.shape[2])
    widths = [sum(columns for _, columns in pieces) for pieces in recipe]
    return pl.pallas_call(
        functools.partial(assemble_kernel, recipe),
        grid_spec=pltpu.PrefetchScalarGridSpec(
            num_scalar_prefetch=1,
            grid=(8,),
            in_specs=[
                pl.BlockSpec(block, lambda g, place: (jnp.minimum(g, 3), 0, 0)),
                pl.BlockSpec(block, lambda g, place: (jnp.maximum(g - 4, 0), 0, 0)),
            ],
            out_specs=[pl.BlockSpec((rows, w), lambda g, place: (g ^ place[2], 0)) for w in widths],
        ),
        out_shape=[jax.ShapeDtypeStruct((8 * rows, w), F32) for w in widths],
        compiler_params=pltpu.CompilerParams(vmem_limit_bytes=16 * 2**20),
        cost_estimate=SMALL,
        name="assemble",
    )(place, near, far)


def assemble_turned_kernel(place_ref, near_ref, far_ref, out_ref, rows_ref):
    height = near_ref.shape[1]
    for far, ref in enumerate((near_ref, far_ref)):
        for at in range(4):
            block = (4 * far + at) ^ place_ref[2]
            start = pl.multiple_of(block * height, height)
            rows_ref[pl.ds(start, height), :] = ref[at].astype(F32)
    out_ref[...] = jnp.transpose(rows_ref[...])


def assemble_turned(place, near, far, firsts, columns):
    rows = near.shape[1]
    chunk = 256
    half = columns // 2 // chunk
    one, two = (first // chunk for first in firsts)

    def where(g, place):
        return (0, 0, jnp.where(g < half, one + g, two + g - half))

    return pl.pallas_call(
        assemble_turned_kernel,
        grid_spec=pltpu.PrefetchScalarGridSpec(
            num_scalar_prefetch=1,
            grid=(2 * half,),
            in_specs=[pl.BlockSpec((4, rows, chunk), where)] * 2,
            out_specs=pl.BlockSpec((chunk, 8 * rows), lambda g, place: (g, 0)),
            scratch_shapes=[pltpu.VMEM((8 * rows, chunk), F32)],
        ),
        out_shape=jax.ShapeDtypeStruct((columns, 8 * rows), F32),
        compiler_params=pltpu.CompilerParams(vmem_limit_bytes=12 * 2**20),
        cost_estimate=SMALL,
        name="assemble_turned",
    )(place, near, far)


def small(name, kernel, shapes, *inputs, scalars=(), cost=TINY):
    many = [jax.ShapeDtypeStruct(shape, BF) for shape in shapes]
    scalars = [jnp.stack(scalars)] if scalars else []
    return pl.pallas_call(
        kernel,
        in_specs=[IN_SMEM] * len(scalars) + [IN_VMEM] * len(inputs),
        out_specs=[IN_VMEM] * len(many),
        out_shape=many,
        compiler_params=pltpu.CompilerParams(vmem_limit_bytes=8 * 2**20),
        cost_estimate=cost,
        name=name,
    )(*scalars, *inputs)


def add_low(left, right):
    return (left.astype(F32) + right.astype(F32)).astype(BF)


def halve(near, arrived):
    half = near.shape[0] // 2
    shape = (half, *near.shape[1:])

    def kernel(near, come, stays, leaves):
        for block in range(half):
            stays[block] = add_low(near[block], come[block])
            leaves[block] = add_low(near[half + block], come[half + block])

    return small("halve", kernel, [shape, shape], near, arrived)


def first_halves_kernel(near, come, one_stays, one_leaves, two_stays, two_leaves):
    step = pl.program_id(0)
    units = near.shape[3]
    half = units // 2
    for number, outs in enumerate(((one_stays, two_stays), (one_leaves, two_leaves))):

        @pl.when((step >= 2) == (number == 1))
        def _(outs=outs):
            last = add_low(near[2, 0], come[2, 0])
            for stream, out in enumerate(outs):
                out[0, :, :units] = add_low(near[stream, 0], come[stream, 0])
                out[0, :, units:] = last[:, stream * half : (stream + 1) * half]


def first_halves(near, come):
    _, blocks, rows, units = near.shape
    wide = units + units // 2
    stays = pl.BlockSpec((1, rows, wide), lambda g: (jnp.minimum(g, 1), 0, 0))
    leaves = pl.BlockSpec((1, rows, wide), lambda g: (jnp.maximum(g - 2, 0), 0, 0))
    block = pl.BlockSpec((3, 1, rows, units), lambda g: (0, g, 0, 0))
    one, one_go, two, two_go = pl.pallas_call(
        first_halves_kernel,
        grid=(blocks,),
        in_specs=[block, block],
        out_specs=[stays, leaves, stays, leaves],
        out_shape=[jax.ShapeDtypeStruct((2, rows, wide), BF)] * 4,
        compiler_params=pltpu.CompilerParams(vmem_limit_bytes=14 * 2**20),
        cost_estimate=SMALL,
        name="first_halves",
    )(near, come)
    return (one, one_go), (two, two_go)


def join(near, arrived):
    half = near.shape[0]

    def kernel(near, come, out):
        for block in range(half):
            out[block] = near[block]
            out[half + block] = come[block]

    return small("join", kernel, [(2 * half, *near.shape[1:])], near, arrived)[0]


def join_both(one, one_come, two, two_come):
    blocks, rows, wide = one.shape
    other = two.shape[2]

    def kernel(one, one_come, two, two_come, out):
        for number, (left, right) in enumerate(((one, two), (one_come, two_come))):
            for block in range(blocks):
                at = blocks * number + block
                out[at, :, :wide] = left[block]
                out[(at >> 1) | ((at & 1) << 1), :, wide:] = right[block]

    shape = (2 * blocks, rows, wide + other)
    return small("join_both", kernel, [shape], one, one_come, two, two_come)[0]


def apart(blocks):
    count = blocks.shape[0]

    def kernel(here, blocks, *outs):
        for bit, out in enumerate(outs):
            out[...] = blocks[here[0] ^ bit]

    return small(
        "apart", kernel, [blocks.shape[1:]] * count, blocks, scalars=[lax.axis_index("band")]
    )


def in_order(*pieces):
    count = len(pieces)

    def kernel(here, *refs):
        for bit in range(count):
            refs[count][here[0] ^ bit] = refs[bit][...]

    shape = (count, *pieces[0].shape)
    return small("in_order", kernel, [shape], *pieces, scalars=[lax.axis_index("band")])[0]


def bit_of(axis, bit):
    return (lax.axis_index(axis) // bit) % 2


def rows_apart(axis, bit):
    def step(*streams):
        height = streams[0].shape[1] // 2
        widths = [stream.shape[2] for stream in streams[::2]]
        shape = (height, sum(widths))

        def kernel(mine, *refs):
            ins, (stays, leaves) = refs[:-2], refs[-2:]
            for out, half in ((stays, mine[0]), (leaves, 1 - mine[0])):
                rows = pl.ds(pl.multiple_of(half * height, height), height)
                at = 0
                for near, come, wide in zip(ins[::2], ins[1::2], widths):
                    out[:, at : at + wide] = add_low(near[0, rows, :], come[0, rows, :])
                    at += wide

        return small(
            "rows_apart", kernel, [shape, shape], *streams, scalars=[bit_of(axis, bit)]
        )

    return step


def add_up(near, come):
    def kernel(near, come, out):
        out[...] = add_low(near[...], come[...])

    return small("add_up", kernel, [near.shape], near, come)[0]


def rows_join(axis, bit, widths):
    def step(near, come):
        height = near.shape[0]

        def kernel(mine, near, come, *outs):
            for piece, half in ((near, mine[0]), (come, 1 - mine[0])):
                rows = pl.ds(pl.multiple_of(half * height, height), height)
                at = 0
                for out, wide in zip(outs, widths):
                    out[0, rows, :] = piece[:, at : at + wide]
                    at += wide

        shapes = [(1, 2 * height, wide) for wide in widths]
        return small("rows_join", kernel, shapes, near, come, scalars=[bit_of(axis, bit)])

    return step


CORE, ACROSS, ALONG = 1, 2, 4


def flip(axis, bit):
    count = lax.axis_size(axis)
    return [(i, i ^ bit) for i in range(count)]


def swap(array, axis, bit):
    return lax.ppermute(array, axis, flip(axis, bit))


def take(array, number, axis=0):
    return lax.dynamic_index_in_dim(array, number, axis, keepdims=False)


def exchange(pieces):
    return pieces[:1] + tuple(swap(piece, "band", bit + 1) for bit, piece in enumerate(pieces[1:]))


def far_bits():
    plots = lax.axis_size("plots")
    band = lax.axis_size("band")
    bits = [("plots", 1 << n) for n in range(3, plots.bit_length() - 1)]
    return bits + [("band", 1 << n) for n in range(band.bit_length() - 1)]


class Line:
    def __init__(self):
        self.last = ()

    def __call__(self, step, *inputs):
        inputs, _ = lax.optimization_barrier((inputs, self.last))
        self.last = step(*inputs)
        return self.last


def side(axis, bit):
    def step(*streams):
        sums = [add_low(near[0], come[0]) for near, come in zip(streams[::2], streams[1::2])]
        return split_far(axis, bit)(jnp.concatenate(sums, 1))

    return step


def split_far(axis, bit):
    def step(matrix):
        halves = matrix.reshape(2, matrix.shape[0] // 2, matrix.shape[1])
        mine = bit_of(axis, bit)
        return take(halves, mine), take(halves, 1 - mine)

    return step


def join_far(axis, bit):
    def step(matrix, other):
        return jnp.where(
            bit_of(axis, bit) == 0,
            jnp.concatenate([matrix, other]),
            jnp.concatenate([other, matrix]),
        )

    return step


def travel(run, widths, *streams):
    far = far_bits()
    if len(far) == 2:
        first, second = far
        near, leaves = run(rows_apart(*first), *streams)
        come = swap(leaves, *first)
        yield
        near = run(add_up, near, come)
        come = swap(near, *second)
        yield
        near = run(add_up, near, come)
        come = swap(near, *first)
        yield
        return run(rows_join(*first, widths), near, come)
    near, leaves = run(side(*far[0]), *streams)
    come = swap(leaves, *far[0])
    yield
    for axis, bit in far[1:]:
        near, leaves = run(
            lambda near, come, far=(axis, bit): split_far(*far)(add_low(near, come)), near, come
        )
        come = swap(leaves, axis, bit)
        yield
    near = run(add_low, near, come)
    for axis, bit in far[::-1]:
        come = swap(near, axis, bit)
        yield
        near = run(join_far(axis, bit), near, come)
    cuts = [sum(widths[: n + 1]) for n in range(len(widths) - 1)]
    return run(lambda a: jnp.split(a[None], cuts, 2), near)


def rest_of(steps):
    while True:
        try:
            next(steps)
        except StopIteration as end:
            return end.value


def rms_norm(values, gain):
    inverse = lax.rsqrt(jnp.mean(values * values, axis=-1, keepdims=True) + 1e-06)
    return values * inverse * gain


def per_device(
    patches,
    norm1_gain,
    w_query,
    w_key,
    w_value,
    w_out,
    norm2_gain,
    w_gate,
    w_up,
    w_down,
    out_grad,
    plot_rows,
    plot_cols,
    global_index,
):
    width = patches.shape[2]
    here = lax.axis_index("band")
    run = Line()
    slots = patches.shape[0] * patches.shape[1]
    count = patches.shape[0]
    pieces = list(run(apart, patches))
    pieces[1:3] = [swap(piece, "band", bit + 1) for bit, piece in enumerate(pieces[1:3])]
    gain = norm1_gain[None]
    weights = w_query, w_key, w_value
    parts = [run(front, pieces[0], gain, *weights)]
    last = run(lambda *a: a, *pieces[3:])
    pieces[3:] = [swap(piece, "band", bit + 3) for bit, piece in enumerate(last)]
    limits = jnp.stack([take(plot_rows, here), take(plot_cols, here)])
    chosen = take(global_index, here)
    index = jnp.broadcast_to(chosen[:, None], (chosen.shape[0], 128))
    index_t = jnp.broadcast_to(chosen[None, :], (8, chosen.shape[0]))
    bias, pick, pick_t = run(functools.partial(masks, slots=slots), limits, index, index_t)
    w_down_t = run(turn, w_down)
    parts.append(run(front, pieces[1], gain, *weights))
    w_query_t, w_key_t, w_value_t = (run(turn, w) for w in weights)
    for piece in pieces[2:-1]:
        parts.append(run(front, piece, gain, *weights))
    dy_pieces = run(apart, out_grad)
    pieces = run(lambda *a: a, *pieces)
    dy_pieces = exchange(run(lambda *a: a, *dy_pieces))
    x_low, hidden, query, keys, values = run(front_last, pieces, parts, gain, *weights)

    me = lax.axis_index("plots")
    core, across, along = me % 2, (me // ACROSS) % 2, (me // ALONG) % 2
    square, square_t = 2 * across + along, 2 * along + across
    whole = 4 * core + square
    place_near = jnp.stack([core, square, whole])
    place_far = jnp.stack([1 - core, square, whole])
    place_near_t = jnp.stack([core, square_t, whole])
    place_far_t = jnp.stack([1 - core, square_t, whole])
    ff = w_gate.shape[1]

    attended, lse = run(attention, query, keys, values, bias, pick)
    resid, hidden2, hidden2_t = run(middle, x_low, attended, w_out, norm2_gain[None])
    w_gate_t, w_up_t, w_out_t = run(turn, w_gate), run(turn, w_up), run(turn, w_out)
    dy = run(in_order, *dy_pieces).reshape(slots, width)
    dy_t = run(turn, dy)
    place_ffn = jnp.stack([core, square, square_t])
    inner, grad_gate, grad_up, ffn_near, ffn_far = run(
        ffn, place_ffn, hidden2, hidden2_t, dy, dy_t, w_gate, w_up, w_down_t
    )
    core_swap = functools.partial(swap, axis="plots", bit=CORE)
    across_swap = functools.partial(swap, axis="plots", bit=ACROSS)
    along_swap = functools.partial(swap, axis="plots", bit=ALONG)
    far = far_bits()

    ffn_come = core_swap(ffn_far)
    mixed_out = run(
        lambda resid, inner, w: (resid + dot_nn(inner, w)).astype(BF), resid, inner, w_down
    )
    mixed_pieces = run(apart, mixed_out.reshape(patches.shape))
    (gate_near, gate_go), (up_near, up_go) = run(first_halves, ffn_near, ffn_come)
    gate_come, up_come = across_swap(gate_go), along_swap(up_go)
    mixed_pieces = exchange(run(lambda *a: a, *mixed_pieces))
    grad_hidden2 = run(
        lambda a, b, c, d: dot_nn(a, c) + dot_nn(b, d), grad_gate, grad_up, w_gate_t, w_up_t
    )

    def resid_back(resid, dy, gain, grad):
        pulled, norm2 = norm_back(resid, gain, grad)
        pulled = pulled + dy.astype(F32)
        return pulled, pulled.astype(BF), jnp.broadcast_to(norm2, (8, width))

    grad_resid, resid_low, norm2 = run(resid_back, resid, dy, norm2_gain, grad_hidden2)
    grad_attended = run(lambda a, w: dot_nn(a, w).astype(BF), resid_low, w_out_t)
    third = width // PAIR // 3

    def back(first):
        return run(
            functools.partial(attention_back, first=first, count=third),
            query,
            keys,
            values,
            grad_attended,
            lse,
            bias,
            pick,
            pick_t,
        )

    back_0 = back(0)
    gate_near, gate_go = run(halve, gate_near, gate_come)
    gate_come = along_swap(gate_go)
    up_near, up_go = run(halve, up_near, up_come)
    up_come = across_swap(up_go)
    back_1 = back(third)
    mixed_out = run(in_order, *mixed_pieces)
    attended_t = run(turn, attended)
    wide_ffn = ff + ff // 2
    ffn_steps = travel(run, [wide_ffn] * 2, gate_near, gate_come, up_near, up_come)
    next(ffn_steps)
    back_2 = back(2 * third)
    hidden_t = run(turn, hidden)
    next(ffn_steps)

    parts = [back_0, back_1, back_2]
    wide = third * PAIR
    half = wide // 2
    rest = width // 2
    out_right = resid_low[None]
    groups = [(hidden_t, parts), (attended_t, [out_right])]
    q_spans = [[[(0, 0, wide), (1, 0, half)]] * 3, [[(0, 0, rest)]]]
    v_spans = [[[(1, half, half), (2, 0, wide)]] * 3, [[(0, rest, width - rest)]]]
    q_grad = functools.partial(weight_grad, spans=q_spans)
    patch_grad, norm1 = run(
        patch_back, parts, x_low, grad_resid, norm1_gain[None], w_query_t, w_key_t, w_value_t
    )
    v_grad = functools.partial(weight_grad, spans=v_spans, swapped=True)
    norms = [norm1, norm2]
    pieces = list(run(apart, patch_grad.reshape(patches.shape)))
    q_come = core_swap(run(q_grad, place_far, groups))
    v_come = core_swap(run(v_grad, place_far_t, groups, norms))
    q_near = run(q_grad, place_near, groups)
    q_near, leaves = run(halve, q_near, q_come)
    q_come = across_swap(leaves)
    v_near = run(v_grad, place_near_t, groups, norms)
    v_near, leaves = run(halve, v_near, v_come)
    v_come = along_swap(leaves)
    next(ffn_steps)
    q_near, leaves = run(halve, q_near, q_come)
    q_come = along_swap(leaves)
    v_near, leaves = run(halve, v_near, v_come)
    v_come = across_swap(leaves)
    cut = 3 * (wide + half) + rest
    qkv_steps = travel(
        run, [cut, 3 * (wide + half) + width - rest + 128], q_near, q_come, v_near, v_come
    )
    next(qkv_steps)
    gate_all, up_all = rest_of(ffn_steps)
    gate_come, up_come = along_swap(gate_all), across_swap(up_all)
    next(qkv_steps)
    gate_all = run(join, gate_all, gate_come)
    gate_come = across_swap(gate_all)
    up_all = run(join, up_all, up_come)
    up_come = along_swap(up_all)
    next(qkv_steps)
    q_all, v_all = rest_of(qkv_steps)
    q_come, v_come = along_swap(q_all), across_swap(v_all)
    far_piece = swap(run(lambda a: a, pieces[2]), "band", 2)
    ffn_near = run(join_both, gate_all, gate_come, up_all, up_come)
    ffn_come = core_swap(ffn_near)
    q_all = run(join, q_all, q_come)
    q_come = across_swap(q_all)
    v_all = run(join, v_all, v_come)
    v_come = along_swap(v_all)
    gate, up = run(
        lambda near, far: assemble(place_near, near, far, [[(0, ff)], [(wide_ffn, ff)]]),
        ffn_near,
        ffn_come,
    )
    pieces[2] = run(lambda a: a, far_piece)
    qkv_near = run(join_both, q_all, q_come, v_all, v_come)
    qkv_come = core_swap(qkv_near)
    one, three = run(lambda *a: a, pieces[1], pieces[3])
    pieces[1], pieces[3] = swap(one, "band", 1), swap(three, "band", 3)
    down = run(
        lambda near, far: assemble_turned(place_near, near, far, (ff, wide_ffn + ff), ff),
        ffn_near,
        ffn_come,
    )
    recipe = [[], [], [], [(cut - rest, rest), (cut + 3 * (wide + half), width - rest)]]
    for number in range(3):
        at = number * (wide + half)
        recipe[0].append((at, wide))
        recipe[1] += [(at + wide, half), (cut + at, half)]
        recipe[2].append((cut + at + half, wide))
    recipe.append([(cut + 3 * (wide + half) + width - rest, 128)])
    q_out, k_out, v_out, out, gains = run(
        lambda near, far: assemble(place_near, near, far, recipe), qkv_near, qkv_come
    )
    patch_grad = run(in_order, *pieces)
    return (
        mixed_out,
        patch_grad,
        gains[:, 0],
        q_out,
        k_out,
        v_out,
        out,
        gains[:, 1],
        gate,
        up,
        down,
    )


def solution(mesh):
    rows = P("plots", "band", None)
    in_specs = (rows,) + (P(),) * 9 + (rows, P("plots"), P("plots"), P("plots", None))
    out_specs = (rows, rows) + (P(),) * 9
    return jax.shard_map(
        per_device, mesh=mesh, in_specs=in_specs, out_specs=out_specs, check_vma=False
    )
```

```python
import functools

import jax
import jax.numpy as jnp
from jax import lax
from jax.experimental import pallas as pl
from jax.experimental.pallas import tpu as pltpu
from jax.sharding import PartitionSpec as P

H = 12
HD = 64
COLS = 64
WIN = 2
TILE_ROWS = 2
PAIR = 2 * HD
BF = jnp.bfloat16
F32 = jnp.float32
LOG2E = 1.4426950408889634
SCALE2 = LOG2E * HD ** (-0.5)
SMALL = pl.CostEstimate(flops=10**10, bytes_accessed=1, transcendentals=0)

TINY = pl.CostEstimate(flops=1, bytes_accessed=1, transcendentals=0)
IN_VMEM = pl.BlockSpec(memory_space=pltpu.VMEM)
IN_SMEM = pl.BlockSpec(memory_space=pltpu.SMEM)


def dot_nt(a, b):
    return lax.dot_general(a, b, (((1,), (1,)), ((), ())), preferred_element_type=F32)


def dot_nn(a, b):
    return lax.dot_general(a, b, (((1,), (0,)), ((), ())), preferred_element_type=F32)


def dot_tn(a, b):
    return lax.dot_general(a, b, (((0,), (0,)), ((), ())), preferred_element_type=F32)


def tiles_of(rows):
    out = []
    for first in range(0, rows, TILE_ROWS):
        low = max(first - WIN, 0)
        high = min(first + TILE_ROWS + WIN, rows)
        out.append((first * COLS, low * COLS, high * COLS))
    return out


def fill_bias(bias_ref, limits_ref, tiles):
    rows_here = limits_ref[0]
    cols_here = limits_ref[1]
    span = TILE_ROWS * COLS
    for number, (query_lo, key_lo, key_hi) in enumerate(tiles):
        count = key_hi - key_lo
        shape = (count, 2 * span)
        key = lax.broadcasted_iota(jnp.int32, shape, 0) + key_lo
        query = lax.broadcasted_iota(jnp.int32, shape, 1) % span + query_lo
        key_row = key // COLS
        apart = key_row - query // COLS
        seen = (apart <= WIN) & (apart >= -WIN) & (key_row < rows_here) & (key % COLS < cols_here)
        bias_ref[number, :count, :] = jnp.where(seen, 0.0, -1e30).astype(F32)


def picker_rows(index_ref, slots):
    chosen = index_ref[:, 0:1]
    lanes = lax.broadcasted_iota(jnp.int32, (chosen.shape[0], slots), 1)
    return (lanes == chosen).astype(F32).astype(BF)


def two_heads(block, lane):
    none = jnp.zeros_like(block)
    return jnp.concatenate([jnp.where(lane < HD, block, none), jnp.where(lane < HD, none, block)])


def own_heads(sums, span):
    return jnp.transpose(jnp.concatenate([sums[:HD, :span], sums[HD:, span:]], axis=0))


def masks_kernel(limits_ref, index_ref, index_t_ref, bias_ref, pick_ref, pick_t_ref):
    slots = pick_ref.shape[1]
    fill_bias(bias_ref, limits_ref, tiles_of(slots // COLS))
    pick_ref[...] = picker_rows(index_ref, slots)
    down = lax.broadcasted_iota(jnp.int32, pick_t_ref.shape, 0)
    pick_t_ref[...] = (down == index_t_ref[0:1, :]).astype(F32).astype(BF)


def masks(limits, index, index_t, slots):
    count = index.shape[0]
    tall = (TILE_ROWS + 2 * WIN) * COLS
    tiles = slots // (TILE_ROWS * COLS)
    return pl.pallas_call(
        masks_kernel,
        in_specs=[IN_SMEM, IN_VMEM, IN_VMEM],
        out_specs=[IN_VMEM] * 3,
        out_shape=[
            jax.ShapeDtypeStruct((tiles, tall, 2 * TILE_ROWS * COLS), F32),
            jax.ShapeDtypeStruct((count, slots), BF),
            jax.ShapeDtypeStruct((slots, count), BF),
        ],
        compiler_params=pltpu.CompilerParams(vmem_limit_bytes=8 * 2**20),
        cost_estimate=SMALL,
        name="masks",
    )(limits, index, index_t)


def attend_kernel(bias_ref, pick_ref, q_ref, k_ref, v_ref, out_ref, lse_ref, value_t):
    slots = q_ref.shape[0]
    tiles = tiles_of(slots // COLS)
    span = TILE_ROWS * COLS
    global_keys = dot_nn(pick_ref[...], k_ref[...]).astype(BF)
    global_values_t = jnp.transpose(dot_nn(pick_ref[...], v_ref[...])).astype(BF)
    value_t[...] = jnp.transpose(v_ref[...].astype(F32)).astype(BF)
    lane = lax.broadcasted_iota(jnp.int32, (span, PAIR), 1)
    for number, (query_lo, key_lo, key_hi) in enumerate(tiles):
        count = key_hi - key_lo
        query = two_heads(q_ref[query_lo : query_lo + span, :], lane)
        window = dot_nt(k_ref[key_lo:key_hi, :], query) * SCALE2 + bias_ref[number, :count, :]
        wide = dot_nt(global_keys, query) * SCALE2
        highest = jnp.maximum(
            jnp.max(window, axis=0, keepdims=True), jnp.max(wide, axis=0, keepdims=True)
        )
        window = jnp.exp2(window - highest)
        wide = jnp.exp2(wide - highest)
        total = jnp.sum(window, axis=0, keepdims=True) + jnp.sum(wide, axis=0, keepdims=True)
        inverse = 1.0 / total
        sums = dot_nn(value_t[:, key_lo:key_hi], (window * inverse).astype(BF))
        sums = sums + dot_nn(global_values_t, (wide * inverse).astype(BF))
        lse_ref[0, number : number + 1, :] = highest + jnp.log2(total)
        out_ref[query_lo : query_lo + span, :] = own_heads(sums, span).astype(BF)


def attend_back_kernel(
    bias_ref,
    pick_ref,
    pick_t_ref,
    q_ref,
    k_ref,
    v_ref,
    g_ref,
    lse_ref,
    out_ref,
    key_t,
    dk_acc,
    dv_acc,
):
    slots = q_ref.shape[0]
    tiles = tiles_of(slots // COLS)
    span = TILE_ROWS * COLS
    globals_here = pick_ref.shape[0]
    global_keys_f = dot_nn(pick_ref[...], k_ref[...])
    global_keys = global_keys_f.astype(BF)
    global_keys_t = jnp.transpose(global_keys_f).astype(BF)
    global_values = dot_nn(pick_ref[...], v_ref[...]).astype(BF)
    key_t[...] = jnp.transpose(k_ref[...].astype(F32)).astype(BF)
    dk_acc[...] = jnp.zeros_like(dk_acc)
    dv_acc[...] = jnp.zeros_like(dv_acc)
    dk_global = jnp.zeros((globals_here, PAIR), F32)
    dv_global = jnp.zeros((globals_here, PAIR), F32)
    lane = lax.broadcasted_iota(jnp.int32, (span, PAIR), 1)
    for number, (query_lo, key_lo, key_hi) in enumerate(tiles):
        count = key_hi - key_lo
        query = two_heads(q_ref[query_lo : query_lo + span, :], lane)
        grad = two_heads(g_ref[query_lo : query_lo + span, :], lane)
        keys = k_ref[key_lo:key_hi, :]
        values = v_ref[key_lo:key_hi, :]
        lse = lse_ref[0, number : number + 1, :]
        window = jnp.exp2(dot_nt(keys, query) * SCALE2 + (bias_ref[number, :count, :] - lse))
        wide = jnp.exp2(dot_nt(global_keys, query) * SCALE2 - lse)
        window_g = dot_nt(values, grad)
        wide_g = dot_nt(global_values, grad)
        weighted = jnp.sum(window * window_g, axis=0, keepdims=True) + jnp.sum(
            wide * wide_g, axis=0, keepdims=True
        )
        window_s = (window * (window_g - weighted)).astype(BF)
        wide_s = (wide * (wide_g - weighted)).astype(BF)
        dv_acc[key_lo:key_hi, :] += dot_nn(window.astype(BF), grad)
        dk_acc[key_lo:key_hi, :] += dot_nn(window_s, query)
        dv_global += dot_nn(wide.astype(BF), grad)
        dk_global += dot_nn(wide_s, query)
        sums = dot_nn(key_t[:, key_lo:key_hi], window_s) + dot_nn(global_keys_t, wide_s)
        sums = own_heads(sums, span) * HD ** (-0.5)
        out_ref[0, query_lo : query_lo + span, :] = sums.astype(BF)

    def spread(part):
        high = part.astype(BF)
        rest = part - high.astype(F32)
        middle = rest.astype(BF)
        low = (rest - middle.astype(F32)).astype(BF)
        picks = pick_t_ref[...]
        return dot_nn(picks, high) + dot_nn(picks, middle) + dot_nn(picks, low)

    out_ref[1] = ((dk_acc[...] + spread(dk_global)) * HD ** (-0.5)).astype(BF)
    out_ref[2] = (dv_acc[...] + spread(dv_global)).astype(BF)


def attention(query, keys, values, bias, pick):
    slots, width = query.shape
    pairs = width // PAIR
    block = pl.BlockSpec((slots, PAIR), lambda p: (0, p))
    tiles = slots // (TILE_ROWS * COLS)
    return pl.pallas_call(
        attend_kernel,
        grid=(pairs,),
        in_specs=[IN_VMEM, IN_VMEM, block, block, block],
        out_specs=[block, pl.BlockSpec((1, tiles, 2 * TILE_ROWS * COLS), lambda p: (p, 0, 0))],
        out_shape=[
            jax.ShapeDtypeStruct((slots, width), BF),
            jax.ShapeDtypeStruct((pairs, tiles, 2 * TILE_ROWS * COLS), F32),
        ],
        scratch_shapes=[pltpu.VMEM((PAIR, slots), BF)],
        compiler_params=pltpu.CompilerParams(vmem_limit_bytes=10 * 2**20),
        cost_estimate=SMALL,
        name="attend",
    )(bias, pick, query, keys, values)


def attention_back(query, keys, values, grad, lse, bias, pick, pick_t, first, count):
    slots = query.shape[0]
    block = pl.BlockSpec((slots, PAIR), lambda p: (0, first + p))
    return pl.pallas_call(
        attend_back_kernel,
        grid=(count,),
        in_specs=[IN_VMEM] * 3
        + [block] * 4
        + [pl.BlockSpec((1, *lse.shape[1:]), lambda p: (first + p, 0, 0))],
        out_specs=pl.BlockSpec((3, slots, PAIR), lambda p: (0, 0, p)),
        out_shape=jax.ShapeDtypeStruct((3, slots, count * PAIR), BF),
        scratch_shapes=[
            pltpu.VMEM((PAIR, slots), BF),
            pltpu.VMEM((slots, PAIR), F32),
            pltpu.VMEM((slots, PAIR), F32),
        ],
        compiler_params=pltpu.CompilerParams(vmem_limit_bytes=12 * 2**20),
        cost_estimate=SMALL,
        name="attend_back",
    )(bias, pick, pick_t, query, keys, values, grad, lse)


def project(piece, gain, weights):
    hidden = rms_norm(piece.astype(F32), gain).astype(BF)
    return [hidden] + [dot_nn(hidden, weight[...]).astype(BF) for weight in weights]


def front(piece, gain, *weights):
    def kernel(piece, gain, *refs):
        for out, value in zip(refs[3:], project(piece[...], gain[...], refs[:3])):
            out[...] = value

    return small("front", kernel, [piece.shape] * 4, piece, gain, *weights, cost=SMALL)


def front_last(pieces, parts, gain, *weights):
    count, (rows, width) = len(pieces), pieces[0].shape

    def kernel(here, *refs):
        refs = list(refs)
        pieces = [refs.pop(0) for _ in range(count)]
        parts = [[refs.pop(0) for _ in range(4)] for _ in range(count - 1)]
        gain, weights, outs = refs[0], refs[1:4], refs[4:]
        for bit in range(count):
            place = pl.ds(pl.multiple_of((here[0] ^ bit) * rows, rows), rows)
            outs[0][place, :] = pieces[bit][...]
            if bit < count - 1:
                values = [part[...] for part in parts[bit]]
            else:
                values = project(pieces[bit][...], gain[...], weights)
            for out, value in zip(outs[1:], values):
                out[place, :] = value

    return small(
        "front_last",
        kernel,
        [(count * rows, width)] * 5,
        *pieces,
        *[array for part in parts for array in part],
        gain,
        *weights,
        scalars=[lax.axis_index("band")],
        cost=SMALL,
    )


def middle_kernel(x_ref, attended_ref, w_out, gain_ref, resid_ref, hidden_ref, hidden_t):
    resid = x_ref[...].astype(F32) + dot_nn(attended_ref[...], w_out[...])
    resid_ref[...] = resid
    hidden = rms_norm(resid, gain_ref[...])
    hidden_ref[...] = hidden.astype(BF)
    hidden_t[...] = jnp.transpose(hidden).astype(BF)


def middle(x, attended, w_out, gain):
    slots, width = x.shape
    rows = 256
    block = pl.BlockSpec((rows, width), lambda g: (g, 0))
    return pl.pallas_call(
        middle_kernel,
        grid=(slots // rows,),
        in_specs=[block, block, IN_VMEM, IN_VMEM],
        out_specs=[block, block, pl.BlockSpec((width, rows), lambda g: (0, g))],
        out_shape=[
            jax.ShapeDtypeStruct((slots, width), F32),
            jax.ShapeDtypeStruct((slots, width), BF),
            jax.ShapeDtypeStruct((width, slots), BF),
        ],
        compiler_params=pltpu.CompilerParams(vmem_limit_bytes=12 * 2**20),
        cost_estimate=SMALL,
        name="middle",
    )(x, attended, w_out, gain)


def turn_kernel(in_ref, out_ref):
    out_ref[...] = jnp.transpose(in_ref[...].astype(F32)).astype(BF)


def turn(matrix):
    rows, columns = matrix.shape
    wide = 256
    return pl.pallas_call(
        turn_kernel,
        grid=(columns // wide,),
        in_specs=[pl.BlockSpec((rows, wide), lambda g: (0, g))],
        out_specs=pl.BlockSpec((wide, rows), lambda g: (g, 0)),
        out_shape=jax.ShapeDtypeStruct((columns, rows), BF),
        compiler_params=pltpu.CompilerParams(vmem_limit_bytes=8 * 2**20),
        cost_estimate=SMALL,
        name="turn",
    )(matrix)


def weight_grad_kernel(groups, swapped, place_ref, *refs):
    refs, out_ref = list(refs[:-1]), refs[-1]
    rows = out_ref.shape[1]
    half = 4 * rows
    start = pl.multiple_of(place_ref[0] * half, half)

    def store(sums, at):
        for block in range(4):
            spot = (block >> 1) | ((block & 1) << 1) if swapped else block
            part = sums[block * rows : (block + 1) * rows]
            out_ref[spot ^ place_ref[1], :, at : at + sums.shape[1]] = part

    at = 0
    for spans in groups:
        mine = refs.pop(0)[pl.ds(start, half), :]
        for span in spans:
            right = refs.pop(0)
            for number, first, count in span:
                for step in range(0, count, 512):
                    wide = min(512, count - step)
                    columns = right[number, :, first + step : first + step + wide]
                    store(dot_nn(mine, columns).astype(BF), at)
                    at += wide


def weight_grad(place, groups, *, spans, swapped=False):
    half = groups[0][0].shape[0] // 2
    inputs = [array for left, rights in groups for array in (left, *rights)]
    total = sum(count for group in spans for span in group for _, _, count in span)
    return pl.pallas_call(
        functools.partial(weight_grad_kernel, spans, swapped),
        in_specs=[IN_SMEM] + [IN_VMEM] * len(inputs),
        out_specs=IN_VMEM,
        out_shape=jax.ShapeDtypeStruct((4, half // 4, total), BF),
        compiler_params=pltpu.CompilerParams(vmem_limit_bytes=8 * 2**20),
        cost_estimate=SMALL,
        name="weight_grad",
    )(place, *inputs)


def ffn_kernel(
    place_ref,
    hidden_ref,
    hidden_t,
    dy_ref,
    dy_t,
    gate_w,
    up_w,
    down_w,
    inner_ref,
    gate_ref,
    up_ref,
    near_ref,
    far_ref,
):
    rows = 256
    slope = (2.0 / 3.141592653589793) ** 0.5
    for start in range(0, hidden_ref.shape[0], rows):
        here = slice(start, start + rows)
        gate = dot_nn(hidden_ref[here, :], gate_w[...])
        up = dot_nn(hidden_ref[here, :], up_w[...])
        back = dot_nn(dy_ref[here, :], down_w[...])
        square = gate * gate
        share = 0.5 + 0.5 * jnp.tanh(gate * (slope + (0.044715 * slope) * square))
        active = gate * share
        inner_ref[here, :] = (active * up).astype(BF)
        up_ref[here, :] = (back * active).astype(BF)
        steep = share + (active - active * share) * (
            2.0 * slope + (6.0 * 0.044715 * slope) * square
        )
        gate_ref[here, :] = (back * up * steep).astype(BF)
    height = near_ref.shape[2]
    late = pl.program_id(0) >= pl.num_programs(0) // 2
    turned = (False, True, late)
    lefts, rights = (hidden_t, hidden_t, dy_t), (gate_ref, up_ref, inner_ref)
    for number, (left, right, swapped) in enumerate(zip(lefts, rights, turned)):
        sums = dot_nn(left[...], right[...]).astype(BF)
        for half in range(2):

            def put(target, half=half, sums=sums, number=number, swapped=swapped):
                for block in range(4):
                    straight = block ^ place_ref[1]
                    crossed = ((block >> 1) | ((block & 1) << 1)) ^ place_ref[2]
                    at = (4 * half + block) * height
                    spot = jnp.where(swapped, crossed, straight)
                    target[number, spot] = sums[at : at + height]

            pl.when(place_ref[0] == half)(functools.partial(put, near_ref))
            pl.when(place_ref[0] != half)(functools.partial(put, far_ref))


def ffn(place, hidden, hidden_t, dy, dy_t, w_gate, w_up, w_down_t):
    tokens, width = hidden.shape
    units = w_gate.shape[1]
    chunk = 512
    weight = pl.BlockSpec((width, chunk), lambda g: (0, g))
    wide = pl.BlockSpec((tokens, chunk), lambda g: (0, g))
    half = pl.BlockSpec((3, 4, width // 8, chunk), lambda g: (0, 0, 0, g))
    return pl.pallas_call(
        ffn_kernel,
        grid=(units // chunk,),
        in_specs=[IN_SMEM] + [IN_VMEM] * 4 + [weight] * 3,
        out_specs=[wide, wide, wide, half, half],
        out_shape=[jax.ShapeDtypeStruct((tokens, units), BF)] * 3
        + [jax.ShapeDtypeStruct((3, 4, width // 8, units), BF)] * 2,
        compiler_params=pltpu.CompilerParams(vmem_limit_bytes=42 * 2**20),
        cost_estimate=SMALL,
        name="ffn",
    )(place, hidden, hidden_t, dy, dy_t, w_gate, w_up, w_down_t)


def norm_back(values, gain, grad):
    inverse = lax.rsqrt(jnp.mean(values * values, axis=-1, keepdims=True) + 1e-06)
    scaled = values * inverse
    pulled = grad * gain
    return inverse * (pulled - scaled * jnp.mean(scaled * pulled, axis=-1, keepdims=True))


def patch_kernel(splits, *refs):
    parts, refs = refs[:splits], refs[splits:]
    x_ref, grad_ref, gain_ref, *weights, out_ref = refs
    grad = 0.0
    for number, weight in enumerate(weights):
        part = jnp.concatenate([ref[number] for ref in parts], axis=1)
        grad = grad + dot_nn(part, weight[...])
    pulled = norm_back(x_ref[...].astype(F32), gain_ref[...], grad)
    out_ref[...] = (pulled + grad_ref[...]).astype(BF)


def patch_back(parts, x, grad, gain, w_query, w_key, w_value):
    tokens, width = x.shape
    rows = 512
    slim = pl.BlockSpec((rows, width), lambda g: (g, 0))
    part_specs = [pl.BlockSpec((3, rows, part.shape[2]), lambda g: (0, g, 0)) for part in parts]
    return pl.pallas_call(
        functools.partial(patch_kernel, len(parts)),
        grid=(tokens // rows,),
        in_specs=part_specs + [slim, slim] + [IN_VMEM] * 4,
        out_specs=slim,
        out_shape=jax.ShapeDtypeStruct((tokens, width), BF),
        compiler_params=pltpu.CompilerParams(vmem_limit_bytes=22 * 2**20),
        cost_estimate=SMALL,
        name="patch_back",
    )(*parts, x, grad, gain, w_query, w_key, w_value)


def assemble_kernel(recipe, scored, place_ref, near_ref, far_ref, *refs):
    weights, outs, sums_ref = refs[:scored], refs[scored:-1], refs[-1]
    step = pl.program_id(0)
    for far, ref in enumerate((near_ref, far_ref)):

        @pl.when((step >= 4) == (far == 1))
        def _(ref=ref):
            sums = jnp.zeros((ref.shape[1], 1), F32)
            for number, (out_ref, pieces) in enumerate(zip(outs, recipe)):
                at = 0
                for first, columns in pieces:
                    part = ref[0, :, first : first + columns].astype(F32)
                    out_ref[:, at : at + columns] = part
                    if number < scored:
                        weight = weights[number][:, at : at + columns].astype(F32)
                        sums = sums + jnp.sum(part * weight, axis=1, keepdims=True)
                    at += columns
            sums_ref[...] = jnp.broadcast_to(sums, sums_ref.shape)


def assemble(place, near, far, weights, recipe):
    rows = near.shape[1]
    block = (1, rows, near.shape[2])
    widths = [sum(columns for _, columns in pieces) for pieces in recipe]
    placed = [pl.BlockSpec((rows, w), lambda g, place: (g ^ place[2], 0)) for w in widths]
    return pl.pallas_call(
        functools.partial(assemble_kernel, recipe, len(weights)),
        grid_spec=pltpu.PrefetchScalarGridSpec(
            num_scalar_prefetch=1,
            grid=(8,),
            in_specs=[
                pl.BlockSpec(block, lambda g, place: (jnp.minimum(g, 3), 0, 0)),
                pl.BlockSpec(block, lambda g, place: (jnp.maximum(g - 4, 0), 0, 0)),
            ]
            + placed[: len(weights)],
            out_specs=placed + [pl.BlockSpec((rows, 128), lambda g, place: (g ^ place[2], 0))],
        ),
        out_shape=[jax.ShapeDtypeStruct((8 * rows, w), F32) for w in widths + [128]],
        compiler_params=pltpu.CompilerParams(vmem_limit_bytes=18 * 2**20),
        cost_estimate=SMALL,
        name="assemble",
    )(place, near, far, *weights)


def assemble_turned_kernel(place_ref, near_ref, far_ref, out_ref, rows_ref):
    height = near_ref.shape[1]
    for far, ref in enumerate((near_ref, far_ref)):
        for at in range(4):
            block = (4 * far + at) ^ place_ref[2]
            start = pl.multiple_of(block * height, height)
            rows_ref[pl.ds(start, height), :] = ref[at].astype(F32)
    out_ref[...] = jnp.transpose(rows_ref[...])


def assemble_turned(place, near, far, firsts, columns):
    rows = near.shape[1]
    chunk = 256
    half = columns // 2 // chunk
    one, two = (first // chunk for first in firsts)

    def where(g, place):
        return (0, 0, jnp.where(g < half, one + g, two + g - half))

    return pl.pallas_call(
        assemble_turned_kernel,
        grid_spec=pltpu.PrefetchScalarGridSpec(
            num_scalar_prefetch=1,
            grid=(2 * half,),
            in_specs=[pl.BlockSpec((4, rows, chunk), where)] * 2,
            out_specs=pl.BlockSpec((chunk, 8 * rows), lambda g, place: (g, 0)),
            scratch_shapes=[pltpu.VMEM((8 * rows, chunk), F32)],
        ),
        out_shape=jax.ShapeDtypeStruct((columns, 8 * rows), F32),
        compiler_params=pltpu.CompilerParams(vmem_limit_bytes=12 * 2**20),
        cost_estimate=SMALL,
        name="assemble_turned",
    )(place, near, far)


def small(name, kernel, shapes, *inputs, scalars=(), cost=TINY):
    many = [jax.ShapeDtypeStruct(shape, BF) for shape in shapes]
    scalars = [jnp.stack(scalars)] if scalars else []
    return pl.pallas_call(
        kernel,
        in_specs=[IN_SMEM] * len(scalars) + [IN_VMEM] * len(inputs),
        out_specs=[IN_VMEM] * len(many),
        out_shape=many,
        compiler_params=pltpu.CompilerParams(vmem_limit_bytes=8 * 2**20),
        cost_estimate=cost,
        name=name,
    )(*scalars, *inputs)


def add_low(left, right):
    return (left.astype(F32) + right.astype(F32)).astype(BF)


def halve(near, arrived):
    half = near.shape[0] // 2
    shape = (half, *near.shape[1:])

    def kernel(near, come, stays, leaves):
        for block in range(half):
            stays[block] = add_low(near[block], come[block])
            leaves[block] = add_low(near[half + block], come[half + block])

    return small("halve", kernel, [shape, shape], near, arrived)


def first_halves_kernel(near, come, one_stays, one_leaves, two_stays, two_leaves):
    step = pl.program_id(0)
    units = near.shape[3]
    half = units // 2
    for number, outs in enumerate(((one_stays, two_stays), (one_leaves, two_leaves))):

        @pl.when((step >= 2) == (number == 1))
        def _(outs=outs):
            last = add_low(near[2, 0], come[2, 0])
            for stream, out in enumerate(outs):
                out[0, :, :units] = add_low(near[stream, 0], come[stream, 0])
                out[0, :, units:] = last[:, stream * half : (stream + 1) * half]


def first_halves(near, come):
    _, blocks, rows, units = near.shape
    wide = units + units // 2
    stays = pl.BlockSpec((1, rows, wide), lambda g: (jnp.minimum(g, 1), 0, 0))
    leaves = pl.BlockSpec((1, rows, wide), lambda g: (jnp.maximum(g - 2, 0), 0, 0))
    block = pl.BlockSpec((3, 1, rows, units), lambda g: (0, g, 0, 0))
    one, one_go, two, two_go = pl.pallas_call(
        first_halves_kernel,
        grid=(blocks,),
        in_specs=[block, block],
        out_specs=[stays, leaves, stays, leaves],
        out_shape=[jax.ShapeDtypeStruct((2, rows, wide), BF)] * 4,
        compiler_params=pltpu.CompilerParams(vmem_limit_bytes=14 * 2**20),
        cost_estimate=SMALL,
        name="first_halves",
    )(near, come)
    return (one, one_go), (two, two_go)


def join(near, arrived):
    half = near.shape[0]

    def kernel(near, come, out):
        for block in range(half):
            out[block] = near[block]
            out[half + block] = come[block]

    return small("join", kernel, [(2 * half, *near.shape[1:])], near, arrived)[0]


def join_both(one, one_come, two, two_come):
    blocks, rows, wide = one.shape
    other = two.shape[2]

    def kernel(one, one_come, two, two_come, out):
        for number, (left, right) in enumerate(((one, two), (one_come, two_come))):
            for block in range(blocks):
                at = blocks * number + block
                out[at, :, :wide] = left[block]
                out[(at >> 1) | ((at & 1) << 1), :, wide:] = right[block]

    shape = (2 * blocks, rows, wide + other)
    return small("join_both", kernel, [shape], one, one_come, two, two_come)[0]


def apart(blocks):
    count = blocks.shape[0]

    def kernel(here, blocks, *outs):
        for bit, out in enumerate(outs):
            out[...] = blocks[here[0] ^ bit]

    return small(
        "apart", kernel, [blocks.shape[1:]] * count, blocks, scalars=[lax.axis_index("band")]
    )


def in_order(*pieces):
    count = len(pieces)

    def kernel(here, *refs):
        for bit in range(count):
            refs[count][here[0] ^ bit] = refs[bit][...]

    shape = (count, *pieces[0].shape)
    return small("in_order", kernel, [shape], *pieces, scalars=[lax.axis_index("band")])[0]


def bit_of(axis, bit):
    return (lax.axis_index(axis) // bit) % 2


def rows_apart(axis, bit):
    def step(*streams):
        height = streams[0].shape[1] // 2
        widths = [stream.shape[2] for stream in streams[::2]]
        shape = (height, sum(widths))

        def kernel(mine, *refs):
            ins, (stays, leaves) = refs[:-2], refs[-2:]
            for out, half in ((stays, mine[0]), (leaves, 1 - mine[0])):
                rows = pl.ds(pl.multiple_of(half * height, height), height)
                at = 0
                for near, come, wide in zip(ins[::2], ins[1::2], widths):
                    out[:, at : at + wide] = add_low(near[0, rows, :], come[0, rows, :])
                    at += wide

        return small(
            "rows_apart", kernel, [shape, shape], *streams, scalars=[bit_of(axis, bit)]
        )

    return step


def add_up(near, come):
    def kernel(near, come, out):
        out[...] = add_low(near[...], come[...])

    return small("add_up", kernel, [near.shape], near, come)[0]


def rows_join(axis, bit, widths):
    def step(near, come):
        height = near.shape[0]

        def kernel(mine, near, come, *outs):
            for piece, half in ((near, mine[0]), (come, 1 - mine[0])):
                rows = pl.ds(pl.multiple_of(half * height, height), height)
                at = 0
                for out, wide in zip(outs, widths):
                    out[0, rows, :] = piece[:, at : at + wide]
                    at += wide

        shapes = [(1, 2 * height, wide) for wide in widths]
        return small("rows_join", kernel, shapes, near, come, scalars=[bit_of(axis, bit)])

    return step


CORE, ACROSS, ALONG = 1, 2, 4


def flip(axis, bit):
    count = lax.axis_size(axis)
    return [(i, i ^ bit) for i in range(count)]


def swap(array, axis, bit):
    return lax.ppermute(array, axis, flip(axis, bit))


def take(array, number, axis=0):
    return lax.dynamic_index_in_dim(array, number, axis, keepdims=False)


def exchange(pieces):
    return pieces[:1] + tuple(swap(piece, "band", bit + 1) for bit, piece in enumerate(pieces[1:]))


def far_bits():
    plots = lax.axis_size("plots")
    band = lax.axis_size("band")
    bits = [("plots", 1 << n) for n in range(3, plots.bit_length() - 1)]
    return bits + [("band", 1 << n) for n in range(band.bit_length() - 1)]


class Line:
    def __init__(self):
        self.last = ()

    def __call__(self, step, *inputs):
        inputs, _ = lax.optimization_barrier((inputs, self.last))
        self.last = step(*inputs)
        return self.last


def side(axis, bit):
    def step(*streams):
        sums = [add_low(near[0], come[0]) for near, come in zip(streams[::2], streams[1::2])]
        return split_far(axis, bit)(jnp.concatenate(sums, 1))

    return step


def split_far(axis, bit):
    def step(matrix):
        halves = matrix.reshape(2, matrix.shape[0] // 2, matrix.shape[1])
        mine = bit_of(axis, bit)
        return take(halves, mine), take(halves, 1 - mine)

    return step


def join_far(axis, bit):
    def step(matrix, other):
        return jnp.where(
            bit_of(axis, bit) == 0,
            jnp.concatenate([matrix, other]),
            jnp.concatenate([other, matrix]),
        )

    return step


def travel(run, widths, *streams):
    far = far_bits()
    if len(far) == 2:
        first, second = far
        near, leaves = run(rows_apart(*first), *streams)
        come = swap(leaves, *first)
        yield
        near = run(add_up, near, come)
        come = swap(near, *second)
        yield
        near = run(add_up, near, come)
        come = swap(near, *first)
        yield
        return run(rows_join(*first, widths), near, come)
    near, leaves = run(side(*far[0]), *streams)
    come = swap(leaves, *far[0])
    yield
    for axis, bit in far[1:]:
        near, leaves = run(
            lambda near, come, far=(axis, bit): split_far(*far)(add_low(near, come)), near, come
        )
        come = swap(leaves, axis, bit)
        yield
    near = run(add_low, near, come)
    for axis, bit in far[::-1]:
        come = swap(near, axis, bit)
        yield
        near = run(join_far(axis, bit), near, come)
    cuts = [sum(widths[: n + 1]) for n in range(len(widths) - 1)]
    return run(lambda a: jnp.split(a[None], cuts, 2), near)


def rest_of(steps):
    while True:
        try:
            next(steps)
        except StopIteration as end:
            return end.value


def rms_norm(values, gain):
    inverse = lax.rsqrt(jnp.mean(values * values, axis=-1, keepdims=True) + 1e-06)
    return values * inverse * gain


def per_device(
    patches,
    norm1_gain,
    w_query,
    w_key,
    w_value,
    w_out,
    norm2_gain,
    w_gate,
    w_up,
    w_down,
    out_grad,
    plot_rows,
    plot_cols,
    global_index,
):
    width = patches.shape[2]
    here = lax.axis_index("band")
    run = Line()
    slots = patches.shape[0] * patches.shape[1]
    count = patches.shape[0]
    pieces = list(run(apart, patches))
    pieces[1:3] = [swap(piece, "band", bit + 1) for bit, piece in enumerate(pieces[1:3])]
    gain = norm1_gain[None]
    weights = w_query, w_key, w_value
    parts = [run(front, pieces[0], gain, *weights)]
    last = run(lambda *a: a, *pieces[3:])
    pieces[3:] = [swap(piece, "band", bit + 3) for bit, piece in enumerate(last)]
    limits = jnp.stack([take(plot_rows, here), take(plot_cols, here)])
    chosen = take(global_index, here)
    index = jnp.broadcast_to(chosen[:, None], (chosen.shape[0], 128))
    index_t = jnp.broadcast_to(chosen[None, :], (8, chosen.shape[0]))
    bias, pick, pick_t = run(functools.partial(masks, slots=slots), limits, index, index_t)
    w_down_t = run(turn, w_down)
    parts.append(run(front, pieces[1], gain, *weights))
    w_query_t, w_key_t, w_value_t = (run(turn, w) for w in weights)
    for piece in pieces[2:-1]:
        parts.append(run(front, piece, gain, *weights))
    dy_pieces = run(apart, out_grad)
    pieces = run(lambda *a: a, *pieces)
    dy_pieces = exchange(run(lambda *a: a, *dy_pieces))
    x_low, hidden, query, keys, values = run(front_last, pieces, parts, gain, *weights)

    me = lax.axis_index("plots")
    core, across, along = me % 2, (me // ACROSS) % 2, (me // ALONG) % 2
    square, square_t = 2 * across + along, 2 * along + across
    whole = 4 * core + square
    place_near = jnp.stack([core, square, whole])
    place_far = jnp.stack([1 - core, square, whole])
    place_near_t = jnp.stack([core, square_t, whole])
    place_far_t = jnp.stack([1 - core, square_t, whole])
    ff = w_gate.shape[1]

    attended, lse = run(attention, query, keys, values, bias, pick)
    resid, hidden2, hidden2_t = run(middle, x_low, attended, w_out, norm2_gain[None])
    w_gate_t, w_up_t, w_out_t = run(turn, w_gate), run(turn, w_up), run(turn, w_out)
    dy = run(in_order, *dy_pieces).reshape(slots, width)
    dy_t = run(turn, dy)
    place_ffn = jnp.stack([core, square, square_t])
    inner, grad_gate, grad_up, ffn_near, ffn_far = run(
        ffn, place_ffn, hidden2, hidden2_t, dy, dy_t, w_gate, w_up, w_down_t
    )
    core_swap = functools.partial(swap, axis="plots", bit=CORE)
    across_swap = functools.partial(swap, axis="plots", bit=ACROSS)
    along_swap = functools.partial(swap, axis="plots", bit=ALONG)
    far = far_bits()

    ffn_come = core_swap(ffn_far)
    mixed_out = run(
        lambda resid, inner, w: (resid + dot_nn(inner, w)).astype(BF), resid, inner, w_down
    )
    mixed_pieces = run(apart, mixed_out.reshape(patches.shape))
    (gate_near, gate_go), (up_near, up_go) = run(first_halves, ffn_near, ffn_come)
    gate_come, up_come = across_swap(gate_go), along_swap(up_go)
    mixed_pieces = exchange(run(lambda *a: a, *mixed_pieces))
    grad_hidden2 = run(
        lambda a, b, c, d: dot_nn(a, c) + dot_nn(b, d), grad_gate, grad_up, w_gate_t, w_up_t
    )

    def resid_back(resid, dy, gain, grad):
        pulled = norm_back(resid, gain, grad) + dy.astype(F32)
        return pulled, pulled.astype(BF)

    grad_resid, resid_low = run(resid_back, resid, dy, norm2_gain, grad_hidden2)
    grad_attended = run(lambda a, w: dot_nn(a, w).astype(BF), resid_low, w_out_t)
    third = width // PAIR // 3

    def back(first):
        return run(
            functools.partial(attention_back, first=first, count=third),
            query,
            keys,
            values,
            grad_attended,
            lse,
            bias,
            pick,
            pick_t,
        )

    back_0 = back(0)
    gate_near, gate_go = run(halve, gate_near, gate_come)
    gate_come = along_swap(gate_go)
    up_near, up_go = run(halve, up_near, up_come)
    up_come = across_swap(up_go)
    back_1 = back(third)
    mixed_out = run(in_order, *mixed_pieces)
    attended_t = run(turn, attended)
    wide_ffn = ff + ff // 2
    ffn_steps = travel(run, [wide_ffn] * 2, gate_near, gate_come, up_near, up_come)
    next(ffn_steps)
    back_2 = back(2 * third)
    hidden_t = run(turn, hidden)
    next(ffn_steps)

    parts = [back_0, back_1, back_2]
    wide = third * PAIR
    half = wide // 2
    rest = width // 2
    out_right = resid_low[None]
    groups = [(hidden_t, parts), (attended_t, [out_right])]
    q_spans = [[[(0, 0, wide), (1, 0, half)]] * 3, [[(0, 0, rest)]]]
    v_spans = [[[(1, half, half), (2, 0, wide)]] * 3, [[(0, rest, width - rest)]]]
    q_grad = functools.partial(weight_grad, spans=q_spans)
    v_grad = functools.partial(weight_grad, spans=v_spans, swapped=True)
    patch_grad = run(
        patch_back, parts, x_low, grad_resid, norm1_gain[None], w_query_t, w_key_t, w_value_t
    )
    pieces = list(run(apart, patch_grad.reshape(patches.shape)))
    q_come = core_swap(run(q_grad, place_far, groups))
    v_come = core_swap(run(v_grad, place_far_t, groups))
    q_near = run(q_grad, place_near, groups)
    q_near, leaves = run(halve, q_near, q_come)
    q_come = across_swap(leaves)
    v_near = run(v_grad, place_near_t, groups)
    v_near, leaves = run(halve, v_near, v_come)
    v_come = along_swap(leaves)
    next(ffn_steps)
    q_near, leaves = run(halve, q_near, q_come)
    q_come = along_swap(leaves)
    v_near, leaves = run(halve, v_near, v_come)
    v_come = across_swap(leaves)
    cut = 3 * (wide + half) + rest
    qkv_steps = travel(
        run, [cut, 3 * (wide + half) + width - rest], q_near, q_come, v_near, v_come
    )
    next(qkv_steps)
    gate_all, up_all = rest_of(ffn_steps)
    gate_come, up_come = along_swap(gate_all), across_swap(up_all)
    next(qkv_steps)
    gate_all = run(join, gate_all, gate_come)
    gate_come = across_swap(gate_all)
    up_all = run(join, up_all, up_come)
    up_come = along_swap(up_all)
    next(qkv_steps)
    q_all, v_all = rest_of(qkv_steps)
    q_come, v_come = along_swap(q_all), across_swap(v_all)
    early = run(lambda *a: a, pieces[1], pieces[2])
    early = [swap(piece, "band", bit + 1) for bit, piece in enumerate(early)]
    ffn_near = run(join_both, gate_all, gate_come, up_all, up_come)
    ffn_come = core_swap(ffn_near)
    q_all = run(join, q_all, q_come)
    q_come = across_swap(q_all)
    v_all = run(join, v_all, v_come)
    v_come = along_swap(v_all)
    recipe_ffn = [[(0, ff)], [(wide_ffn, ff)]]
    gate, up, sums2 = run(
        lambda *arrays: assemble(place_near, *arrays, recipe_ffn),
        ffn_near,
        ffn_come,
        [w_gate, w_up],
    )
    pieces[1:3] = run(lambda *a: a, *early)
    qkv_near = run(join_both, q_all, q_come, v_all, v_come)
    qkv_come = core_swap(qkv_near)
    pieces[3] = swap(run(lambda a: a, pieces[3]), "band", 3)
    down = run(
        lambda near, far: assemble_turned(place_near, near, far, (ff, wide_ffn + ff), ff),
        ffn_near,
        ffn_come,
    )
    recipe = [[], [], [], [(cut - rest, rest), (cut + 3 * (wide + half), width - rest)]]
    for number in range(3):
        at = number * (wide + half)
        recipe[0].append((at, wide))
        recipe[1] += [(at + wide, half), (cut + at, half)]
        recipe[2].append((cut + at + half, wide))
    q_out, k_out, v_out, out, sums1 = run(
        lambda *arrays: assemble(place_near, *arrays, recipe), qkv_near, qkv_come, list(weights)
    )
    patch_grad = run(in_order, *pieces)
    return (
        mixed_out,
        patch_grad,
        sums1[:, 0] / norm1_gain,
        q_out,
        k_out,
        v_out,
        out,
        sums2[:, 0] / norm2_gain,
        gate,
        up,
        down,
    )


def solution(mesh):
    rows = P("plots", "band", None)
    in_specs = (rows,) + (P(),) * 9 + (rows, P("plots"), P("plots"), P("plots", None))
    out_specs = (rows, rows) + (P(),) * 9
    return jax.shard_map(
        per_device, mesh=mesh, in_specs=in_specs, out_specs=out_specs, check_vma=False
    )
```

```python
import functools

import jax
import jax.numpy as jnp
from jax import lax
from jax.experimental import pallas as pl
from jax.experimental.pallas import tpu as pltpu
from jax.sharding import PartitionSpec as P

H = 12
HD = 64
COLS = 64
WIN = 2
TILE_ROWS = 2
PAIR = 2 * HD
BF = jnp.bfloat16
F32 = jnp.float32
LOG2E = 1.4426950408889634
SCALE2 = LOG2E * HD ** (-0.5)
SMALL = pl.CostEstimate(flops=10**10, bytes_accessed=1, transcendentals=0)

TINY = pl.CostEstimate(flops=1, bytes_accessed=1, transcendentals=0)
IN_VMEM = pl.BlockSpec(memory_space=pltpu.VMEM)
IN_SMEM = pl.BlockSpec(memory_space=pltpu.SMEM)


def dot_nt(a, b):
    return lax.dot_general(a, b, (((1,), (1,)), ((), ())), preferred_element_type=F32)


def dot_nn(a, b):
    return lax.dot_general(a, b, (((1,), (0,)), ((), ())), preferred_element_type=F32)


def dot_tn(a, b):
    return lax.dot_general(a, b, (((0,), (0,)), ((), ())), preferred_element_type=F32)


def tiles_of(rows):
    out = []
    for first in range(0, rows, TILE_ROWS):
        low = max(first - WIN, 0)
        high = min(first + TILE_ROWS + WIN, rows)
        out.append((first * COLS, low * COLS, high * COLS))
    return out


def fill_bias(bias_ref, limits_ref, tiles):
    rows_here = limits_ref[0]
    cols_here = limits_ref[1]
    span = TILE_ROWS * COLS
    for number, (query_lo, key_lo, key_hi) in enumerate(tiles):
        count = key_hi - key_lo
        shape = (count, 2 * span)
        key = lax.broadcasted_iota(jnp.int32, shape, 0) + key_lo
        query = lax.broadcasted_iota(jnp.int32, shape, 1) % span + query_lo
        key_row = key // COLS
        apart = key_row - query // COLS
        seen = (apart <= WIN) & (apart >= -WIN) & (key_row < rows_here) & (key % COLS < cols_here)
        bias_ref[number, :count, :] = jnp.where(seen, 0.0, -1e30).astype(F32)


def picker_rows(index_ref, slots):
    chosen = index_ref[:, 0:1]
    lanes = lax.broadcasted_iota(jnp.int32, (chosen.shape[0], slots), 1)
    return (lanes == chosen).astype(F32).astype(BF)


def two_heads(block, lane):
    none = jnp.zeros_like(block)
    return jnp.concatenate([jnp.where(lane < HD, block, none), jnp.where(lane < HD, none, block)])


def own_heads(sums, span):
    return jnp.transpose(jnp.concatenate([sums[:HD, :span], sums[HD:, span:]], axis=0))


def masks_kernel(limits_ref, index_ref, index_t_ref, bias_ref, pick_ref, pick_t_ref):
    slots = pick_ref.shape[1]
    fill_bias(bias_ref, limits_ref, tiles_of(slots // COLS))
    pick_ref[...] = picker_rows(index_ref, slots)
    down = lax.broadcasted_iota(jnp.int32, pick_t_ref.shape, 0)
    pick_t_ref[...] = (down == index_t_ref[0:1, :]).astype(F32).astype(BF)


def masks(limits, index, index_t, slots):
    count = index.shape[0]
    tall = (TILE_ROWS + 2 * WIN) * COLS
    tiles = slots // (TILE_ROWS * COLS)
    return pl.pallas_call(
        masks_kernel,
        in_specs=[IN_SMEM, IN_VMEM, IN_VMEM],
        out_specs=[IN_VMEM] * 3,
        out_shape=[
            jax.ShapeDtypeStruct((tiles, tall, 2 * TILE_ROWS * COLS), F32),
            jax.ShapeDtypeStruct((count, slots), BF),
            jax.ShapeDtypeStruct((slots, count), BF),
        ],
        compiler_params=pltpu.CompilerParams(vmem_limit_bytes=8 * 2**20),
        cost_estimate=SMALL,
        name="masks",
    )(limits, index, index_t)


def attend_kernel(bias_ref, pick_ref, q_ref, k_ref, v_ref, out_ref, lse_ref, value_t):
    slots = q_ref.shape[0]
    tiles = tiles_of(slots // COLS)
    span = TILE_ROWS * COLS
    global_keys = dot_nn(pick_ref[...], k_ref[...]).astype(BF)
    global_values_t = jnp.transpose(dot_nn(pick_ref[...], v_ref[...])).astype(BF)
    value_t[...] = jnp.transpose(v_ref[...].astype(F32)).astype(BF)
    lane = lax.broadcasted_iota(jnp.int32, (span, PAIR), 1)
    for number, (query_lo, key_lo, key_hi) in enumerate(tiles):
        count = key_hi - key_lo
        query = two_heads(q_ref[query_lo : query_lo + span, :], lane)
        window = dot_nt(k_ref[key_lo:key_hi, :], query) * SCALE2 + bias_ref[number, :count, :]
        wide = dot_nt(global_keys, query) * SCALE2
        highest = jnp.maximum(
            jnp.max(window, axis=0, keepdims=True), jnp.max(wide, axis=0, keepdims=True)
        )
        window = jnp.exp2(window - highest)
        wide = jnp.exp2(wide - highest)
        total = jnp.sum(window, axis=0, keepdims=True) + jnp.sum(wide, axis=0, keepdims=True)
        inverse = 1.0 / total
        sums = dot_nn(value_t[:, key_lo:key_hi], (window * inverse).astype(BF))
        sums = sums + dot_nn(global_values_t, (wide * inverse).astype(BF))
        lse_ref[0, number : number + 1, :] = highest + jnp.log2(total)
        out_ref[query_lo : query_lo + span, :] = own_heads(sums, span).astype(BF)


def attend_back_kernel(
    bias_ref,
    pick_ref,
    pick_t_ref,
    q_ref,
    k_ref,
    v_ref,
    g_ref,
    lse_ref,
    out_ref,
    key_t,
    dk_acc,
    dv_acc,
):
    slots = q_ref.shape[0]
    tiles = tiles_of(slots // COLS)
    span = TILE_ROWS * COLS
    globals_here = pick_ref.shape[0]
    global_keys_f = dot_nn(pick_ref[...], k_ref[...])
    global_keys = global_keys_f.astype(BF)
    global_keys_t = jnp.transpose(global_keys_f).astype(BF)
    global_values = dot_nn(pick_ref[...], v_ref[...]).astype(BF)
    key_t[...] = jnp.transpose(k_ref[...].astype(F32)).astype(BF)
    dk_acc[...] = jnp.zeros_like(dk_acc)
    dv_acc[...] = jnp.zeros_like(dv_acc)
    dk_global = jnp.zeros((globals_here, PAIR), F32)
    dv_global = jnp.zeros((globals_here, PAIR), F32)
    lane = lax.broadcasted_iota(jnp.int32, (span, PAIR), 1)
    for number, (query_lo, key_lo, key_hi) in enumerate(tiles):
        count = key_hi - key_lo
        query = two_heads(q_ref[query_lo : query_lo + span, :], lane)
        grad = two_heads(g_ref[query_lo : query_lo + span, :], lane)
        keys = jnp.concatenate([k_ref[key_lo:key_hi, :], global_keys])
        values = jnp.concatenate([v_ref[key_lo:key_hi, :], global_values])
        lse = lse_ref[0, number : number + 1, :]
        scores = dot_nt(keys, query) * SCALE2 - lse
        probs = jnp.exp2(
            jnp.concatenate([scores[:count] + bias_ref[number, :count, :], scores[count:]])
        )
        grad_probs = dot_nt(values, grad)
        weighted = jnp.sum(probs * grad_probs, axis=0, keepdims=True)
        grad_scores = (probs * (grad_probs - weighted)).astype(BF)
        dv = dot_nn(probs.astype(BF), grad)
        dk = dot_nn(grad_scores, query)
        dv_acc[key_lo:key_hi, :] += dv[:count]
        dk_acc[key_lo:key_hi, :] += dk[:count]
        dv_global += dv[count:]
        dk_global += dk[count:]
        seen_t = jnp.concatenate([key_t[:, key_lo:key_hi], global_keys_t], axis=1)
        sums = dot_nn(seen_t, grad_scores)
        sums = own_heads(sums, span) * HD ** (-0.5)
        out_ref[0, query_lo : query_lo + span, :] = sums.astype(BF)

    def spread(part):
        high = part.astype(BF)
        rest = part - high.astype(F32)
        middle = rest.astype(BF)
        low = (rest - middle.astype(F32)).astype(BF)
        picks = pick_t_ref[...]
        return dot_nn(picks, high) + dot_nn(picks, middle) + dot_nn(picks, low)

    out_ref[1] = ((dk_acc[...] + spread(dk_global)) * HD ** (-0.5)).astype(BF)
    out_ref[2] = (dv_acc[...] + spread(dv_global)).astype(BF)


def attention(query, keys, values, bias, pick):
    slots, width = query.shape
    pairs = width // PAIR
    block = pl.BlockSpec((slots, PAIR), lambda p: (0, p))
    tiles = slots // (TILE_ROWS * COLS)
    return pl.pallas_call(
        attend_kernel,
        grid=(pairs,),
        in_specs=[IN_VMEM, IN_VMEM, block, block, block],
        out_specs=[block, pl.BlockSpec((1, tiles, 2 * TILE_ROWS * COLS), lambda p: (p, 0, 0))],
        out_shape=[
            jax.ShapeDtypeStruct((slots, width), BF),
            jax.ShapeDtypeStruct((pairs, tiles, 2 * TILE_ROWS * COLS), F32),
        ],
        scratch_shapes=[pltpu.VMEM((PAIR, slots), BF)],
        compiler_params=pltpu.CompilerParams(vmem_limit_bytes=10 * 2**20),
        cost_estimate=SMALL,
        name="attend",
    )(bias, pick, query, keys, values)


def attention_back(query, keys, values, grad, lse, bias, pick, pick_t, first, count):
    slots = query.shape[0]
    block = pl.BlockSpec((slots, PAIR), lambda p: (0, first + p))
    return pl.pallas_call(
        attend_back_kernel,
        grid=(count,),
        in_specs=[IN_VMEM] * 3
        + [block] * 4
        + [pl.BlockSpec((1, *lse.shape[1:]), lambda p: (first + p, 0, 0))],
        out_specs=pl.BlockSpec((3, slots, PAIR), lambda p: (0, 0, p)),
        out_shape=jax.ShapeDtypeStruct((3, slots, count * PAIR), BF),
        scratch_shapes=[
            pltpu.VMEM((PAIR, slots), BF),
            pltpu.VMEM((slots, PAIR), F32),
            pltpu.VMEM((slots, PAIR), F32),
        ],
        compiler_params=pltpu.CompilerParams(vmem_limit_bytes=12 * 2**20),
        cost_estimate=SMALL,
        name="attend_back",
    )(bias, pick, pick_t, query, keys, values, grad, lse)


def project(piece, gain, weights):
    hidden = rms_norm(piece.astype(F32), gain).astype(BF)
    return [hidden] + [dot_nn(hidden, weight[...]).astype(BF) for weight in weights]


def front(piece, gain, *weights):
    def kernel(piece, gain, *refs):
        for out, value in zip(refs[3:], project(piece[...], gain[...], refs[:3])):
            out[...] = value

    return small("front", kernel, [piece.shape] * 4, piece, gain, *weights, cost=SMALL)


def front_last(pieces, parts, gain, *weights):
    count, (rows, width) = len(pieces), pieces[0].shape

    def kernel(here, *refs):
        refs = list(refs)
        pieces = [refs.pop(0) for _ in range(count)]
        parts = [[refs.pop(0) for _ in range(4)] for _ in range(count - 1)]
        gain, weights, outs = refs[0], refs[1:4], refs[4:]
        for bit in range(count):
            place = pl.ds(pl.multiple_of((here[0] ^ bit) * rows, rows), rows)
            outs[0][place, :] = pieces[bit][...]
            if bit < count - 1:
                values = [part[...] for part in parts[bit]]
            else:
                values = project(pieces[bit][...], gain[...], weights)
            for out, value in zip(outs[1:], values):
                out[place, :] = value

    return small(
        "front_last",
        kernel,
        [(count * rows, width)] * 5,
        *pieces,
        *[array for part in parts for array in part],
        gain,
        *weights,
        scalars=[lax.axis_index("band")],
        cost=SMALL,
    )


def middle_kernel(x_ref, attended_ref, w_out, gain_ref, resid_ref, hidden_ref, hidden_t):
    resid = x_ref[...].astype(F32) + dot_nn(attended_ref[...], w_out[...])
    resid_ref[...] = resid
    hidden = rms_norm(resid, gain_ref[...])
    hidden_ref[...] = hidden.astype(BF)
    hidden_t[...] = jnp.transpose(hidden).astype(BF)


def middle(x, attended, w_out, gain):
    slots, width = x.shape
    rows = 256
    block = pl.BlockSpec((rows, width), lambda g: (g, 0))
    return pl.pallas_call(
        middle_kernel,
        grid=(slots // rows,),
        in_specs=[block, block, IN_VMEM, IN_VMEM],
        out_specs=[block, block, pl.BlockSpec((width, rows), lambda g: (0, g))],
        out_shape=[
            jax.ShapeDtypeStruct((slots, width), F32),
            jax.ShapeDtypeStruct((slots, width), BF),
            jax.ShapeDtypeStruct((width, slots), BF),
        ],
        compiler_params=pltpu.CompilerParams(vmem_limit_bytes=12 * 2**20),
        cost_estimate=SMALL,
        name="middle",
    )(x, attended, w_out, gain)


def turn_kernel(in_ref, out_ref):
    out_ref[...] = jnp.transpose(in_ref[...].astype(F32)).astype(BF)


def turn(matrix):
    rows, columns = matrix.shape
    wide = 256
    return pl.pallas_call(
        turn_kernel,
        grid=(columns // wide,),
        in_specs=[pl.BlockSpec((rows, wide), lambda g: (0, g))],
        out_specs=pl.BlockSpec((wide, rows), lambda g: (g, 0)),
        out_shape=jax.ShapeDtypeStruct((columns, rows), BF),
        compiler_params=pltpu.CompilerParams(vmem_limit_bytes=8 * 2**20),
        cost_estimate=SMALL,
        name="turn",
    )(matrix)


def weight_grad_kernel(groups, swapped, place_ref, *refs):
    refs, out_ref = list(refs[:-1]), refs[-1]
    rows = out_ref.shape[1]
    half = 4 * rows
    start = pl.multiple_of(place_ref[0] * half, half)

    def store(sums, at):
        for block in range(4):
            spot = (block >> 1) | ((block & 1) << 1) if swapped else block
            part = sums[block * rows : (block + 1) * rows]
            out_ref[spot ^ place_ref[1], :, at : at + sums.shape[1]] = part

    at = 0
    for spans in groups:
        mine = refs.pop(0)[pl.ds(start, half), :]
        for span in spans:
            right = refs.pop(0)
            for number, first, count in span:
                for step in range(0, count, 512):
                    wide = min(512, count - step)
                    columns = right[number, :, first + step : first + step + wide]
                    store(dot_nn(mine, columns).astype(BF), at)
                    at += wide


def weight_grad(place, groups, *, spans, swapped=False):
    half = groups[0][0].shape[0] // 2
    inputs = [array for left, rights in groups for array in (left, *rights)]
    total = sum(count for group in spans for span in group for _, _, count in span)
    return pl.pallas_call(
        functools.partial(weight_grad_kernel, spans, swapped),
        in_specs=[IN_SMEM] + [IN_VMEM] * len(inputs),
        out_specs=IN_VMEM,
        out_shape=jax.ShapeDtypeStruct((4, half // 4, total), BF),
        compiler_params=pltpu.CompilerParams(vmem_limit_bytes=8 * 2**20),
        cost_estimate=SMALL,
        name="weight_grad",
    )(place, *inputs)


def ffn_kernel(
    place_ref,
    hidden_ref,
    hidden_t,
    dy_ref,
    dy_t,
    gate_w,
    up_w,
    down_w,
    inner_ref,
    gate_ref,
    up_ref,
    near_ref,
    far_ref,
    gate_w_t,
    up_w_t,
):
    rows = 256
    slope = (2.0 / 3.141592653589793) ** 0.5
    for start in range(0, hidden_ref.shape[0], rows):
        here = slice(start, start + rows)
        gate = dot_nn(hidden_ref[here, :], gate_w[...])
        up = dot_nn(hidden_ref[here, :], up_w[...])
        back = dot_nn(dy_ref[here, :], down_w[...])
        square = gate * gate
        share = 0.5 + 0.5 * jnp.tanh(gate * (slope + (0.044715 * slope) * square))
        active = gate * share
        inner_ref[here, :] = (active * up).astype(BF)
        up_ref[here, :] = (back * active).astype(BF)
        steep = share + (active - active * share) * (
            2.0 * slope + (6.0 * 0.044715 * slope) * square
        )
        gate_ref[here, :] = (back * up * steep).astype(BF)
    gate_w_t[...] = jnp.transpose(gate_w[...].astype(F32)).astype(BF)
    up_w_t[...] = jnp.transpose(up_w[...].astype(F32)).astype(BF)
    height = near_ref.shape[2]
    late = pl.program_id(0) >= pl.num_programs(0) // 2
    turned = (False, True, late)
    lefts, rights = (hidden_t, hidden_t, dy_t), (gate_ref, up_ref, inner_ref)
    for number, (left, right, swapped) in enumerate(zip(lefts, rights, turned)):
        sums = dot_nn(left[...], right[...]).astype(BF)
        for half in range(2):

            def put(target, half=half, sums=sums, number=number, swapped=swapped):
                for block in range(4):
                    straight = block ^ place_ref[1]
                    crossed = ((block >> 1) | ((block & 1) << 1)) ^ place_ref[2]
                    at = (4 * half + block) * height
                    spot = jnp.where(swapped, crossed, straight)
                    target[number, spot] = sums[at : at + height]

            pl.when(place_ref[0] == half)(functools.partial(put, near_ref))
            pl.when(place_ref[0] != half)(functools.partial(put, far_ref))


def ffn(place, hidden, hidden_t, dy, dy_t, w_gate, w_up, w_down_t):
    tokens, width = hidden.shape
    units = w_gate.shape[1]
    chunk = 512
    weight = pl.BlockSpec((width, chunk), lambda g: (0, g))
    wide = pl.BlockSpec((tokens, chunk), lambda g: (0, g))
    half = pl.BlockSpec((3, 4, width // 8, chunk), lambda g: (0, 0, 0, g))
    turned = pl.BlockSpec((chunk, width), lambda g: (g, 0))
    return pl.pallas_call(
        ffn_kernel,
        grid=(units // chunk,),
        in_specs=[IN_SMEM] + [IN_VMEM] * 4 + [weight] * 3,
        out_specs=[wide, wide, wide, half, half, turned, turned],
        out_shape=[jax.ShapeDtypeStruct((tokens, units), BF)] * 3
        + [jax.ShapeDtypeStruct((3, 4, width // 8, units), BF)] * 2
        + [jax.ShapeDtypeStruct((units, width), BF)] * 2,
        compiler_params=pltpu.CompilerParams(vmem_limit_bytes=42 * 2**20),
        cost_estimate=SMALL,
        name="ffn",
    )(place, hidden, hidden_t, dy, dy_t, w_gate, w_up, w_down_t)


def norm_back(values, gain, grad):
    inverse = lax.rsqrt(jnp.mean(values * values, axis=-1, keepdims=True) + 1e-06)
    scaled = values * inverse
    pulled = grad * gain
    return inverse * (pulled - scaled * jnp.mean(scaled * pulled, axis=-1, keepdims=True))


def patch_kernel(splits, *refs):
    parts, refs = refs[:splits], refs[splits:]
    x_ref, grad_ref, gain_ref, *weights, out_ref = refs
    grad = 0.0
    for number, weight in enumerate(weights):
        part = jnp.concatenate([ref[number] for ref in parts], axis=1)
        grad = grad + dot_nn(part, weight[...])
    pulled = norm_back(x_ref[...].astype(F32), gain_ref[...], grad)
    out_ref[...] = (pulled + grad_ref[...]).astype(BF)


def patch_back(parts, x, grad, gain, w_query, w_key, w_value):
    tokens, width = x.shape
    rows = 512
    slim = pl.BlockSpec((rows, width), lambda g: (g, 0))
    part_specs = [pl.BlockSpec((3, rows, part.shape[2]), lambda g: (0, g, 0)) for part in parts]
    return pl.pallas_call(
        functools.partial(patch_kernel, len(parts)),
        grid=(tokens // rows,),
        in_specs=part_specs + [slim, slim] + [IN_VMEM] * 4,
        out_specs=slim,
        out_shape=jax.ShapeDtypeStruct((tokens, width), BF),
        compiler_params=pltpu.CompilerParams(vmem_limit_bytes=22 * 2**20),
        cost_estimate=SMALL,
        name="patch_back",
    )(*parts, x, grad, gain, w_query, w_key, w_value)


def assemble_kernel(recipe, scored, place_ref, near_ref, far_ref, *refs):
    weights, outs, sums_ref = refs[:scored], refs[scored:-1], refs[-1]
    step = pl.program_id(0)
    for far, ref in enumerate((near_ref, far_ref)):

        @pl.when((step >= 4) == (far == 1))
        def _(ref=ref):
            sums = jnp.zeros((ref.shape[1], 1), F32)
            for number, (out_ref, pieces) in enumerate(zip(outs, recipe)):
                at = 0
                for first, columns in pieces:
                    part = ref[0, :, first : first + columns].astype(F32)
                    out_ref[:, at : at + columns] = part
                    if number < scored:
                        weight = weights[number][:, at : at + columns].astype(F32)
                        sums = sums + jnp.sum(part * weight, axis=1, keepdims=True)
                    at += columns
            sums_ref[...] = jnp.broadcast_to(sums, sums_ref.shape)


def assemble(place, near, far, weights, recipe):
    rows = near.shape[1]
    block = (1, rows, near.shape[2])
    widths = [sum(columns for _, columns in pieces) for pieces in recipe]
    placed = [pl.BlockSpec((rows, w), lambda g, place: (g ^ place[2], 0)) for w in widths]
    return pl.pallas_call(
        functools.partial(assemble_kernel, recipe, len(weights)),
        grid_spec=pltpu.PrefetchScalarGridSpec(
            num_scalar_prefetch=1,
            grid=(8,),
            in_specs=[
                pl.BlockSpec(block, lambda g, place: (jnp.minimum(g, 3), 0, 0)),
                pl.BlockSpec(block, lambda g, place: (jnp.maximum(g - 4, 0), 0, 0)),
            ]
            + placed[: len(weights)],
            out_specs=placed + [pl.BlockSpec((rows, 128), lambda g, place: (g ^ place[2], 0))],
        ),
        out_shape=[jax.ShapeDtypeStruct((8 * rows, w), F32) for w in widths + [128]],
        compiler_params=pltpu.CompilerParams(vmem_limit_bytes=18 * 2**20),
        cost_estimate=SMALL,
        name="assemble",
    )(place, near, far, *weights)


def assemble_turned_kernel(place_ref, near_ref, far_ref, out_ref, rows_ref):
    height = near_ref.shape[1]
    for far, ref in enumerate((near_ref, far_ref)):
        for at in range(4):
            block = (4 * far + at) ^ place_ref[2]
            start = pl.multiple_of(block * height, height)
            rows_ref[pl.ds(start, height), :] = ref[at].astype(F32)
    out_ref[...] = jnp.transpose(rows_ref[...])


def assemble_turned(place, near, far, firsts, columns):
    rows = near.shape[1]
    chunk = 256
    half = columns // 2 // chunk
    one, two = (first // chunk for first in firsts)

    def where(g, place):
        return (0, 0, jnp.where(g < half, one + g, two + g - half))

    return pl.pallas_call(
        assemble_turned_kernel,
        grid_spec=pltpu.PrefetchScalarGridSpec(
            num_scalar_prefetch=1,
            grid=(2 * half,),
            in_specs=[pl.BlockSpec((4, rows, chunk), where)] * 2,
            out_specs=pl.BlockSpec((chunk, 8 * rows), lambda g, place: (g, 0)),
            scratch_shapes=[pltpu.VMEM((8 * rows, chunk), F32)],
        ),
        out_shape=jax.ShapeDtypeStruct((columns, 8 * rows), F32),
        compiler_params=pltpu.CompilerParams(vmem_limit_bytes=12 * 2**20),
        cost_estimate=SMALL,
        name="assemble_turned",
    )(place, near, far)


def small(name, kernel, shapes, *inputs, scalars=(), cost=TINY):
    many = [jax.ShapeDtypeStruct(shape, BF) for shape in shapes]
    scalars = [jnp.stack(scalars)] if scalars else []
    return pl.pallas_call(
        kernel,
        in_specs=[IN_SMEM] * len(scalars) + [IN_VMEM] * len(inputs),
        out_specs=[IN_VMEM] * len(many),
        out_shape=many,
        compiler_params=pltpu.CompilerParams(vmem_limit_bytes=8 * 2**20),
        cost_estimate=cost,
        name=name,
    )(*scalars, *inputs)


def add_low(left, right):
    return (left.astype(F32) + right.astype(F32)).astype(BF)


def halve(near, arrived):
    half = near.shape[0] // 2
    shape = (half, *near.shape[1:])

    def kernel(near, come, stays, leaves):
        for block in range(half):
            stays[block] = add_low(near[block], come[block])
            leaves[block] = add_low(near[half + block], come[half + block])

    return small("halve", kernel, [shape, shape], near, arrived)


def first_halves_kernel(near, come, one_stays, one_leaves, two_stays, two_leaves):
    step = pl.program_id(0)
    units = near.shape[3]
    half = units // 2
    for number, outs in enumerate(((one_stays, two_stays), (one_leaves, two_leaves))):

        @pl.when((step >= 2) == (number == 1))
        def _(outs=outs):
            last = add_low(near[2, 0], come[2, 0])
            for stream, out in enumerate(outs):
                out[0, :, :units] = add_low(near[stream, 0], come[stream, 0])
                out[0, :, units:] = last[:, stream * half : (stream + 1) * half]


def first_halves(near, come):
    _, blocks, rows, units = near.shape
    wide = units + units // 2
    stays = pl.BlockSpec((1, rows, wide), lambda g: (jnp.minimum(g, 1), 0, 0))
    leaves = pl.BlockSpec((1, rows, wide), lambda g: (jnp.maximum(g - 2, 0), 0, 0))
    block = pl.BlockSpec((3, 1, rows, units), lambda g: (0, g, 0, 0))
    one, one_go, two, two_go = pl.pallas_call(
        first_halves_kernel,
        grid=(blocks,),
        in_specs=[block, block],
        out_specs=[stays, leaves, stays, leaves],
        out_shape=[jax.ShapeDtypeStruct((2, rows, wide), BF)] * 4,
        compiler_params=pltpu.CompilerParams(vmem_limit_bytes=14 * 2**20),
        cost_estimate=SMALL,
        name="first_halves",
    )(near, come)
    return (one, one_go), (two, two_go)


def join(near, arrived):
    half = near.shape[0]

    def kernel(near, come, out):
        for block in range(half):
            out[block] = near[block]
            out[half + block] = come[block]

    return small("join", kernel, [(2 * half, *near.shape[1:])], near, arrived)[0]


def join_both(one, one_come, two, two_come):
    blocks, rows, wide = one.shape
    other = two.shape[2]

    def kernel(one, one_come, two, two_come, out):
        for number, (left, right) in enumerate(((one, two), (one_come, two_come))):
            for block in range(blocks):
                at = blocks * number + block
                out[at, :, :wide] = left[block]
                out[(at >> 1) | ((at & 1) << 1), :, wide:] = right[block]

    shape = (2 * blocks, rows, wide + other)
    return small("join_both", kernel, [shape], one, one_come, two, two_come)[0]


def apart(blocks):
    count = blocks.shape[0]

    def kernel(here, blocks, *outs):
        for bit, out in enumerate(outs):
            out[...] = blocks[here[0] ^ bit]

    return small(
        "apart", kernel, [blocks.shape[1:]] * count, blocks, scalars=[lax.axis_index("band")]
    )


def in_order(*pieces):
    count = len(pieces)

    def kernel(here, *refs):
        for bit in range(count):
            refs[count][here[0] ^ bit] = refs[bit][...]

    shape = (count, *pieces[0].shape)
    return small("in_order", kernel, [shape], *pieces, scalars=[lax.axis_index("band")])[0]


def bit_of(axis, bit):
    return (lax.axis_index(axis) // bit) % 2


def rows_apart(axis, bit):
    def step(*streams):
        height = streams[0].shape[1] // 2
        widths = [stream.shape[2] for stream in streams[::2]]
        shape = (height, sum(widths))

        def kernel(mine, *refs):
            ins, (stays, leaves) = refs[:-2], refs[-2:]
            for out, half in ((stays, mine[0]), (leaves, 1 - mine[0])):
                rows = pl.ds(pl.multiple_of(half * height, height), height)
                at = 0
                for near, come, wide in zip(ins[::2], ins[1::2], widths):
                    out[:, at : at + wide] = add_low(near[0, rows, :], come[0, rows, :])
                    at += wide

        return small(
            "rows_apart", kernel, [shape, shape], *streams, scalars=[bit_of(axis, bit)]
        )

    return step


def add_up(near, come):
    def kernel(near, come, out):
        out[...] = add_low(near[...], come[...])

    return small("add_up", kernel, [near.shape], near, come)[0]


def rows_join(axis, bit, widths):
    def step(near, come):
        height = near.shape[0]

        def kernel(mine, near, come, *outs):
            for piece, half in ((near, mine[0]), (come, 1 - mine[0])):
                rows = pl.ds(pl.multiple_of(half * height, height), height)
                at = 0
                for out, wide in zip(outs, widths):
                    out[0, rows, :] = piece[:, at : at + wide]
                    at += wide

        shapes = [(1, 2 * height, wide) for wide in widths]
        return small("rows_join", kernel, shapes, near, come, scalars=[bit_of(axis, bit)])

    return step


CORE, ACROSS, ALONG = 1, 2, 4


def flip(axis, bit):
    count = lax.axis_size(axis)
    return [(i, i ^ bit) for i in range(count)]


def swap(array, axis, bit):
    return lax.ppermute(array, axis, flip(axis, bit))


def take(array, number, axis=0):
    return lax.dynamic_index_in_dim(array, number, axis, keepdims=False)


def exchange(pieces):
    return pieces[:1] + tuple(swap(piece, "band", bit + 1) for bit, piece in enumerate(pieces[1:]))


def far_bits():
    plots = lax.axis_size("plots")
    band = lax.axis_size("band")
    bits = [("plots", 1 << n) for n in range(3, plots.bit_length() - 1)]
    return bits + [("band", 1 << n) for n in range(band.bit_length() - 1)]


class Line:
    def __init__(self):
        self.last = ()

    def __call__(self, step, *inputs):
        inputs, _ = lax.optimization_barrier((inputs, self.last))
        self.last = step(*inputs)
        return self.last


def side(axis, bit):
    def step(*streams):
        sums = [add_low(near[0], come[0]) for near, come in zip(streams[::2], streams[1::2])]
        return split_far(axis, bit)(jnp.concatenate(sums, 1))

    return step


def split_far(axis, bit):
    def step(matrix):
        halves = matrix.reshape(2, matrix.shape[0] // 2, matrix.shape[1])
        mine = bit_of(axis, bit)
        return take(halves, mine), take(halves, 1 - mine)

    return step


def join_far(axis, bit):
    def step(matrix, other):
        return jnp.where(
            bit_of(axis, bit) == 0,
            jnp.concatenate([matrix, other]),
            jnp.concatenate([other, matrix]),
        )

    return step


def travel(run, widths, *streams):
    far = far_bits()
    if len(far) == 2:
        first, second = far
        near, leaves = run(rows_apart(*first), *streams)
        come = swap(leaves, *first)
        yield
        near = run(add_up, near, come)
        come = swap(near, *second)
        yield
        near = run(add_up, near, come)
        come = swap(near, *first)
        yield
        return run(rows_join(*first, widths), near, come)
    near, leaves = run(side(*far[0]), *streams)
    come = swap(leaves, *far[0])
    yield
    for axis, bit in far[1:]:
        near, leaves = run(
            lambda near, come, far=(axis, bit): split_far(*far)(add_low(near, come)), near, come
        )
        come = swap(leaves, axis, bit)
        yield
    near = run(add_low, near, come)
    for axis, bit in far[::-1]:
        come = swap(near, axis, bit)
        yield
        near = run(join_far(axis, bit), near, come)
    cuts = [sum(widths[: n + 1]) for n in range(len(widths) - 1)]
    return run(lambda a: jnp.split(a[None], cuts, 2), near)


def rest_of(steps):
    while True:
        try:
            next(steps)
        except StopIteration as end:
            return end.value


def rms_norm(values, gain):
    inverse = lax.rsqrt(jnp.mean(values * values, axis=-1, keepdims=True) + 1e-06)
    return values * inverse * gain


def per_device(
    patches,
    norm1_gain,
    w_query,
    w_key,
    w_value,
    w_out,
    norm2_gain,
    w_gate,
    w_up,
    w_down,
    out_grad,
    plot_rows,
    plot_cols,
    global_index,
):
    width = patches.shape[2]
    here = lax.axis_index("band")
    run = Line()
    slots = patches.shape[0] * patches.shape[1]
    count = patches.shape[0]
    pieces = list(run(apart, patches))
    pieces[1:3] = [swap(piece, "band", bit + 1) for bit, piece in enumerate(pieces[1:3])]
    gain = norm1_gain[None]
    weights = w_query, w_key, w_value
    parts = [run(front, pieces[0], gain, *weights)]
    last = run(lambda *a: a, *pieces[3:])
    pieces[3:] = [swap(piece, "band", bit + 3) for bit, piece in enumerate(last)]
    limits = jnp.stack([take(plot_rows, here), take(plot_cols, here)])
    chosen = take(global_index, here)
    index = jnp.broadcast_to(chosen[:, None], (chosen.shape[0], 128))
    index_t = jnp.broadcast_to(chosen[None, :], (8, chosen.shape[0]))
    bias, pick, pick_t = run(functools.partial(masks, slots=slots), limits, index, index_t)
    w_down_t = run(turn, w_down)
    parts.append(run(front, pieces[1], gain, *weights))
    w_query_t, w_key_t, w_value_t = (run(turn, w) for w in weights)
    for piece in pieces[2:-1]:
        parts.append(run(front, piece, gain, *weights))
    dy_pieces = run(apart, out_grad)
    pieces = run(lambda *a: a, *pieces)
    dy_pieces = exchange(run(lambda *a: a, *dy_pieces))
    x_low, hidden, query, keys, values = run(front_last, pieces, parts, gain, *weights)

    me = lax.axis_index("plots")
    core, across, along = me % 2, (me // ACROSS) % 2, (me // ALONG) % 2
    square, square_t = 2 * across + along, 2 * along + across
    whole = 4 * core + square
    place_near = jnp.stack([core, square, whole])
    place_far = jnp.stack([1 - core, square, whole])
    place_near_t = jnp.stack([core, square_t, whole])
    place_far_t = jnp.stack([1 - core, square_t, whole])
    ff = w_gate.shape[1]

    attended, lse = run(attention, query, keys, values, bias, pick)
    resid, hidden2, hidden2_t = run(middle, x_low, attended, w_out, norm2_gain[None])
    w_out_t = run(turn, w_out)
    dy = run(in_order, *dy_pieces).reshape(slots, width)
    dy_t = run(turn, dy)
    place_ffn = jnp.stack([core, square, square_t])
    inner, grad_gate, grad_up, ffn_near, ffn_far, w_gate_t, w_up_t = run(
        ffn, place_ffn, hidden2, hidden2_t, dy, dy_t, w_gate, w_up, w_down_t
    )
    core_swap = functools.partial(swap, axis="plots", bit=CORE)
    across_swap = functools.partial(swap, axis="plots", bit=ACROSS)
    along_swap = functools.partial(swap, axis="plots", bit=ALONG)
    far = far_bits()

    ffn_come = core_swap(ffn_far)
    mixed_out = run(
        lambda resid, inner, w: (resid + dot_nn(inner, w)).astype(BF), resid, inner, w_down
    )
    mixed_pieces = run(apart, mixed_out.reshape(patches.shape))
    (gate_near, gate_go), (up_near, up_go) = run(first_halves, ffn_near, ffn_come)
    gate_come, up_come = across_swap(gate_go), along_swap(up_go)
    mixed_pieces = exchange(run(lambda *a: a, *mixed_pieces))
    grad_hidden2 = run(
        lambda a, b, c, d: dot_nn(a, c) + dot_nn(b, d), grad_gate, grad_up, w_gate_t, w_up_t
    )

    def resid_back(resid, dy, gain, grad):
        pulled = norm_back(resid, gain, grad) + dy.astype(F32)
        return pulled, pulled.astype(BF)

    grad_resid, resid_low = run(resid_back, resid, dy, norm2_gain, grad_hidden2)
    grad_attended = run(lambda a, w: dot_nn(a, w).astype(BF), resid_low, w_out_t)
    third = width // PAIR // 3

    def back(first):
        return run(
            functools.partial(attention_back, first=first, count=third),
            query,
            keys,
            values,
            grad_attended,
            lse,
            bias,
            pick,
            pick_t,
        )

    back_0 = back(0)
    gate_near, gate_go = run(halve, gate_near, gate_come)
    gate_come = along_swap(gate_go)
    up_near, up_go = run(halve, up_near, up_come)
    up_come = across_swap(up_go)
    back_1 = back(third)
    mixed_out = run(in_order, *mixed_pieces)
    attended_t = run(turn, attended)
    wide_ffn = ff + ff // 2
    ffn_steps = travel(run, [wide_ffn] * 2, gate_near, gate_come, up_near, up_come)
    next(ffn_steps)
    back_2 = back(2 * third)
    hidden_t = run(turn, hidden)
    next(ffn_steps)

    parts = [back_0, back_1, back_2]
    wide = third * PAIR
    half = wide // 2
    rest = width // 2
    out_right = resid_low[None]
    groups = [(hidden_t, parts), (attended_t, [out_right])]
    q_spans = [[[(0, 0, wide), (1, 0, half)]] * 3, [[(0, 0, rest)]]]
    v_spans = [[[(1, half, half), (2, 0, wide)]] * 3, [[(0, rest, width - rest)]]]
    q_grad = functools.partial(weight_grad, spans=q_spans)
    v_grad = functools.partial(weight_grad, spans=v_spans, swapped=True)
    patch_grad = run(
        patch_back, parts, x_low, grad_resid, norm1_gain[None], w_query_t, w_key_t, w_value_t
    )
    pieces = list(run(apart, patch_grad.reshape(patches.shape)))
    q_come = core_swap(run(q_grad, place_far, groups))
    v_come = core_swap(run(v_grad, place_far_t, groups))
    q_near = run(q_grad, place_near, groups)
    q_near, leaves = run(halve, q_near, q_come)
    q_come = across_swap(leaves)
    v_near = run(v_grad, place_near_t, groups)
    v_near, leaves = run(halve, v_near, v_come)
    v_come = along_swap(leaves)
    next(ffn_steps)
    q_near, leaves = run(halve, q_near, q_come)
    q_come = along_swap(leaves)
    v_near, leaves = run(halve, v_near, v_come)
    v_come = across_swap(leaves)
    cut = 3 * (wide + half) + rest
    qkv_steps = travel(
        run, [cut, 3 * (wide + half) + width - rest], q_near, q_come, v_near, v_come
    )
    next(qkv_steps)
    gate_all, up_all = rest_of(ffn_steps)
    gate_come, up_come = along_swap(gate_all), across_swap(up_all)
    next(qkv_steps)
    gate_all = run(join, gate_all, gate_come)
    gate_come = across_swap(gate_all)
    up_all = run(join, up_all, up_come)
    up_come = along_swap(up_all)
    next(qkv_steps)
    q_all, v_all = rest_of(qkv_steps)
    q_come, v_come = along_swap(q_all), across_swap(v_all)
    early = run(lambda *a: a, pieces[1], pieces[2])
    early = [swap(piece, "band", bit + 1) for bit, piece in enumerate(early)]
    ffn_near = run(join_both, gate_all, gate_come, up_all, up_come)
    ffn_come = core_swap(ffn_near)
    q_all = run(join, q_all, q_come)
    q_come = across_swap(q_all)
    v_all = run(join, v_all, v_come)
    v_come = along_swap(v_all)
    recipe_ffn = [[(0, ff)], [(wide_ffn, ff)]]
    gate, up, sums2 = run(
        lambda *arrays: assemble(place_near, *arrays, recipe_ffn),
        ffn_near,
        ffn_come,
        [w_gate, w_up],
    )
    pieces[1:3] = run(lambda *a: a, *early)
    qkv_near = run(join_both, q_all, q_come, v_all, v_come)
    qkv_come = core_swap(qkv_near)
    pieces[3] = swap(run(lambda a: a, pieces[3]), "band", 3)
    down = run(
        lambda near, far: assemble_turned(place_near, near, far, (ff, wide_ffn + ff), ff),
        ffn_near,
        ffn_come,
    )
    recipe = [[], [], [], [(cut - rest, rest), (cut + 3 * (wide + half), width - rest)]]
    for number in range(3):
        at = number * (wide + half)
        recipe[0].append((at, wide))
        recipe[1] += [(at + wide, half), (cut + at, half)]
        recipe[2].append((cut + at + half, wide))
    q_out, k_out, v_out, out, sums1 = run(
        lambda *arrays: assemble(place_near, *arrays, recipe), qkv_near, qkv_come, list(weights)
    )
    patch_grad = run(in_order, *pieces)
    return (
        mixed_out,
        patch_grad,
        sums1[:, 0] / norm1_gain,
        q_out,
        k_out,
        v_out,
        out,
        sums2[:, 0] / norm2_gain,
        gate,
        up,
        down,
    )


def solution(mesh):
    rows = P("plots", "band", None)
    in_specs = (rows,) + (P(),) * 9 + (rows, P("plots"), P("plots"), P("plots", None))
    out_specs = (rows, rows) + (P(),) * 9
    return jax.shard_map(
        per_device, mesh=mesh, in_specs=in_specs, out_specs=out_specs, check_vma=False
    )
```

```python
import functools

import jax
import jax.numpy as jnp
from jax import lax
from jax.experimental import pallas as pl
from jax.experimental.pallas import tpu as pltpu
from jax.sharding import PartitionSpec as P

H = 12
HD = 64
COLS = 64
WIN = 2
TILE_ROWS = 2
PAIR = 2 * HD
BF = jnp.bfloat16
F32 = jnp.float32
LOG2E = 1.4426950408889634
SCALE2 = LOG2E * HD ** (-0.5)
SMALL = pl.CostEstimate(flops=10**10, bytes_accessed=1, transcendentals=0)

TINY = pl.CostEstimate(flops=1, bytes_accessed=1, transcendentals=0)
IN_VMEM = pl.BlockSpec(memory_space=pltpu.VMEM)
IN_SMEM = pl.BlockSpec(memory_space=pltpu.SMEM)


def dot_nt(a, b):
    return lax.dot_general(a, b, (((1,), (1,)), ((), ())), preferred_element_type=F32)


def dot_nn(a, b):
    return lax.dot_general(a, b, (((1,), (0,)), ((), ())), preferred_element_type=F32)


def dot_tn(a, b):
    return lax.dot_general(a, b, (((0,), (0,)), ((), ())), preferred_element_type=F32)


def tiles_of(rows):
    out = []
    for first in range(0, rows, TILE_ROWS):
        low = max(first - WIN, 0)
        high = min(first + TILE_ROWS + WIN, rows)
        out.append((first * COLS, low * COLS, high * COLS))
    return out


def fill_bias(bias_ref, limits_ref, tiles):
    rows_here = limits_ref[0]
    cols_here = limits_ref[1]
    span = TILE_ROWS * COLS
    for number, (query_lo, key_lo, key_hi) in enumerate(tiles):
        count = key_hi - key_lo
        shape = (count, 2 * span)
        key = lax.broadcasted_iota(jnp.int32, shape, 0) + key_lo
        query = lax.broadcasted_iota(jnp.int32, shape, 1) % span + query_lo
        key_row = key // COLS
        apart = key_row - query // COLS
        seen = (apart <= WIN) & (apart >= -WIN) & (key_row < rows_here) & (key % COLS < cols_here)
        bias_ref[number, :count, :] = jnp.where(seen, 0.0, -1e30).astype(F32)


def picker_rows(index_ref, slots):
    chosen = index_ref[:, 0:1]
    lanes = lax.broadcasted_iota(jnp.int32, (chosen.shape[0], slots), 1)
    return (lanes == chosen).astype(F32).astype(BF)


def two_heads(block, lane):
    none = jnp.zeros_like(block)
    return jnp.concatenate([jnp.where(lane < HD, block, none), jnp.where(lane < HD, none, block)])


def own_heads(sums, span):
    return jnp.transpose(jnp.concatenate([sums[:HD, :span], sums[HD:, span:]], axis=0))


def masks_kernel(limits_ref, index_ref, index_t_ref, bias_ref, pick_ref, pick_t_ref):
    slots = pick_ref.shape[1]
    fill_bias(bias_ref, limits_ref, tiles_of(slots // COLS))
    pick_ref[...] = picker_rows(index_ref, slots)
    down = lax.broadcasted_iota(jnp.int32, pick_t_ref.shape, 0)
    pick_t_ref[...] = (down == index_t_ref[0:1, :]).astype(F32).astype(BF)


def masks(limits, index, index_t, slots):
    count = index.shape[0]
    tall = (TILE_ROWS + 2 * WIN) * COLS
    tiles = slots // (TILE_ROWS * COLS)
    return pl.pallas_call(
        masks_kernel,
        in_specs=[IN_SMEM, IN_VMEM, IN_VMEM],
        out_specs=[IN_VMEM] * 3,
        out_shape=[
            jax.ShapeDtypeStruct((tiles, tall, 2 * TILE_ROWS * COLS), F32),
            jax.ShapeDtypeStruct((count, slots), BF),
            jax.ShapeDtypeStruct((slots, count), BF),
        ],
        compiler_params=pltpu.CompilerParams(vmem_limit_bytes=8 * 2**20),
        cost_estimate=SMALL,
        name="masks",
    )(limits, index, index_t)


def attend_kernel(bias_ref, pick_ref, q_ref, k_ref, v_ref, out_ref, lse_ref, value_t):
    slots = q_ref.shape[0]
    tiles = tiles_of(slots // COLS)
    span = TILE_ROWS * COLS
    global_keys = dot_nn(pick_ref[...], k_ref[...]).astype(BF)
    global_values_t = jnp.transpose(dot_nn(pick_ref[...], v_ref[...])).astype(BF)
    value_t[...] = jnp.transpose(v_ref[...].astype(F32)).astype(BF)
    lane = lax.broadcasted_iota(jnp.int32, (span, PAIR), 1)
    for number, (query_lo, key_lo, key_hi) in enumerate(tiles):
        count = key_hi - key_lo
        query = two_heads(q_ref[query_lo : query_lo + span, :], lane)
        window = dot_nt(k_ref[key_lo:key_hi, :], query) * SCALE2 + bias_ref[number, :count, :]
        wide = dot_nt(global_keys, query) * SCALE2
        highest = jnp.maximum(
            jnp.max(window, axis=0, keepdims=True), jnp.max(wide, axis=0, keepdims=True)
        )
        window = jnp.exp2(window - highest)
        wide = jnp.exp2(wide - highest)
        total = jnp.sum(window, axis=0, keepdims=True) + jnp.sum(wide, axis=0, keepdims=True)
        inverse = 1.0 / total
        sums = dot_nn(value_t[:, key_lo:key_hi], (window * inverse).astype(BF))
        sums = sums + dot_nn(global_values_t, (wide * inverse).astype(BF))
        lse_ref[0, number : number + 1, :] = highest + jnp.log2(total)
        out_ref[query_lo : query_lo + span, :] = own_heads(sums, span).astype(BF)


def attend_back_kernel(
    bias_ref,
    pick_ref,
    pick_t_ref,
    q_ref,
    k_ref,
    v_ref,
    g_ref,
    lse_ref,
    out_ref,
    key_t,
    dk_acc,
    dv_acc,
):
    slots = q_ref.shape[0]
    tiles = tiles_of(slots // COLS)
    span = TILE_ROWS * COLS
    globals_here = pick_ref.shape[0]
    global_keys_f = dot_nn(pick_ref[...], k_ref[...])
    global_keys = global_keys_f.astype(BF)
    global_keys_t = jnp.transpose(global_keys_f).astype(BF)
    global_values = dot_nn(pick_ref[...], v_ref[...]).astype(BF)
    key_t[...] = jnp.transpose(k_ref[...].astype(F32)).astype(BF)
    dk_acc[...] = jnp.zeros_like(dk_acc)
    dv_acc[...] = jnp.zeros_like(dv_acc)
    dk_global = jnp.zeros((globals_here, PAIR), F32)
    dv_global = jnp.zeros((globals_here, PAIR), F32)
    lane = lax.broadcasted_iota(jnp.int32, (span, PAIR), 1)
    for number, (query_lo, key_lo, key_hi) in enumerate(tiles):
        count = key_hi - key_lo
        query = two_heads(q_ref[query_lo : query_lo + span, :], lane)
        grad = two_heads(g_ref[query_lo : query_lo + span, :], lane)
        keys = jnp.concatenate([k_ref[key_lo:key_hi, :], global_keys])
        values = jnp.concatenate([v_ref[key_lo:key_hi, :], global_values])
        lse = lse_ref[0, number : number + 1, :]
        scores = dot_nt(keys, query) * SCALE2 - lse
        probs = jnp.exp2(
            jnp.concatenate([scores[:count] + bias_ref[number, :count, :], scores[count:]])
        )
        grad_probs = dot_nt(values, grad)
        weighted = jnp.sum(probs * grad_probs, axis=0, keepdims=True)
        grad_scores = (probs * (grad_probs - weighted)).astype(BF)
        dv = dot_nn(probs.astype(BF), grad)
        dk = dot_nn(grad_scores, query)
        dv_acc[key_lo:key_hi, :] += dv[:count]
        dk_acc[key_lo:key_hi, :] += dk[:count]
        dv_global += dv[count:]
        dk_global += dk[count:]
        seen_t = jnp.concatenate([key_t[:, key_lo:key_hi], global_keys_t], axis=1)
        sums = dot_nn(seen_t, grad_scores)
        sums = own_heads(sums, span) * HD ** (-0.5)
        out_ref[0, query_lo : query_lo + span, :] = sums.astype(BF)

    def spread(part):
        high = part.astype(BF)
        rest = part - high.astype(F32)
        middle = rest.astype(BF)
        low = (rest - middle.astype(F32)).astype(BF)
        picks = pick_t_ref[...]
        return dot_nn(picks, high) + dot_nn(picks, middle) + dot_nn(picks, low)

    out_ref[1] = ((dk_acc[...] + spread(dk_global)) * HD ** (-0.5)).astype(BF)
    out_ref[2] = (dv_acc[...] + spread(dv_global)).astype(BF)


def attention(query, keys, values, bias, pick):
    slots, width = query.shape
    pairs = width // PAIR
    block = pl.BlockSpec((slots, PAIR), lambda p: (0, p))
    tiles = slots // (TILE_ROWS * COLS)
    return pl.pallas_call(
        attend_kernel,
        grid=(pairs,),
        in_specs=[IN_VMEM, IN_VMEM, block, block, block],
        out_specs=[block, pl.BlockSpec((1, tiles, 2 * TILE_ROWS * COLS), lambda p: (p, 0, 0))],
        out_shape=[
            jax.ShapeDtypeStruct((slots, width), BF),
            jax.ShapeDtypeStruct((pairs, tiles, 2 * TILE_ROWS * COLS), F32),
        ],
        scratch_shapes=[pltpu.VMEM((PAIR, slots), BF)],
        compiler_params=pltpu.CompilerParams(vmem_limit_bytes=10 * 2**20),
        cost_estimate=SMALL,
        name="attend",
    )(bias, pick, query, keys, values)


def attention_back(query, keys, values, grad, lse, bias, pick, pick_t, first, count):
    slots = query.shape[0]
    block = pl.BlockSpec((slots, PAIR), lambda p: (0, first + p))
    return pl.pallas_call(
        attend_back_kernel,
        grid=(count,),
        in_specs=[IN_VMEM] * 3
        + [block] * 4
        + [pl.BlockSpec((1, *lse.shape[1:]), lambda p: (first + p, 0, 0))],
        out_specs=pl.BlockSpec((3, slots, PAIR), lambda p: (0, 0, p)),
        out_shape=jax.ShapeDtypeStruct((3, slots, count * PAIR), BF),
        scratch_shapes=[
            pltpu.VMEM((PAIR, slots), BF),
            pltpu.VMEM((slots, PAIR), F32),
            pltpu.VMEM((slots, PAIR), F32),
        ],
        compiler_params=pltpu.CompilerParams(vmem_limit_bytes=12 * 2**20),
        cost_estimate=SMALL,
        name="attend_back",
    )(bias, pick, pick_t, query, keys, values, grad, lse)


def project(piece, gain, weights):
    hidden = rms_norm(piece.astype(F32), gain).astype(BF)
    return [hidden] + [dot_nn(hidden, weight[...]).astype(BF) for weight in weights]


def front(piece, gain, *weights):
    def kernel(piece, gain, *refs):
        for out, value in zip(refs[3:], project(piece[...], gain[...], refs[:3])):
            out[...] = value

    return small("front", kernel, [piece.shape] * 4, piece, gain, *weights, cost=SMALL)


def front_last(pieces, parts, gain, *weights):
    count, (rows, width) = len(pieces), pieces[0].shape

    def kernel(here, *refs):
        refs = list(refs)
        pieces = [refs.pop(0) for _ in range(count)]
        parts = [[refs.pop(0) for _ in range(4)] for _ in range(count - 1)]
        gain, weights, outs = refs[0], refs[1:4], refs[4:]
        for bit in range(count):
            place = pl.ds(pl.multiple_of((here[0] ^ bit) * rows, rows), rows)
            outs[0][place, :] = pieces[bit][...]
            if bit < count - 1:
                values = [part[...] for part in parts[bit]]
            else:
                values = project(pieces[bit][...], gain[...], weights)
            for out, value in zip(outs[1:], values):
                out[place, :] = value

    return small(
        "front_last",
        kernel,
        [(count * rows, width)] * 5,
        *pieces,
        *[array for part in parts for array in part],
        gain,
        *weights,
        scalars=[lax.axis_index("band")],
        cost=SMALL,
    )


def middle_kernel(x_ref, attended_ref, w_out, gain_ref, resid_ref, hidden_ref, hidden_t):
    resid = x_ref[...].astype(F32) + dot_nn(attended_ref[...], w_out[...])
    resid_ref[...] = resid
    hidden = rms_norm(resid, gain_ref[...])
    hidden_ref[...] = hidden.astype(BF)
    hidden_t[...] = jnp.transpose(hidden).astype(BF)


def middle(x, attended, w_out, gain):
    slots, width = x.shape
    rows = 256
    block = pl.BlockSpec((rows, width), lambda g: (g, 0))
    return pl.pallas_call(
        middle_kernel,
        grid=(slots // rows,),
        in_specs=[block, block, IN_VMEM, IN_VMEM],
        out_specs=[block, block, pl.BlockSpec((width, rows), lambda g: (0, g))],
        out_shape=[
            jax.ShapeDtypeStruct((slots, width), F32),
            jax.ShapeDtypeStruct((slots, width), BF),
            jax.ShapeDtypeStruct((width, slots), BF),
        ],
        compiler_params=pltpu.CompilerParams(vmem_limit_bytes=12 * 2**20),
        cost_estimate=SMALL,
        name="middle",
    )(x, attended, w_out, gain)


def turn_kernel(in_ref, out_ref):
    out_ref[...] = jnp.transpose(in_ref[...].astype(F32)).astype(BF)


def turn(matrix):
    rows, columns = matrix.shape
    wide = 256
    return pl.pallas_call(
        turn_kernel,
        grid=(columns // wide,),
        in_specs=[pl.BlockSpec((rows, wide), lambda g: (0, g))],
        out_specs=pl.BlockSpec((wide, rows), lambda g: (g, 0)),
        out_shape=jax.ShapeDtypeStruct((columns, rows), BF),
        compiler_params=pltpu.CompilerParams(vmem_limit_bytes=8 * 2**20),
        cost_estimate=SMALL,
        name="turn",
    )(matrix)


def weight_grad_kernel(groups, swapped, place_ref, *refs):
    refs, out_ref = list(refs[:-1]), refs[-1]
    rows = out_ref.shape[1]
    half = 4 * rows
    start = pl.multiple_of(place_ref[0] * half, half)

    def store(sums, at):
        for block in range(4):
            spot = (block >> 1) | ((block & 1) << 1) if swapped else block
            part = sums[block * rows : (block + 1) * rows]
            out_ref[spot ^ place_ref[1], :, at : at + sums.shape[1]] = part

    at = 0
    for spans in groups:
        mine = refs.pop(0)[pl.ds(start, half), :]
        for span in spans:
            right = refs.pop(0)
            for number, first, count in span:
                for step in range(0, count, 512):
                    wide = min(512, count - step)
                    columns = right[number, :, first + step : first + step + wide]
                    store(dot_nn(mine, columns).astype(BF), at)
                    at += wide


def weight_grad(place, groups, *, spans, swapped=False):
    half = groups[0][0].shape[0] // 2
    inputs = [array for left, rights in groups for array in (left, *rights)]
    total = sum(count for group in spans for span in group for _, _, count in span)
    return pl.pallas_call(
        functools.partial(weight_grad_kernel, spans, swapped),
        in_specs=[IN_SMEM] + [IN_VMEM] * len(inputs),
        out_specs=IN_VMEM,
        out_shape=jax.ShapeDtypeStruct((4, half // 4, total), BF),
        compiler_params=pltpu.CompilerParams(vmem_limit_bytes=8 * 2**20),
        cost_estimate=SMALL,
        name="weight_grad",
    )(place, *inputs)


def ffn_kernel(
    place_ref,
    hidden_ref,
    hidden_t,
    dy_ref,
    dy_t,
    gate_w,
    up_w,
    down_w,
    inner_ref,
    gate_ref,
    up_ref,
    near_ref,
    far_ref,
    gate_w_t,
    up_w_t,
):
    rows = 256
    slope = (2.0 / 3.141592653589793) ** 0.5
    for start in range(0, hidden_ref.shape[0], rows):
        here = slice(start, start + rows)
        gate = dot_nn(hidden_ref[here, :], gate_w[...])
        up = dot_nn(hidden_ref[here, :], up_w[...])
        back = dot_nn(dy_ref[here, :], down_w[...])
        square = gate * gate
        share = 0.5 + 0.5 * jnp.tanh(gate * (slope + (0.044715 * slope) * square))
        active = gate * share
        inner_ref[here, :] = (active * up).astype(BF)
        up_ref[here, :] = (back * active).astype(BF)
        steep = share + (active - active * share) * (
            2.0 * slope + (6.0 * 0.044715 * slope) * square
        )
        gate_ref[here, :] = (back * up * steep).astype(BF)
    gate_w_t[...] = jnp.transpose(gate_w[...].astype(F32)).astype(BF)
    up_w_t[...] = jnp.transpose(up_w[...].astype(F32)).astype(BF)
    height = near_ref.shape[2]
    late = pl.program_id(0) >= pl.num_programs(0) // 2
    turned = (False, True, late)
    lefts, rights = (hidden_t, hidden_t, dy_t), (gate_ref, up_ref, inner_ref)
    for number, (left, right, swapped) in enumerate(zip(lefts, rights, turned)):
        sums = dot_nn(left[...], right[...]).astype(BF)
        for half in range(2):

            def put(target, half=half, sums=sums, number=number, swapped=swapped):
                for block in range(4):
                    straight = block ^ place_ref[1]
                    crossed = ((block >> 1) | ((block & 1) << 1)) ^ place_ref[2]
                    at = (4 * half + block) * height
                    spot = jnp.where(swapped, crossed, straight)
                    target[number, spot] = sums[at : at + height]

            pl.when(place_ref[0] == half)(functools.partial(put, near_ref))
            pl.when(place_ref[0] != half)(functools.partial(put, far_ref))


def ffn(place, hidden, hidden_t, dy, dy_t, w_gate, w_up, w_down_t):
    tokens, width = hidden.shape
    units = w_gate.shape[1]
    chunk = 512
    weight = pl.BlockSpec((width, chunk), lambda g: (0, g))
    wide = pl.BlockSpec((tokens, chunk), lambda g: (0, g))
    half = pl.BlockSpec((3, 4, width // 8, chunk), lambda g: (0, 0, 0, g))
    turned = pl.BlockSpec((chunk, width), lambda g: (g, 0))
    return pl.pallas_call(
        ffn_kernel,
        grid=(units // chunk,),
        in_specs=[IN_SMEM] + [IN_VMEM] * 4 + [weight] * 3,
        out_specs=[wide, wide, wide, half, half, turned, turned],
        out_shape=[jax.ShapeDtypeStruct((tokens, units), BF)] * 3
        + [jax.ShapeDtypeStruct((3, 4, width // 8, units), BF)] * 2
        + [jax.ShapeDtypeStruct((units, width), BF)] * 2,
        compiler_params=pltpu.CompilerParams(vmem_limit_bytes=42 * 2**20),
        cost_estimate=SMALL,
        name="ffn",
    )(place, hidden, hidden_t, dy, dy_t, w_gate, w_up, w_down_t)


def norm_back(values, gain, grad):
    inverse = lax.rsqrt(jnp.mean(values * values, axis=-1, keepdims=True) + 1e-06)
    scaled = values * inverse
    pulled = grad * gain
    return inverse * (pulled - scaled * jnp.mean(scaled * pulled, axis=-1, keepdims=True))


def patch_kernel(splits, *refs):
    parts, refs = refs[:splits], refs[splits:]
    x_ref, grad_ref, gain_ref, *weights, out_ref = refs
    grad = 0.0
    for number, weight in enumerate(weights):
        part = jnp.concatenate([ref[number] for ref in parts], axis=1)
        grad = grad + dot_nn(part, weight[...])
    pulled = norm_back(x_ref[...].astype(F32), gain_ref[...], grad)
    out_ref[...] = (pulled + grad_ref[...]).astype(BF)


def patch_back(parts, x, grad, gain, w_query, w_key, w_value):
    tokens, width = x.shape
    rows = 512
    slim = pl.BlockSpec((rows, width), lambda g: (g, 0))
    part_specs = [pl.BlockSpec((3, rows, part.shape[2]), lambda g: (0, g, 0)) for part in parts]
    return pl.pallas_call(
        functools.partial(patch_kernel, len(parts)),
        grid=(tokens // rows,),
        in_specs=part_specs + [slim, slim] + [IN_VMEM] * 4,
        out_specs=slim,
        out_shape=jax.ShapeDtypeStruct((tokens, width), BF),
        compiler_params=pltpu.CompilerParams(vmem_limit_bytes=22 * 2**20),
        cost_estimate=SMALL,
        name="patch_back",
    )(*parts, x, grad, gain, w_query, w_key, w_value)


def assemble_kernel(recipe, scored, place_ref, near_ref, far_ref, *refs):
    weights, outs, sums_ref = refs[:scored], refs[scored:-1], refs[-1]
    step = pl.program_id(0)
    for far, ref in enumerate((near_ref, far_ref)):

        @pl.when((step >= 4) == (far == 1))
        def _(ref=ref):
            sums = jnp.zeros((ref.shape[1], 1), F32)
            for number, (out_ref, pieces) in enumerate(zip(outs, recipe)):
                at = 0
                for first, columns in pieces:
                    part = ref[0, :, first : first + columns].astype(F32)
                    out_ref[:, at : at + columns] = part
                    if number < scored:
                        weight = weights[number][:, at : at + columns].astype(F32)
                        sums = sums + jnp.sum(part * weight, axis=1, keepdims=True)
                    at += columns
            sums_ref[...] = jnp.broadcast_to(sums, sums_ref.shape)


def assemble(place, near, far, weights, recipe):
    rows = near.shape[1]
    block = (1, rows, near.shape[2])
    widths = [sum(columns for _, columns in pieces) for pieces in recipe]
    placed = [pl.BlockSpec((rows, w), lambda g, place: (g ^ place[2], 0)) for w in widths]
    return pl.pallas_call(
        functools.partial(assemble_kernel, recipe, len(weights)),
        grid_spec=pltpu.PrefetchScalarGridSpec(
            num_scalar_prefetch=1,
            grid=(8,),
            in_specs=[
                pl.BlockSpec(block, lambda g, place: (jnp.minimum(g, 3), 0, 0)),
                pl.BlockSpec(block, lambda g, place: (jnp.maximum(g - 4, 0), 0, 0)),
            ]
            + placed[: len(weights)],
            out_specs=placed + [pl.BlockSpec((rows, 128), lambda g, place: (g ^ place[2], 0))],
        ),
        out_shape=[jax.ShapeDtypeStruct((8 * rows, w), F32) for w in widths + [128]],
        compiler_params=pltpu.CompilerParams(vmem_limit_bytes=18 * 2**20),
        cost_estimate=SMALL,
        name="assemble",
    )(place, near, far, *weights)


def assemble_turned_kernel(place_ref, near_ref, far_ref, out_ref, rows_ref):
    height = near_ref.shape[1]
    for far, ref in enumerate((near_ref, far_ref)):
        for at in range(4):
            block = (4 * far + at) ^ place_ref[2]
            start = pl.multiple_of(block * height, height)
            rows_ref[pl.ds(start, height), :] = ref[at].astype(F32)
    out_ref[...] = jnp.transpose(rows_ref[...])


def assemble_turned(place, near, far, firsts, columns):
    rows = near.shape[1]
    chunk = 256
    half = columns // 2 // chunk
    one, two = (first // chunk for first in firsts)

    def where(g, place):
        return (0, 0, jnp.where(g < half, one + g, two + g - half))

    return pl.pallas_call(
        assemble_turned_kernel,
        grid_spec=pltpu.PrefetchScalarGridSpec(
            num_scalar_prefetch=1,
            grid=(2 * half,),
            in_specs=[pl.BlockSpec((4, rows, chunk), where)] * 2,
            out_specs=pl.BlockSpec((chunk, 8 * rows), lambda g, place: (g, 0)),
            scratch_shapes=[pltpu.VMEM((8 * rows, chunk), F32)],
        ),
        out_shape=jax.ShapeDtypeStruct((columns, 8 * rows), F32),
        compiler_params=pltpu.CompilerParams(vmem_limit_bytes=12 * 2**20),
        cost_estimate=SMALL,
        name="assemble_turned",
    )(place, near, far)


def small(name, kernel, shapes, *inputs, scalars=(), cost=TINY):
    many = [jax.ShapeDtypeStruct(shape, BF) for shape in shapes]
    scalars = [jnp.stack(scalars)] if scalars else []
    return pl.pallas_call(
        kernel,
        in_specs=[IN_SMEM] * len(scalars) + [IN_VMEM] * len(inputs),
        out_specs=[IN_VMEM] * len(many),
        out_shape=many,
        compiler_params=pltpu.CompilerParams(vmem_limit_bytes=8 * 2**20),
        cost_estimate=cost,
        name=name,
    )(*scalars, *inputs)


def add_low(left, right):
    return (left.astype(F32) + right.astype(F32)).astype(BF)


def halve(near, arrived):
    half = near.shape[0] // 2
    shape = (half, *near.shape[1:])

    def kernel(near, come, stays, leaves):
        for block in range(half):
            stays[block] = add_low(near[block], come[block])
            leaves[block] = add_low(near[half + block], come[half + block])

    return small("halve", kernel, [shape, shape], near, arrived)


def first_halves_kernel(near, come, one_stays, one_leaves, two_stays, two_leaves):
    step = pl.program_id(0)
    units = near.shape[3]
    half = units // 2
    for number, outs in enumerate(((one_stays, two_stays), (one_leaves, two_leaves))):

        @pl.when((step >= 2) == (number == 1))
        def _(outs=outs):
            last = add_low(near[2, 0], come[2, 0])
            for stream, out in enumerate(outs):
                out[0, :, :units] = add_low(near[stream, 0], come[stream, 0])
                out[0, :, units:] = last[:, stream * half : (stream + 1) * half]


def first_halves(near, come):
    _, blocks, rows, units = near.shape
    wide = units + units // 2
    stays = pl.BlockSpec((1, rows, wide), lambda g: (jnp.minimum(g, 1), 0, 0))
    leaves = pl.BlockSpec((1, rows, wide), lambda g: (jnp.maximum(g - 2, 0), 0, 0))
    block = pl.BlockSpec((3, 1, rows, units), lambda g: (0, g, 0, 0))
    one, one_go, two, two_go = pl.pallas_call(
        first_halves_kernel,
        grid=(blocks,),
        in_specs=[block, block],
        out_specs=[stays, leaves, stays, leaves],
        out_shape=[jax.ShapeDtypeStruct((2, rows, wide), BF)] * 4,
        compiler_params=pltpu.CompilerParams(vmem_limit_bytes=14 * 2**20),
        cost_estimate=SMALL,
        name="first_halves",
    )(near, come)
    return (one, one_go), (two, two_go)


def join(near, arrived):
    half = near.shape[0]

    def kernel(near, come, out):
        for block in range(half):
            out[block] = near[block]
            out[half + block] = come[block]

    return small("join", kernel, [(2 * half, *near.shape[1:])], near, arrived)[0]


def join_both(one, one_come, two, two_come):
    blocks, rows, wide = one.shape
    other = two.shape[2]

    def kernel(one, one_come, two, two_come, out):
        for number, (left, right) in enumerate(((one, two), (one_come, two_come))):
            for block in range(blocks):
                at = blocks * number + block
                out[at, :, :wide] = left[block]
                out[(at >> 1) | ((at & 1) << 1), :, wide:] = right[block]

    shape = (2 * blocks, rows, wide + other)
    return small("join_both", kernel, [shape], one, one_come, two, two_come)[0]


def apart(blocks):
    count = blocks.shape[0]

    def kernel(here, blocks, *outs):
        for bit, out in enumerate(outs):
            out[...] = blocks[here[0] ^ bit]

    return small(
        "apart", kernel, [blocks.shape[1:]] * count, blocks, scalars=[lax.axis_index("band")]
    )


def in_order(*pieces):
    count = len(pieces)

    def kernel(here, *refs):
        for bit in range(count):
            refs[count][here[0] ^ bit] = refs[bit][...]

    shape = (count, *pieces[0].shape)
    return small("in_order", kernel, [shape], *pieces, scalars=[lax.axis_index("band")])[0]


def bit_of(axis, bit):
    return (lax.axis_index(axis) // bit) % 2


def rows_apart(axis, bit):
    def step(*streams):
        height = streams[0].shape[1] // 2
        widths = [stream.shape[2] for stream in streams[::2]]
        shape = (height, sum(widths))

        def kernel(mine, *refs):
            ins, (stays, leaves) = refs[:-2], refs[-2:]
            for out, half in ((stays, mine[0]), (leaves, 1 - mine[0])):
                rows = pl.ds(pl.multiple_of(half * height, height), height)
                at = 0
                for near, come, wide in zip(ins[::2], ins[1::2], widths):
                    out[:, at : at + wide] = add_low(near[0, rows, :], come[0, rows, :])
                    at += wide

        return small(
            "rows_apart", kernel, [shape, shape], *streams, scalars=[bit_of(axis, bit)]
        )

    return step


def add_up(near, come):
    def kernel(near, come, out):
        out[...] = add_low(near[...], come[...])

    return small("add_up", kernel, [near.shape], near, come)[0]


def rows_join(axis, bit, widths):
    def step(near, come):
        height = near.shape[0]

        def kernel(mine, near, come, *outs):
            for piece, half in ((near, mine[0]), (come, 1 - mine[0])):
                rows = pl.ds(pl.multiple_of(half * height, height), height)
                at = 0
                for out, wide in zip(outs, widths):
                    out[0, rows, :] = piece[:, at : at + wide]
                    at += wide

        shapes = [(1, 2 * height, wide) for wide in widths]
        return small("rows_join", kernel, shapes, near, come, scalars=[bit_of(axis, bit)])

    return step


CORE, ACROSS, ALONG = 1, 2, 4


def flip(axis, bit):
    count = lax.axis_size(axis)
    return [(i, i ^ bit) for i in range(count)]


def swap(array, axis, bit):
    return lax.ppermute(array, axis, flip(axis, bit))


def take(array, number, axis=0):
    return lax.dynamic_index_in_dim(array, number, axis, keepdims=False)


def exchange(pieces):
    return pieces[:1] + tuple(swap(piece, "band", bit + 1) for bit, piece in enumerate(pieces[1:]))


def far_bits():
    plots = lax.axis_size("plots")
    band = lax.axis_size("band")
    bits = [("plots", 1 << n) for n in range(3, plots.bit_length() - 1)]
    return bits + [("band", 1 << n) for n in range(band.bit_length() - 1)]


class Line:
    def __init__(self):
        self.last = ()

    def __call__(self, step, *inputs):
        inputs, _ = lax.optimization_barrier((inputs, self.last))
        self.last = step(*inputs)
        return self.last


def side(axis, bit):
    def step(*streams):
        sums = [add_low(near[0], come[0]) for near, come in zip(streams[::2], streams[1::2])]
        return split_far(axis, bit)(jnp.concatenate(sums, 1))

    return step


def split_far(axis, bit):
    def step(matrix):
        halves = matrix.reshape(2, matrix.shape[0] // 2, matrix.shape[1])
        mine = bit_of(axis, bit)
        return take(halves, mine), take(halves, 1 - mine)

    return step


def join_far(axis, bit):
    def step(matrix, other):
        return jnp.where(
            bit_of(axis, bit) == 0,
            jnp.concatenate([matrix, other]),
            jnp.concatenate([other, matrix]),
        )

    return step


def travel(run, widths, *streams):
    far = far_bits()
    if len(far) == 2:
        first, second = far
        near, leaves = run(rows_apart(*first), *streams)
        come = swap(leaves, *first)
        yield
        near = run(add_up, near, come)
        come = swap(near, *second)
        yield
        near = run(add_up, near, come)
        come = swap(near, *first)
        yield
        return run(rows_join(*first, widths), near, come)
    near, leaves = run(side(*far[0]), *streams)
    come = swap(leaves, *far[0])
    yield
    for axis, bit in far[1:]:
        near, leaves = run(
            lambda near, come, far=(axis, bit): split_far(*far)(add_low(near, come)), near, come
        )
        come = swap(leaves, axis, bit)
        yield
    near = run(add_low, near, come)
    for axis, bit in far[::-1]:
        come = swap(near, axis, bit)
        yield
        near = run(join_far(axis, bit), near, come)
    cuts = [sum(widths[: n + 1]) for n in range(len(widths) - 1)]
    return run(lambda a: jnp.split(a[None], cuts, 2), near)


def rest_of(steps):
    while True:
        try:
            next(steps)
        except StopIteration as end:
            return end.value


def rms_norm(values, gain):
    inverse = lax.rsqrt(jnp.mean(values * values, axis=-1, keepdims=True) + 1e-06)
    return values * inverse * gain


def per_device(
    patches,
    norm1_gain,
    w_query,
    w_key,
    w_value,
    w_out,
    norm2_gain,
    w_gate,
    w_up,
    w_down,
    out_grad,
    plot_rows,
    plot_cols,
    global_index,
):
    width = patches.shape[2]
    here = lax.axis_index("band")
    run = Line()
    slots = patches.shape[0] * patches.shape[1]
    count = patches.shape[0]
    pieces = list(run(apart, patches))
    pieces[1:3] = [swap(piece, "band", bit + 1) for bit, piece in enumerate(pieces[1:3])]
    gain = norm1_gain[None]
    weights = w_query, w_key, w_value
    parts = [run(front, pieces[0], gain, *weights)]
    last = run(lambda *a: a, *pieces[3:])
    pieces[3:] = [swap(piece, "band", bit + 3) for bit, piece in enumerate(last)]
    limits = jnp.stack([take(plot_rows, here), take(plot_cols, here)])
    chosen = take(global_index, here)
    index = jnp.broadcast_to(chosen[:, None], (chosen.shape[0], 128))
    index_t = jnp.broadcast_to(chosen[None, :], (8, chosen.shape[0]))
    bias, pick, pick_t = run(functools.partial(masks, slots=slots), limits, index, index_t)
    w_down_t = run(turn, w_down)
    parts.append(run(front, pieces[1], gain, *weights))
    w_query_t, w_key_t, w_value_t = (run(turn, w) for w in weights)
    for piece in pieces[2:-1]:
        parts.append(run(front, piece, gain, *weights))
    dy_pieces = run(apart, out_grad)
    pieces = run(lambda *a: a, *pieces)
    dy_pieces = exchange(run(lambda *a: a, *dy_pieces))
    x_low, hidden, query, keys, values = run(front_last, pieces, parts, gain, *weights)

    me = lax.axis_index("plots")
    core, across, along = me % 2, (me // ACROSS) % 2, (me // ALONG) % 2
    square, square_t = 2 * across + along, 2 * along + across
    whole = 4 * core + square
    place_near = jnp.stack([core, square, whole])
    place_far = jnp.stack([1 - core, square, whole])
    place_near_t = jnp.stack([core, square_t, whole])
    place_far_t = jnp.stack([1 - core, square_t, whole])
    ff = w_gate.shape[1]

    attended, lse = run(attention, query, keys, values, bias, pick)
    resid, hidden2, hidden2_t = run(middle, x_low, attended, w_out, norm2_gain[None])
    w_out_t = run(turn, w_out)
    attended_t, hidden_t = run(turn, attended), run(turn, hidden)
    dy = run(in_order, *dy_pieces).reshape(slots, width)
    dy_t = run(turn, dy)
    place_ffn = jnp.stack([core, square, square_t])
    inner, grad_gate, grad_up, ffn_near, ffn_far, w_gate_t, w_up_t = run(
        ffn, place_ffn, hidden2, hidden2_t, dy, dy_t, w_gate, w_up, w_down_t
    )
    core_swap = functools.partial(swap, axis="plots", bit=CORE)
    across_swap = functools.partial(swap, axis="plots", bit=ACROSS)
    along_swap = functools.partial(swap, axis="plots", bit=ALONG)
    far = far_bits()

    ffn_come = core_swap(ffn_far)
    mixed_out = run(
        lambda resid, inner, w: (resid + dot_nn(inner, w)).astype(BF), resid, inner, w_down
    )
    mixed_pieces = run(apart, mixed_out.reshape(patches.shape))
    (gate_near, gate_go), (up_near, up_go) = run(first_halves, ffn_near, ffn_come)
    gate_come, up_come = across_swap(gate_go), along_swap(up_go)
    mixed_pieces = exchange(run(lambda *a: a, *mixed_pieces))
    grad_hidden2 = run(
        lambda a, b, c, d: dot_nn(a, c) + dot_nn(b, d), grad_gate, grad_up, w_gate_t, w_up_t
    )

    def resid_back(resid, dy, gain, grad):
        pulled = norm_back(resid, gain, grad) + dy.astype(F32)
        return pulled, pulled.astype(BF)

    grad_resid, resid_low = run(resid_back, resid, dy, norm2_gain, grad_hidden2)
    grad_attended = run(lambda a, w: dot_nn(a, w).astype(BF), resid_low, w_out_t)
    third = width // PAIR // 3

    def back(first):
        return run(
            functools.partial(attention_back, first=first, count=third),
            query,
            keys,
            values,
            grad_attended,
            lse,
            bias,
            pick,
            pick_t,
        )

    back_0 = back(0)
    gate_near, gate_go = run(halve, gate_near, gate_come)
    gate_come = along_swap(gate_go)
    up_near, up_go = run(halve, up_near, up_come)
    up_come = across_swap(up_go)
    back_1 = back(third)
    mixed_out = run(in_order, *mixed_pieces)
    wide_ffn = ff + ff // 2
    ffn_steps = travel(run, [wide_ffn] * 2, gate_near, gate_come, up_near, up_come)
    next(ffn_steps)
    back_2 = back(2 * third)
    next(ffn_steps)

    parts = [back_0, back_1, back_2]
    wide = third * PAIR
    half = wide // 2
    rest = width // 2
    out_right = resid_low[None]
    groups = [(hidden_t, parts), (attended_t, [out_right])]
    q_spans = [[[(0, 0, wide), (1, 0, half)]] * 3, [[(0, 0, rest)]]]
    v_spans = [[[(1, half, half), (2, 0, wide)]] * 3, [[(0, rest, width - rest)]]]
    q_grad = functools.partial(weight_grad, spans=q_spans)
    v_grad = functools.partial(weight_grad, spans=v_spans, swapped=True)
    patch_grad = run(
        patch_back, parts, x_low, grad_resid, norm1_gain[None], w_query_t, w_key_t, w_value_t
    )
    pieces = list(run(apart, patch_grad.reshape(patches.shape)))
    q_come = core_swap(run(q_grad, place_far, groups))
    v_come = core_swap(run(v_grad, place_far_t, groups))
    q_near = run(q_grad, place_near, groups)
    q_near, leaves = run(halve, q_near, q_come)
    q_come = across_swap(leaves)
    v_near = run(v_grad, place_near_t, groups)
    v_near, leaves = run(halve, v_near, v_come)
    v_come = along_swap(leaves)
    next(ffn_steps)
    q_near, leaves = run(halve, q_near, q_come)
    q_come = along_swap(leaves)
    v_near, leaves = run(halve, v_near, v_come)
    v_come = across_swap(leaves)
    cut = 3 * (wide + half) + rest
    qkv_steps = travel(
        run, [cut, 3 * (wide + half) + width - rest], q_near, q_come, v_near, v_come
    )
    next(qkv_steps)
    gate_all, up_all = rest_of(ffn_steps)
    gate_come, up_come = along_swap(gate_all), across_swap(up_all)
    next(qkv_steps)
    gate_all = run(join, gate_all, gate_come)
    gate_come = across_swap(gate_all)
    up_all = run(join, up_all, up_come)
    up_come = along_swap(up_all)
    next(qkv_steps)
    q_all, v_all = rest_of(qkv_steps)
    q_come, v_come = along_swap(q_all), across_swap(v_all)
    early = run(lambda *a: a, pieces[1], pieces[2])
    early = [swap(piece, "band", bit + 1) for bit, piece in enumerate(early)]
    ffn_near = run(join_both, gate_all, gate_come, up_all, up_come)
    ffn_come = core_swap(ffn_near)
    q_all = run(join, q_all, q_come)
    q_come = across_swap(q_all)
    v_all = run(join, v_all, v_come)
    v_come = along_swap(v_all)
    recipe_ffn = [[(0, ff)], [(wide_ffn, ff)]]
    gate, up, sums2 = run(
        lambda *arrays: assemble(place_near, *arrays, recipe_ffn),
        ffn_near,
        ffn_come,
        [w_gate, w_up],
    )
    pieces[1:3] = run(lambda *a: a, *early)
    qkv_near = run(join_both, q_all, q_come, v_all, v_come)
    qkv_come = core_swap(qkv_near)
    pieces[3] = swap(run(lambda a: a, pieces[3]), "band", 3)
    down = run(
        lambda near, far: assemble_turned(place_near, near, far, (ff, wide_ffn + ff), ff),
        ffn_near,
        ffn_come,
    )
    recipe = [[], [], [], [(cut - rest, rest), (cut + 3 * (wide + half), width - rest)]]
    for number in range(3):
        at = number * (wide + half)
        recipe[0].append((at, wide))
        recipe[1] += [(at + wide, half), (cut + at, half)]
        recipe[2].append((cut + at + half, wide))
    q_out, k_out, v_out, out, sums1 = run(
        lambda *arrays: assemble(place_near, *arrays, recipe), qkv_near, qkv_come, list(weights)
    )
    patch_grad = run(in_order, *pieces)
    return (
        mixed_out,
        patch_grad,
        sums1[:, 0] / norm1_gain,
        q_out,
        k_out,
        v_out,
        out,
        sums2[:, 0] / norm2_gain,
        gate,
        up,
        down,
    )


def solution(mesh):
    rows = P("plots", "band", None)
    in_specs = (rows,) + (P(),) * 9 + (rows, P("plots"), P("plots"), P("plots", None))
    out_specs = (rows, rows) + (P(),) * 9
    return jax.shard_map(
        per_device, mesh=mesh, in_specs=in_specs, out_specs=out_specs, check_vma=False
    )
```

```python
import functools

import jax
import jax.numpy as jnp
from jax import lax
from jax.experimental import pallas as pl
from jax.experimental.pallas import tpu as pltpu
from jax.sharding import PartitionSpec as P

H = 12
HD = 64
COLS = 64
WIN = 2
TILE_ROWS = 2
PAIR = 2 * HD
BF = jnp.bfloat16
F32 = jnp.float32
LOG2E = 1.4426950408889634
SCALE2 = LOG2E * HD ** (-0.5)
SMALL = pl.CostEstimate(flops=10**10, bytes_accessed=1, transcendentals=0)

TINY = pl.CostEstimate(flops=1, bytes_accessed=1, transcendentals=0)
IN_VMEM = pl.BlockSpec(memory_space=pltpu.VMEM)
IN_SMEM = pl.BlockSpec(memory_space=pltpu.SMEM)


def dot_nt(a, b):
    return lax.dot_general(a, b, (((1,), (1,)), ((), ())), preferred_element_type=F32)


def dot_nn(a, b):
    return lax.dot_general(a, b, (((1,), (0,)), ((), ())), preferred_element_type=F32)


def dot_tn(a, b):
    return lax.dot_general(a, b, (((0,), (0,)), ((), ())), preferred_element_type=F32)


def tiles_of(rows):
    out = []
    for first in range(0, rows, TILE_ROWS):
        low = max(first - WIN, 0)
        high = min(first + TILE_ROWS + WIN, rows)
        out.append((first * COLS, low * COLS, high * COLS))
    return out


def fill_bias(bias_ref, limits_ref, tiles):
    rows_here = limits_ref[0]
    cols_here = limits_ref[1]
    span = TILE_ROWS * COLS
    for number, (query_lo, key_lo, key_hi) in enumerate(tiles):
        count = key_hi - key_lo
        shape = (count, 2 * span)
        key = lax.broadcasted_iota(jnp.int32, shape, 0) + key_lo
        query = lax.broadcasted_iota(jnp.int32, shape, 1) % span + query_lo
        key_row = key // COLS
        apart = key_row - query // COLS
        seen = (apart <= WIN) & (apart >= -WIN) & (key_row < rows_here) & (key % COLS < cols_here)
        bias_ref[number, :count, :] = jnp.where(seen, 0.0, -1e30).astype(F32)


def picker_rows(index_ref, slots):
    chosen = index_ref[:, 0:1]
    lanes = lax.broadcasted_iota(jnp.int32, (chosen.shape[0], slots), 1)
    return (lanes == chosen).astype(F32).astype(BF)


def two_heads(block, lane):
    none = jnp.zeros_like(block)
    return jnp.concatenate([jnp.where(lane < HD, block, none), jnp.where(lane < HD, none, block)])


def own_heads(sums, span):
    return jnp.transpose(jnp.concatenate([sums[:HD, :span], sums[HD:, span:]], axis=0))


def masks_kernel(limits_ref, index_ref, index_t_ref, bias_ref, pick_ref, pick_t_ref):
    slots = pick_ref.shape[1]
    fill_bias(bias_ref, limits_ref, tiles_of(slots // COLS))
    pick_ref[...] = picker_rows(index_ref, slots)
    down = lax.broadcasted_iota(jnp.int32, pick_t_ref.shape, 0)
    pick_t_ref[...] = (down == index_t_ref[0:1, :]).astype(F32).astype(BF)


def masks(limits, index, index_t, slots):
    count = index.shape[0]
    tall = (TILE_ROWS + 2 * WIN) * COLS
    tiles = slots // (TILE_ROWS * COLS)
    return pl.pallas_call(
        masks_kernel,
        in_specs=[IN_SMEM, IN_VMEM, IN_VMEM],
        out_specs=[IN_VMEM] * 3,
        out_shape=[
            jax.ShapeDtypeStruct((tiles, tall, 2 * TILE_ROWS * COLS), F32),
            jax.ShapeDtypeStruct((count, slots), BF),
            jax.ShapeDtypeStruct((slots, count), BF),
        ],
        compiler_params=pltpu.CompilerParams(vmem_limit_bytes=8 * 2**20),
        cost_estimate=SMALL,
        name="masks",
    )(limits, index, index_t)


def attend_kernel(bias_ref, pick_ref, q_ref, k_ref, v_ref, out_ref, lse_ref, value_t):
    slots = q_ref.shape[0]
    tiles = tiles_of(slots // COLS)
    span = TILE_ROWS * COLS
    global_keys = dot_nn(pick_ref[...], k_ref[...]).astype(BF)
    global_values_t = jnp.transpose(dot_nn(pick_ref[...], v_ref[...])).astype(BF)
    value_t[...] = jnp.transpose(v_ref[...].astype(F32)).astype(BF)
    lane = lax.broadcasted_iota(jnp.int32, (span, PAIR), 1)
    for number, (query_lo, key_lo, key_hi) in enumerate(tiles):
        count = key_hi - key_lo
        query = two_heads(q_ref[query_lo : query_lo + span, :], lane)
        window = dot_nt(k_ref[key_lo:key_hi, :], query) * SCALE2 + bias_ref[number, :count, :]
        wide = dot_nt(global_keys, query) * SCALE2
        highest = jnp.maximum(
            jnp.max(window, axis=0, keepdims=True), jnp.max(wide, axis=0, keepdims=True)
        )
        window = jnp.exp2(window - highest)
        wide = jnp.exp2(wide - highest)
        total = jnp.sum(window, axis=0, keepdims=True) + jnp.sum(wide, axis=0, keepdims=True)
        inverse = 1.0 / total
        sums = dot_nn(value_t[:, key_lo:key_hi], (window * inverse).astype(BF))
        sums = sums + dot_nn(global_values_t, (wide * inverse).astype(BF))
        lse_ref[0, number : number + 1, :] = highest + jnp.log2(total)
        out_ref[query_lo : query_lo + span, :] = own_heads(sums, span).astype(BF)


def attend_back_kernel(
    bias_ref,
    pick_ref,
    pick_t_ref,
    q_ref,
    k_ref,
    v_ref,
    g_ref,
    lse_ref,
    out_ref,
    key_t,
    dk_acc,
    dv_acc,
):
    slots = q_ref.shape[0]
    tiles = tiles_of(slots // COLS)
    span = TILE_ROWS * COLS
    globals_here = pick_ref.shape[0]
    global_keys_f = dot_nn(pick_ref[...], k_ref[...])
    global_keys = global_keys_f.astype(BF)
    global_keys_t = jnp.transpose(global_keys_f).astype(BF)
    global_values = dot_nn(pick_ref[...], v_ref[...]).astype(BF)
    key_t[...] = jnp.transpose(k_ref[...].astype(F32)).astype(BF)
    dk_acc[...] = jnp.zeros_like(dk_acc)
    dv_acc[...] = jnp.zeros_like(dv_acc)
    dk_global = jnp.zeros((globals_here, PAIR), F32)
    dv_global = jnp.zeros((globals_here, PAIR), F32)
    lane = lax.broadcasted_iota(jnp.int32, (span, PAIR), 1)
    for number, (query_lo, key_lo, key_hi) in enumerate(tiles):
        count = key_hi - key_lo
        query = two_heads(q_ref[query_lo : query_lo + span, :], lane)
        grad = two_heads(g_ref[query_lo : query_lo + span, :], lane)
        keys = jnp.concatenate([k_ref[key_lo:key_hi, :], global_keys])
        values = jnp.concatenate([v_ref[key_lo:key_hi, :], global_values])
        lse = lse_ref[0, number : number + 1, :]
        scores = dot_nt(keys, query) * SCALE2 - lse
        probs = jnp.exp2(
            jnp.concatenate([scores[:count] + bias_ref[number, :count, :], scores[count:]])
        )
        grad_probs = dot_nt(values, grad)
        weighted = jnp.sum(probs * grad_probs, axis=0, keepdims=True)
        grad_scores = (probs * (grad_probs - weighted)).astype(BF)
        dv = dot_nn(probs.astype(BF), grad)
        dk = dot_nn(grad_scores, query)
        dv_acc[key_lo:key_hi, :] += dv[:count]
        dk_acc[key_lo:key_hi, :] += dk[:count]
        dv_global += dv[count:]
        dk_global += dk[count:]
        seen_t = jnp.concatenate([key_t[:, key_lo:key_hi], global_keys_t], axis=1)
        sums = dot_nn(seen_t, grad_scores)
        sums = own_heads(sums, span) * HD ** (-0.5)
        out_ref[0, query_lo : query_lo + span, :] = sums.astype(BF)

    def spread(part):
        high = part.astype(BF)
        rest = part - high.astype(F32)
        middle = rest.astype(BF)
        low = (rest - middle.astype(F32)).astype(BF)
        picks = pick_t_ref[...]
        return dot_nn(picks, high) + dot_nn(picks, middle) + dot_nn(picks, low)

    out_ref[1] = ((dk_acc[...] + spread(dk_global)) * HD ** (-0.5)).astype(BF)
    out_ref[2] = (dv_acc[...] + spread(dv_global)).astype(BF)


def attention(query, keys, values, bias, pick):
    slots, width = query.shape
    pairs = width // PAIR
    block = pl.BlockSpec((slots, PAIR), lambda p: (0, p))
    tiles = slots // (TILE_ROWS * COLS)
    return pl.pallas_call(
        attend_kernel,
        grid=(pairs,),
        in_specs=[IN_VMEM, IN_VMEM, block, block, block],
        out_specs=[block, pl.BlockSpec((1, tiles, 2 * TILE_ROWS * COLS), lambda p: (p, 0, 0))],
        out_shape=[
            jax.ShapeDtypeStruct((slots, width), BF),
            jax.ShapeDtypeStruct((pairs, tiles, 2 * TILE_ROWS * COLS), F32),
        ],
        scratch_shapes=[pltpu.VMEM((PAIR, slots), BF)],
        compiler_params=pltpu.CompilerParams(vmem_limit_bytes=10 * 2**20),
        cost_estimate=SMALL,
        name="attend",
    )(bias, pick, query, keys, values)


def attention_back(query, keys, values, grad, lse, bias, pick, pick_t, first, count):
    slots = query.shape[0]
    block = pl.BlockSpec((slots, PAIR), lambda p: (0, first + p))
    return pl.pallas_call(
        attend_back_kernel,
        grid=(count,),
        in_specs=[IN_VMEM] * 3
        + [block] * 4
        + [pl.BlockSpec((1, *lse.shape[1:]), lambda p: (first + p, 0, 0))],
        out_specs=pl.BlockSpec((3, slots, PAIR), lambda p: (0, 0, p)),
        out_shape=jax.ShapeDtypeStruct((3, slots, count * PAIR), BF),
        scratch_shapes=[
            pltpu.VMEM((PAIR, slots), BF),
            pltpu.VMEM((slots, PAIR), F32),
            pltpu.VMEM((slots, PAIR), F32),
        ],
        compiler_params=pltpu.CompilerParams(vmem_limit_bytes=12 * 2**20),
        cost_estimate=SMALL,
        name="attend_back",
    )(bias, pick, pick_t, query, keys, values, grad, lse)


def project(piece, gain, weights):
    hidden = rms_norm(piece.astype(F32), gain).astype(BF)
    return [hidden] + [dot_nn(hidden, weight[...]).astype(BF) for weight in weights]


def front(piece, gain, *weights):
    def kernel(piece, gain, *refs):
        for out, value in zip(refs[3:], project(piece[...], gain[...], refs[:3])):
            out[...] = value

    return small("front", kernel, [piece.shape] * 4, piece, gain, *weights, cost=SMALL)


def front_last(pieces, parts, gain, *weights):
    count, (rows, width) = len(pieces), pieces[0].shape

    def kernel(here, *refs):
        refs = list(refs)
        pieces = [refs.pop(0) for _ in range(count)]
        parts = [[refs.pop(0) for _ in range(4)] for _ in range(count - 1)]
        gain, weights, outs = refs[0], refs[1:4], refs[4:]
        for bit in range(count):
            place = pl.ds(pl.multiple_of((here[0] ^ bit) * rows, rows), rows)
            outs[0][place, :] = pieces[bit][...]
            if bit < count - 1:
                values = [part[...] for part in parts[bit]]
            else:
                values = project(pieces[bit][...], gain[...], weights)
            for out, value in zip(outs[1:], values):
                out[place, :] = value

    return small(
        "front_last",
        kernel,
        [(count * rows, width)] * 5,
        *pieces,
        *[array for part in parts for array in part],
        gain,
        *weights,
        scalars=[lax.axis_index("band")],
        cost=SMALL,
    )


def middle_kernel(x_ref, attended_ref, w_out, gain_ref, resid_ref, hidden_ref, hidden_t):
    resid = x_ref[...].astype(F32) + dot_nn(attended_ref[...], w_out[...])
    resid_ref[...] = resid
    hidden = rms_norm(resid, gain_ref[...])
    hidden_ref[...] = hidden.astype(BF)
    hidden_t[...] = jnp.transpose(hidden).astype(BF)


def middle(x, attended, w_out, gain):
    slots, width = x.shape
    rows = 256
    block = pl.BlockSpec((rows, width), lambda g: (g, 0))
    return pl.pallas_call(
        middle_kernel,
        grid=(slots // rows,),
        in_specs=[block, block, IN_VMEM, IN_VMEM],
        out_specs=[block, block, pl.BlockSpec((width, rows), lambda g: (0, g))],
        out_shape=[
            jax.ShapeDtypeStruct((slots, width), F32),
            jax.ShapeDtypeStruct((slots, width), BF),
            jax.ShapeDtypeStruct((width, slots), BF),
        ],
        compiler_params=pltpu.CompilerParams(vmem_limit_bytes=12 * 2**20),
        cost_estimate=SMALL,
        name="middle",
    )(x, attended, w_out, gain)


def turn_kernel(in_ref, out_ref):
    out_ref[...] = jnp.transpose(in_ref[...].astype(F32)).astype(BF)


def turn(matrix):
    rows, columns = matrix.shape
    wide = 256
    return pl.pallas_call(
        turn_kernel,
        grid=(columns // wide,),
        in_specs=[pl.BlockSpec((rows, wide), lambda g: (0, g))],
        out_specs=pl.BlockSpec((wide, rows), lambda g: (g, 0)),
        out_shape=jax.ShapeDtypeStruct((columns, rows), BF),
        compiler_params=pltpu.CompilerParams(vmem_limit_bytes=8 * 2**20),
        cost_estimate=SMALL,
        name="turn",
    )(matrix)


def weight_grad_kernel(groups, swapped, place_ref, *refs):
    refs, out_ref = list(refs[:-1]), refs[-1]
    rows = out_ref.shape[1]
    half = 4 * rows
    start = pl.multiple_of(place_ref[0] * half, half)

    def store(sums, at):
        for block in range(4):
            spot = (block >> 1) | ((block & 1) << 1) if swapped else block
            part = sums[block * rows : (block + 1) * rows]
            out_ref[spot ^ place_ref[1], :, at : at + sums.shape[1]] = part

    at = 0
    for spans in groups:
        mine = refs.pop(0)[pl.ds(start, half), :]
        for span in spans:
            right = refs.pop(0)
            for number, first, count in span:
                for step in range(0, count, 512):
                    wide = min(512, count - step)
                    columns = right[number, :, first + step : first + step + wide]
                    store(dot_nn(mine, columns).astype(BF), at)
                    at += wide


def weight_grad(place, groups, *, spans, swapped=False):
    half = groups[0][0].shape[0] // 2
    inputs = [array for left, rights in groups for array in (left, *rights)]
    total = sum(count for group in spans for span in group for _, _, count in span)
    return pl.pallas_call(
        functools.partial(weight_grad_kernel, spans, swapped),
        in_specs=[IN_SMEM] + [IN_VMEM] * len(inputs),
        out_specs=IN_VMEM,
        out_shape=jax.ShapeDtypeStruct((4, half // 4, total), BF),
        compiler_params=pltpu.CompilerParams(vmem_limit_bytes=8 * 2**20),
        cost_estimate=SMALL,
        name="weight_grad",
    )(place, *inputs)


def ffn_kernel(
    place_ref,
    hidden_ref,
    hidden_t,
    dy_ref,
    dy_t,
    gate_w,
    up_w,
    down_w,
    inner_ref,
    gate_ref,
    up_ref,
    near_ref,
    far_ref,
    gate_w_t,
    up_w_t,
):
    rows = 256
    slope = (2.0 / 3.141592653589793) ** 0.5
    for start in range(0, hidden_ref.shape[0], rows):
        here = slice(start, start + rows)
        gate = dot_nn(hidden_ref[here, :], gate_w[...])
        up = dot_nn(hidden_ref[here, :], up_w[...])
        back = dot_nn(dy_ref[here, :], down_w[...])
        square = gate * gate
        share = 0.5 + 0.5 * jnp.tanh(gate * (slope + (0.044715 * slope) * square))
        active = gate * share
        inner_ref[here, :] = (active * up).astype(BF)
        up_ref[here, :] = (back * active).astype(BF)
        steep = share + (active - active * share) * (
            2.0 * slope + (6.0 * 0.044715 * slope) * square
        )
        gate_ref[here, :] = (back * up * steep).astype(BF)
    gate_w_t[...] = jnp.transpose(gate_w[...].astype(F32)).astype(BF)
    up_w_t[...] = jnp.transpose(up_w[...].astype(F32)).astype(BF)
    height = near_ref.shape[2]
    late = pl.program_id(0) >= pl.num_programs(0) // 2
    turned = (False, True, late)
    lefts, rights = (hidden_t, hidden_t, dy_t), (gate_ref, up_ref, inner_ref)
    for number, (left, right, swapped) in enumerate(zip(lefts, rights, turned)):
        sums = dot_nn(left[...], right[...]).astype(BF)
        for half in range(2):

            def put(target, half=half, sums=sums, number=number, swapped=swapped):
                for block in range(4):
                    straight = block ^ place_ref[1]
                    crossed = ((block >> 1) | ((block & 1) << 1)) ^ place_ref[2]
                    at = (4 * half + block) * height
                    spot = jnp.where(swapped, crossed, straight)
                    target[number, spot] = sums[at : at + height]

            pl.when(place_ref[0] == half)(functools.partial(put, near_ref))
            pl.when(place_ref[0] != half)(functools.partial(put, far_ref))


def ffn(place, hidden, hidden_t, dy, dy_t, w_gate, w_up, w_down_t):
    tokens, width = hidden.shape
    units = w_gate.shape[1]
    chunk = 512
    weight = pl.BlockSpec((width, chunk), lambda g: (0, g))
    wide = pl.BlockSpec((tokens, chunk), lambda g: (0, g))
    half = pl.BlockSpec((3, 4, width // 8, chunk), lambda g: (0, 0, 0, g))
    turned = pl.BlockSpec((chunk, width), lambda g: (g, 0))
    return pl.pallas_call(
        ffn_kernel,
        grid=(units // chunk,),
        in_specs=[IN_SMEM] + [IN_VMEM] * 4 + [weight] * 3,
        out_specs=[wide, wide, wide, half, half, turned, turned],
        out_shape=[jax.ShapeDtypeStruct((tokens, units), BF)] * 3
        + [jax.ShapeDtypeStruct((3, 4, width // 8, units), BF)] * 2
        + [jax.ShapeDtypeStruct((units, width), BF)] * 2,
        compiler_params=pltpu.CompilerParams(vmem_limit_bytes=42 * 2**20),
        cost_estimate=SMALL,
        name="ffn",
    )(place, hidden, hidden_t, dy, dy_t, w_gate, w_up, w_down_t)


def norm_back(values, gain, grad):
    inverse = lax.rsqrt(jnp.mean(values * values, axis=-1, keepdims=True) + 1e-06)
    scaled = values * inverse
    pulled = grad * gain
    return inverse * (pulled - scaled * jnp.mean(scaled * pulled, axis=-1, keepdims=True))


def patch_kernel(splits, *refs):
    parts, refs = refs[:splits], refs[splits:]
    x_ref, grad_ref, gain_ref, *weights, out_ref = refs
    grad = 0.0
    for number, weight in enumerate(weights):
        part = jnp.concatenate([ref[number] for ref in parts], axis=1)
        grad = grad + dot_nn(part, weight[...])
    pulled = norm_back(x_ref[...].astype(F32), gain_ref[...], grad)
    out_ref[...] = (pulled + grad_ref[...]).astype(BF)


def patch_back(parts, x, grad, gain, w_query, w_key, w_value):
    tokens, width = x.shape
    rows = 512
    slim = pl.BlockSpec((rows, width), lambda g: (g, 0))
    part_specs = [pl.BlockSpec((3, rows, part.shape[2]), lambda g: (0, g, 0)) for part in parts]
    return pl.pallas_call(
        functools.partial(patch_kernel, len(parts)),
        grid=(tokens // rows,),
        in_specs=part_specs + [slim, slim] + [IN_VMEM] * 4,
        out_specs=slim,
        out_shape=jax.ShapeDtypeStruct((tokens, width), BF),
        compiler_params=pltpu.CompilerParams(vmem_limit_bytes=22 * 2**20),
        cost_estimate=SMALL,
        name="patch_back",
    )(*parts, x, grad, gain, w_query, w_key, w_value)


def assemble_kernel(recipe, scored, place_ref, near_ref, far_ref, gain_ref, *refs):
    weights, outs, sums_ref = refs[:scored], refs[scored:-1], refs[-1]
    step = pl.program_id(0)
    for far, ref in enumerate((near_ref, far_ref)):

        @pl.when((step >= 4) == (far == 1))
        def _(ref=ref):
            sums = jnp.zeros((ref.shape[1], 1), F32)
            for number, (out_ref, pieces) in enumerate(zip(outs, recipe)):
                at = 0
                for first, columns in pieces:
                    part = ref[0, :, first : first + columns].astype(F32)
                    out_ref[:, at : at + columns] = part
                    if number < scored:
                        weight = weights[number][:, at : at + columns].astype(F32)
                        sums = sums + jnp.sum(part * weight, axis=1, keepdims=True)
                    at += columns
            sums_ref[...] = sums / gain_ref[...]


def assemble(place, near, far, gain, weights, recipe):
    rows = near.shape[1]
    block = (1, rows, near.shape[2])
    widths = [sum(columns for _, columns in pieces) for pieces in recipe]
    placed = [pl.BlockSpec((rows, w), lambda g, place: (g ^ place[2], 0)) for w in widths]
    narrow = pl.BlockSpec((rows, 128), lambda g, place: (g ^ place[2], 0))
    return pl.pallas_call(
        functools.partial(assemble_kernel, recipe, len(weights)),
        grid_spec=pltpu.PrefetchScalarGridSpec(
            num_scalar_prefetch=1,
            grid=(8,),
            in_specs=[
                pl.BlockSpec(block, lambda g, place: (jnp.minimum(g, 3), 0, 0)),
                pl.BlockSpec(block, lambda g, place: (jnp.maximum(g - 4, 0), 0, 0)),
                narrow,
            ]
            + placed[: len(weights)],
            out_specs=placed + [narrow],
        ),
        out_shape=[jax.ShapeDtypeStruct((8 * rows, w), F32) for w in widths + [128]],
        compiler_params=pltpu.CompilerParams(vmem_limit_bytes=18 * 2**20),
        cost_estimate=SMALL,
        name="assemble",
    )(place, near, far, gain, *weights)


def assemble_turned_kernel(place_ref, near_ref, far_ref, out_ref, rows_ref):
    height = near_ref.shape[1]
    for far, ref in enumerate((near_ref, far_ref)):
        for at in range(4):
            block = (4 * far + at) ^ place_ref[2]
            start = pl.multiple_of(block * height, height)
            rows_ref[pl.ds(start, height), :] = ref[at].astype(F32)
    out_ref[...] = jnp.transpose(rows_ref[...])


def assemble_turned(place, near, far, firsts, columns):
    rows = near.shape[1]
    chunk = 256
    half = columns // 2 // chunk
    one, two = (first // chunk for first in firsts)

    def where(g, place):
        return (0, 0, jnp.where(g < half, one + g, two + g - half))

    return pl.pallas_call(
        assemble_turned_kernel,
        grid_spec=pltpu.PrefetchScalarGridSpec(
            num_scalar_prefetch=1,
            grid=(2 * half,),
            in_specs=[pl.BlockSpec((4, rows, chunk), where)] * 2,
            out_specs=pl.BlockSpec((chunk, 8 * rows), lambda g, place: (g, 0)),
            scratch_shapes=[pltpu.VMEM((8 * rows, chunk), F32)],
        ),
        out_shape=jax.ShapeDtypeStruct((columns, 8 * rows), F32),
        compiler_params=pltpu.CompilerParams(vmem_limit_bytes=12 * 2**20),
        cost_estimate=SMALL,
        name="assemble_turned",
    )(place, near, far)


def small(name, kernel, shapes, *inputs, scalars=(), cost=TINY):
    many = [jax.ShapeDtypeStruct(shape, BF) for shape in shapes]
    scalars = [jnp.stack(scalars)] if scalars else []
    return pl.pallas_call(
        kernel,
        in_specs=[IN_SMEM] * len(scalars) + [IN_VMEM] * len(inputs),
        out_specs=[IN_VMEM] * len(many),
        out_shape=many,
        compiler_params=pltpu.CompilerParams(vmem_limit_bytes=8 * 2**20),
        cost_estimate=cost,
        name=name,
    )(*scalars, *inputs)


def add_low(left, right):
    return (left.astype(F32) + right.astype(F32)).astype(BF)


def halve(near, arrived):
    half = near.shape[0] // 2
    shape = (half, *near.shape[1:])

    def kernel(near, come, stays, leaves):
        for block in range(half):
            stays[block] = add_low(near[block], come[block])
            leaves[block] = add_low(near[half + block], come[half + block])

    return small("halve", kernel, [shape, shape], near, arrived)


def first_halves_kernel(near, come, one_stays, one_leaves, two_stays, two_leaves):
    step = pl.program_id(0)
    units = near.shape[3]
    half = units // 2
    for number, outs in enumerate(((one_stays, two_stays), (one_leaves, two_leaves))):

        @pl.when((step >= 2) == (number == 1))
        def _(outs=outs):
            last = add_low(near[2, 0], come[2, 0])
            for stream, out in enumerate(outs):
                out[0, :, :units] = add_low(near[stream, 0], come[stream, 0])
                out[0, :, units:] = last[:, stream * half : (stream + 1) * half]


def first_halves(near, come):
    _, blocks, rows, units = near.shape
    wide = units + units // 2
    stays = pl.BlockSpec((1, rows, wide), lambda g: (jnp.minimum(g, 1), 0, 0))
    leaves = pl.BlockSpec((1, rows, wide), lambda g: (jnp.maximum(g - 2, 0), 0, 0))
    block = pl.BlockSpec((3, 1, rows, units), lambda g: (0, g, 0, 0))
    one, one_go, two, two_go = pl.pallas_call(
        first_halves_kernel,
        grid=(blocks,),
        in_specs=[block, block],
        out_specs=[stays, leaves, stays, leaves],
        out_shape=[jax.ShapeDtypeStruct((2, rows, wide), BF)] * 4,
        compiler_params=pltpu.CompilerParams(vmem_limit_bytes=14 * 2**20),
        cost_estimate=SMALL,
        name="first_halves",
    )(near, come)
    return (one, one_go), (two, two_go)


def join(near, arrived):
    half = near.shape[0]

    def kernel(near, come, out):
        for block in range(half):
            out[block] = near[block]
            out[half + block] = come[block]

    return small("join", kernel, [(2 * half, *near.shape[1:])], near, arrived)[0]


def join_both(one, one_come, two, two_come):
    blocks, rows, wide = one.shape
    other = two.shape[2]

    def kernel(one, one_come, two, two_come, out):
        for number, (left, right) in enumerate(((one, two), (one_come, two_come))):
            for block in range(blocks):
                at = blocks * number + block
                out[at, :, :wide] = left[block]
                out[(at >> 1) | ((at & 1) << 1), :, wide:] = right[block]

    shape = (2 * blocks, rows, wide + other)
    return small("join_both", kernel, [shape], one, one_come, two, two_come)[0]


def apart(blocks):
    count = blocks.shape[0]

    def kernel(here, blocks, *outs):
        for bit, out in enumerate(outs):
            out[...] = blocks[here[0] ^ bit]

    return small(
        "apart", kernel, [blocks.shape[1:]] * count, blocks, scalars=[lax.axis_index("band")]
    )


def in_order(*pieces):
    count = len(pieces)

    def kernel(here, *refs):
        for bit in range(count):
            refs[count][here[0] ^ bit] = refs[bit][...]

    shape = (count, *pieces[0].shape)
    return small("in_order", kernel, [shape], *pieces, scalars=[lax.axis_index("band")])[0]


def bit_of(axis, bit):
    return (lax.axis_index(axis) // bit) % 2


def rows_apart(axis, bit):
    def step(*streams):
        height = streams[0].shape[1] // 2
        widths = [stream.shape[2] for stream in streams[::2]]
        shape = (height, sum(widths))

        def kernel(mine, *refs):
            ins, (stays, leaves) = refs[:-2], refs[-2:]
            for out, half in ((stays, mine[0]), (leaves, 1 - mine[0])):
                rows = pl.ds(pl.multiple_of(half * height, height), height)
                at = 0
                for near, come, wide in zip(ins[::2], ins[1::2], widths):
                    out[:, at : at + wide] = add_low(near[0, rows, :], come[0, rows, :])
                    at += wide

        return small(
            "rows_apart", kernel, [shape, shape], *streams, scalars=[bit_of(axis, bit)]
        )

    return step


def add_up(near, come):
    def kernel(near, come, out):
        out[...] = add_low(near[...], come[...])

    return small("add_up", kernel, [near.shape], near, come)[0]


def rows_join(axis, bit, widths):
    def step(near, come):
        height = near.shape[0]

        def kernel(mine, near, come, *outs):
            for piece, half in ((near, mine[0]), (come, 1 - mine[0])):
                rows = pl.ds(pl.multiple_of(half * height, height), height)
                at = 0
                for out, wide in zip(outs, widths):
                    out[0, rows, :] = piece[:, at : at + wide]
                    at += wide

        shapes = [(1, 2 * height, wide) for wide in widths]
        return small("rows_join", kernel, shapes, near, come, scalars=[bit_of(axis, bit)])

    return step


CORE, ACROSS, ALONG = 1, 2, 4


def flip(axis, bit):
    count = lax.axis_size(axis)
    return [(i, i ^ bit) for i in range(count)]


def swap(array, axis, bit):
    return lax.ppermute(array, axis, flip(axis, bit))


def take(array, number, axis=0):
    return lax.dynamic_index_in_dim(array, number, axis, keepdims=False)


def exchange(pieces):
    return pieces[:1] + tuple(swap(piece, "band", bit + 1) for bit, piece in enumerate(pieces[1:]))


def far_bits():
    plots = lax.axis_size("plots")
    band = lax.axis_size("band")
    bits = [("plots", 1 << n) for n in range(3, plots.bit_length() - 1)]
    return bits + [("band", 1 << n) for n in range(band.bit_length() - 1)]


class Line:
    def __init__(self):
        self.last = ()

    def __call__(self, step, *inputs):
        inputs, _ = lax.optimization_barrier((inputs, self.last))
        self.last = step(*inputs)
        return self.last


def side(axis, bit):
    def step(*streams):
        sums = [add_low(near[0], come[0]) for near, come in zip(streams[::2], streams[1::2])]
        return split_far(axis, bit)(jnp.concatenate(sums, 1))

    return step


def split_far(axis, bit):
    def step(matrix):
        halves = matrix.reshape(2, matrix.shape[0] // 2, matrix.shape[1])
        mine = bit_of(axis, bit)
        return take(halves, mine), take(halves, 1 - mine)

    return step


def join_far(axis, bit):
    def step(matrix, other):
        return jnp.where(
            bit_of(axis, bit) == 0,
            jnp.concatenate([matrix, other]),
            jnp.concatenate([other, matrix]),
        )

    return step


def travel(run, widths, *streams):
    far = far_bits()
    if len(far) == 2:
        first, second = far
        near, leaves = run(rows_apart(*first), *streams)
        come = swap(leaves, *first)
        yield
        near = run(add_up, near, come)
        come = swap(near, *second)
        yield
        near = run(add_up, near, come)
        come = swap(near, *first)
        yield
        return run(rows_join(*first, widths), near, come)
    near, leaves = run(side(*far[0]), *streams)
    come = swap(leaves, *far[0])
    yield
    for axis, bit in far[1:]:
        near, leaves = run(
            lambda near, come, far=(axis, bit): split_far(*far)(add_low(near, come)), near, come
        )
        come = swap(leaves, axis, bit)
        yield
    near = run(add_low, near, come)
    for axis, bit in far[::-1]:
        come = swap(near, axis, bit)
        yield
        near = run(join_far(axis, bit), near, come)
    cuts = [sum(widths[: n + 1]) for n in range(len(widths) - 1)]
    return run(lambda a: jnp.split(a[None], cuts, 2), near)


def rest_of(steps):
    while True:
        try:
            next(steps)
        except StopIteration as end:
            return end.value


def rms_norm(values, gain):
    inverse = lax.rsqrt(jnp.mean(values * values, axis=-1, keepdims=True) + 1e-06)
    return values * inverse * gain


def per_device(
    patches,
    norm1_gain,
    w_query,
    w_key,
    w_value,
    w_out,
    norm2_gain,
    w_gate,
    w_up,
    w_down,
    out_grad,
    plot_rows,
    plot_cols,
    global_index,
):
    width = patches.shape[2]
    here = lax.axis_index("band")
    run = Line()
    slots = patches.shape[0] * patches.shape[1]
    count = patches.shape[0]
    pieces = list(run(apart, patches))
    pieces[1:3] = [swap(piece, "band", bit + 1) for bit, piece in enumerate(pieces[1:3])]
    gain = norm1_gain[None]
    weights = w_query, w_key, w_value
    parts = [run(front, pieces[0], gain, *weights)]
    last = run(lambda *a: a, *pieces[3:])
    pieces[3:] = [swap(piece, "band", bit + 3) for bit, piece in enumerate(last)]
    limits = jnp.stack([take(plot_rows, here), take(plot_cols, here)])
    chosen = take(global_index, here)
    index = jnp.broadcast_to(chosen[:, None], (chosen.shape[0], 128))
    index_t = jnp.broadcast_to(chosen[None, :], (8, chosen.shape[0]))
    bias, pick, pick_t = run(functools.partial(masks, slots=slots), limits, index, index_t)
    gain1_rows, gain2_rows = run(
        lambda *gains: tuple(jnp.broadcast_to(g[:, None], (width, 128)) for g in gains),
        norm1_gain,
        norm2_gain,
    )
    w_down_t = run(turn, w_down)
    parts.append(run(front, pieces[1], gain, *weights))
    w_query_t, w_key_t, w_value_t = (run(turn, w) for w in weights)
    for piece in pieces[2:-1]:
        parts.append(run(front, piece, gain, *weights))
    dy_pieces = run(apart, out_grad)
    pieces = run(lambda *a: a, *pieces)
    dy_pieces = exchange(run(lambda *a: a, *dy_pieces))
    x_low, hidden, query, keys, values = run(front_last, pieces, parts, gain, *weights)

    me = lax.axis_index("plots")
    core, across, along = me % 2, (me // ACROSS) % 2, (me // ALONG) % 2
    square, square_t = 2 * across + along, 2 * along + across
    whole = 4 * core + square
    place_near = jnp.stack([core, square, whole])
    place_far = jnp.stack([1 - core, square, whole])
    place_near_t = jnp.stack([core, square_t, whole])
    place_far_t = jnp.stack([1 - core, square_t, whole])
    ff = w_gate.shape[1]

    attended, lse = run(attention, query, keys, values, bias, pick)
    resid, hidden2, hidden2_t = run(middle, x_low, attended, w_out, norm2_gain[None])
    w_out_t = run(turn, w_out)
    attended_t, hidden_t = run(turn, attended), run(turn, hidden)
    dy = run(in_order, *dy_pieces).reshape(slots, width)
    dy_t = run(turn, dy)
    place_ffn = jnp.stack([core, square, square_t])
    inner, grad_gate, grad_up, ffn_near, ffn_far, w_gate_t, w_up_t = run(
        ffn, place_ffn, hidden2, hidden2_t, dy, dy_t, w_gate, w_up, w_down_t
    )
    core_swap = functools.partial(swap, axis="plots", bit=CORE)
    across_swap = functools.partial(swap, axis="plots", bit=ACROSS)
    along_swap = functools.partial(swap, axis="plots", bit=ALONG)
    far = far_bits()

    ffn_come = core_swap(ffn_far)
    mixed_out = run(
        lambda resid, inner, w: (resid + dot_nn(inner, w)).astype(BF), resid, inner, w_down
    )
    mixed_pieces = run(apart, mixed_out.reshape(patches.shape))
    (gate_near, gate_go), (up_near, up_go) = run(first_halves, ffn_near, ffn_come)
    gate_come, up_come = across_swap(gate_go), along_swap(up_go)
    mixed_pieces = exchange(run(lambda *a: a, *mixed_pieces))
    grad_hidden2 = run(
        lambda a, b, c, d: dot_nn(a, c) + dot_nn(b, d), grad_gate, grad_up, w_gate_t, w_up_t
    )

    def resid_back(resid, dy, gain, grad):
        pulled = norm_back(resid, gain, grad) + dy.astype(F32)
        return pulled, pulled.astype(BF)

    grad_resid, resid_low = run(resid_back, resid, dy, norm2_gain, grad_hidden2)
    grad_attended = run(lambda a, w: dot_nn(a, w).astype(BF), resid_low, w_out_t)
    third = width // PAIR // 3

    def back(first):
        return run(
            functools.partial(attention_back, first=first, count=third),
            query,
            keys,
            values,
            grad_attended,
            lse,
            bias,
            pick,
            pick_t,
        )

    back_0 = back(0)
    gate_near, gate_go = run(halve, gate_near, gate_come)
    gate_come = along_swap(gate_go)
    up_near, up_go = run(halve, up_near, up_come)
    up_come = across_swap(up_go)
    back_1 = back(third)
    mixed_out = run(in_order, *mixed_pieces)
    wide_ffn = ff + ff // 2
    ffn_steps = travel(run, [wide_ffn] * 2, gate_near, gate_come, up_near, up_come)
    next(ffn_steps)
    back_2 = back(2 * third)
    next(ffn_steps)

    parts = [back_0, back_1, back_2]
    wide = third * PAIR
    half = wide // 2
    rest = width // 2
    out_right = resid_low[None]
    groups = [(hidden_t, parts), (attended_t, [out_right])]
    q_spans = [[[(0, 0, wide), (1, 0, half)]] * 3, [[(0, 0, rest)]]]
    v_spans = [[[(1, half, half), (2, 0, wide)]] * 3, [[(0, rest, width - rest)]]]
    q_grad = functools.partial(weight_grad, spans=q_spans)
    v_grad = functools.partial(weight_grad, spans=v_spans, swapped=True)
    patch_grad = run(
        patch_back, parts, x_low, grad_resid, norm1_gain[None], w_query_t, w_key_t, w_value_t
    )
    pieces = list(run(apart, patch_grad.reshape(patches.shape)))
    q_come = core_swap(run(q_grad, place_far, groups))
    v_come = core_swap(run(v_grad, place_far_t, groups))
    q_near = run(q_grad, place_near, groups)
    q_near, leaves = run(halve, q_near, q_come)
    q_come = across_swap(leaves)
    v_near = run(v_grad, place_near_t, groups)
    v_near, leaves = run(halve, v_near, v_come)
    v_come = along_swap(leaves)
    next(ffn_steps)
    q_near, leaves = run(halve, q_near, q_come)
    q_come = along_swap(leaves)
    v_near, leaves = run(halve, v_near, v_come)
    v_come = across_swap(leaves)
    cut = 3 * (wide + half) + rest
    qkv_steps = travel(
        run, [cut, 3 * (wide + half) + width - rest], q_near, q_come, v_near, v_come
    )
    next(qkv_steps)
    gate_all, up_all = rest_of(ffn_steps)
    gate_come, up_come = along_swap(gate_all), across_swap(up_all)
    next(qkv_steps)
    gate_all = run(join, gate_all, gate_come)
    gate_come = across_swap(gate_all)
    up_all = run(join, up_all, up_come)
    up_come = along_swap(up_all)
    next(qkv_steps)
    q_all, v_all = rest_of(qkv_steps)
    q_come, v_come = along_swap(q_all), across_swap(v_all)
    early = run(lambda *a: a, pieces[1], pieces[2])
    early = [swap(piece, "band", bit + 1) for bit, piece in enumerate(early)]
    ffn_near = run(join_both, gate_all, gate_come, up_all, up_come)
    ffn_come = core_swap(ffn_near)
    q_all = run(join, q_all, q_come)
    q_come = across_swap(q_all)
    v_all = run(join, v_all, v_come)
    v_come = along_swap(v_all)
    recipe_ffn = [[(0, ff)], [(wide_ffn, ff)]]
    gate, up, sums2 = run(
        lambda *arrays: assemble(place_near, *arrays, recipe_ffn),
        ffn_near,
        ffn_come,
        gain2_rows,
        [w_gate, w_up],
    )
    pieces[1:3] = run(lambda *a: a, *early)
    qkv_near = run(join_both, q_all, q_come, v_all, v_come)
    qkv_come = core_swap(qkv_near)
    pieces[3] = swap(run(lambda a: a, pieces[3]), "band", 3)
    down = run(
        lambda near, far: assemble_turned(place_near, near, far, (ff, wide_ffn + ff), ff),
        ffn_near,
        ffn_come,
    )
    recipe = [[], [], [], [(cut - rest, rest), (cut + 3 * (wide + half), width - rest)]]
    for number in range(3):
        at = number * (wide + half)
        recipe[0].append((at, wide))
        recipe[1] += [(at + wide, half), (cut + at, half)]
        recipe[2].append((cut + at + half, wide))
    q_out, k_out, v_out, out, sums1 = run(
        lambda *arrays: assemble(place_near, *arrays, recipe), qkv_near, qkv_come, gain1_rows, list(weights)
    )
    patch_grad = run(in_order, *pieces)
    return (
        mixed_out,
        patch_grad,
        sums1[:, 0],
        q_out,
        k_out,
        v_out,
        out,
        sums2[:, 0],
        gate,
        up,
        down,
    )


def solution(mesh):
    rows = P("plots", "band", None)
    in_specs = (rows,) + (P(),) * 9 + (rows, P("plots"), P("plots"), P("plots", None))
    out_specs = (rows, rows) + (P(),) * 9
    return jax.shard_map(
        per_device, mesh=mesh, in_specs=in_specs, out_specs=out_specs, check_vma=False
    )
```
